32 devices in a mesh: seq: 8 (over z, x), ch: 4 (over y, core).
Axes of the slice: x: 2, y: 2, z: 4, core: 2. Of those that a mesh axis runs over, the one named last changes fastest.
Arguments:
- out_gate: bfloat16 [3072, 4096], P('seq', 'ch'), may hold values from -6 to 6
- in_gate: bfloat16 [3072, 4096], P('seq', 'ch'), may hold values from -6 to 6
- values: bfloat16 [3072, 4096], P('seq', 'ch'), may hold values from -6 to 6
- short_filter: float32 [3, 3, 4096], P(None, None, 'ch'), may hold values from -3 to 3
- long_filter: float32 [3072, 4096], P('seq', 'ch'), may hold values from -1.5 to 1.5
- skip_gain: float32 [4096], P('ch'), may hold values from -4 to 4
- out_weight: bfloat16 [4096, 4096], P(None, 'ch'), may hold values from -0.09375 to 0.09375
Outputs:
- projected: bfloat16 [3072, 4096], P('seq', 'ch')
The draws below stay inside these ranges and needn't reach their ends.
All inputs are finite; a program needn't handle non-finite values.
Results may differ from the reference program's by a relative error of at most 0.0049.
Values may be sent and summed in bfloat16 or wider, within the bound.
No kernel may reach another device: no remote copies, remote signals or barrier semaphores. Data moves between devices by JAX's collectives and lax.ppermute only.
A program may use at most 128 MiB of HBM per device.

```python
import math
import jax
import jax.numpy as jnp

D = 4096
TAPS = 3
SEQ_LEN = 3072


def draw_long_filter(key, part):
    rate_key, noise_key = jax.random.split(jax.random.fold_in(key, 11))
    times = jnp.arange(SEQ_LEN).astype(jnp.float32)[:, None]
    lower = math.log(1.0 / SEQ_LEN)
    upper = math.log(1.0 / 32.0)
    noise = jax.random.truncated_normal(noise_key, -4.0, 4.0, (SEQ_LEN, D), jnp.float32)
    rates = jnp.exp(jax.random.uniform(rate_key, (1, D), jnp.float32, lower, upper))
    scaling = jnp.sqrt(2.0 * rates / (1.0 - jnp.exp(-2.0 * rates * SEQ_LEN)))
    return noise * jnp.exp(-rates * times) * scaling


def block_scale(key, dims, cuts, least, top_value):
    def one(axis_at, blocks):
        draws = jax.random.uniform(jax.random.fold_in(jax.random.fold_in(key, 6), axis_at), (blocks,), jnp.float32, least / len(cuts), top_value / len(cuts))
        return jnp.repeat(jnp.exp(draws), dims[axis_at] // blocks).reshape((-1,) + (1,) * (len(dims) - axis_at - 1))

    factor_of = one(*cuts[0])
    for cut in cuts[1:]:
        factor_of = factor_of * one(*cut)
    return factor_of


def bell_draw(rng, extent, width, reach, cuts=(), kind=jnp.bfloat16):
    array = width * jax.random.normal(rng, extent, jnp.float32)
    if cuts:
        array = array * block_scale(rng, extent, cuts, -0.22, 0.18)
    return jnp.clip(array, -reach, reach).astype(kind)


def setup_inputs(seed: int = 0) -> dict:
    seeds = jax.random.split(jax.random.key(seed), 8)
    out_gate = bell_draw(seeds[0], (SEQ_LEN, D), 1.0, 6.0, ((0, 8), (1, 4)))
    in_gate = bell_draw(seeds[1], (SEQ_LEN, D), 1.0, 6.0, ((0, 8), (1, 4)))
    values = bell_draw(seeds[2], (SEQ_LEN, D), 1.0, 6.0, ((0, 8), (1, 4)))
    short_filter = bell_draw(seeds[3], (3, TAPS, D), 0.6, 3.0, ((2, 4),), jnp.float32)
    long_filter = draw_long_filter(jax.random.fold_in(seeds[7], 71), 0)
    skip_gain = bell_draw(seeds[5], (D,), 1.0, 4.0, ((0, 4),), jnp.float32)
    out_weight = bell_draw(seeds[6], (D, D), D ** -0.5, 0.09375, ((1, 4),))
    return dict(out_gate=out_gate, in_gate=in_gate, values=values, short_filter=short_filter, long_filter=long_filter, skip_gain=skip_gain, out_weight=out_weight)


def short_conv(signal, taps):
    widened = jnp.pad(signal.astype(jnp.float32), ((TAPS - 1, 0), (0, 0)))
    summed = taps[0] * widened[TAPS - 1:]
    for offset in range(1, TAPS):
        summed = summed + taps[offset] * widened[TAPS - 1 - offset:TAPS - 1 - offset + SEQ_LEN]
    return summed


def reference(out_gate, in_gate, values, short_filter, long_filter, skip_gain, out_weight):
    gate_late = short_conv(out_gate, short_filter[0])
    mixed_in = short_conv(in_gate, short_filter[1]) * short_conv(values, short_filter[2])
    padded_size = 2 * SEQ_LEN
    spectrum = jnp.fft.rfft(mixed_in, n=padded_size, axis=0) * jnp.fft.rfft(long_filter, n=padded_size, axis=0)
    long_out = jnp.fft.irfft(spectrum, n=padded_size, axis=0)[:SEQ_LEN].astype(jnp.float32)
    filtered = long_out + skip_gain * mixed_in
    mixed = (gate_late * filtered).astype(jnp.bfloat16)
    return jnp.dot(mixed, out_weight, preferred_element_type=jnp.float32).astype(jnp.bfloat16)
```

```python
import functools
import math

import jax
import jax.numpy as jnp
import ml_dtypes
import numpy as np
from jax import lax
from jax.experimental import pallas as pl
from jax.experimental.pallas import tpu as pltpu
from jax.sharding import PartitionSpec as P

LANES = 128
ROW_PARTS = 2
BF16 = jnp.bfloat16
F32 = jnp.float32


def two_terms(table):
    high = table.astype(ml_dtypes.bfloat16)
    low = (table - high.astype(np.float64)).astype(ml_dtypes.bfloat16)
    return high, low


def transform_tables(rows):
    order = np.concatenate([np.arange(0, rows, 2), np.arange(1, rows, 2)])
    product = (2 * order[:, None] + 1) * np.arange(rows)[None, :] % (4 * rows)
    angles = product * (math.pi / (2 * rows))
    forward = np.concatenate([np.cos(angles), -np.sin(angles)])
    fwd_high, fwd_low = two_terms(forward)
    inv_high, inv_low = two_terms(forward.T / rows)
    return (
        np.concatenate([fwd_high, fwd_low], axis=1),
        np.concatenate([inv_high, inv_low, inv_high], axis=1),
    )


def short_conv(pad_ref, block, rim, taps):
    rows = block.shape[0]
    pad_ref[pl.ds(0, 8), :] = rim
    pad_ref[pl.ds(8, rows), :] = block
    total = taps[0:1] * block
    for offset in range(1, taps.shape[0]):
        total = total + taps[offset : offset + 1] * pad_ref[pl.ds(8 - offset, rows), :]
    return total


def mix_kernel(gate_ref, value_ref, rim_ref, taps_ref, out_ref, pad_a, pad_b):
    first = short_conv(pad_a, gate_ref[...].astype(F32), rim_ref[1], taps_ref[1])
    second = short_conv(pad_b, value_ref[...].astype(F32), rim_ref[2], taps_ref[2])
    out_ref[0] = (first * second).astype(out_ref.dtype)


def mix_inputs(in_gate, values, rims, taps):
    rows, width = in_gate.shape
    span = LANES
    parts = width // span
    return pl.pallas_call(
        mix_kernel,
        grid=(parts,),
        in_specs=[
            pl.BlockSpec((rows, span), lambda i: (0, i)),
            pl.BlockSpec((rows, span), lambda i: (0, i)),
            pl.BlockSpec((3, 8, span), lambda i: (0, 0, i)),
            pl.BlockSpec((3, taps.shape[1], span), lambda i: (0, 0, i)),
        ],
        out_specs=pl.BlockSpec((1, rows, span), lambda i: (i, 0, 0)),
        out_shape=jax.ShapeDtypeStruct((parts, rows, span), BF16),
        scratch_shapes=[pltpu.VMEM((rows + 8, span), F32)] * 2,
        cost_estimate=pl.CostEstimate(flops=12 * rows * width, bytes_accessed=6 * rows * width, transcendentals=0),
    )(in_gate, values, rims, taps)


def side_kernel(late_ref, gate_ref, value_ref, rim_ref, taps_ref, skip_ref, late_out, skip_out, pad_a, pad_b, pad_c):
    late_out[...] = short_conv(pad_a, late_ref[...].astype(F32), rim_ref[0], taps_ref[0])
    first = short_conv(pad_b, gate_ref[...].astype(F32), rim_ref[1], taps_ref[1])
    second = short_conv(pad_c, value_ref[...].astype(F32), rim_ref[2], taps_ref[2])
    skip_out[...] = skip_ref[...] * (first * second)


def side_terms(out_gate, in_gate, values, rims, taps, skip_gain):
    rows, width = in_gate.shape
    span = min(width, 128)
    column = pl.BlockSpec((rows, span), lambda i: (0, i))
    return pl.pallas_call(
        side_kernel,
        grid=(width // span,),
        in_specs=[
            column,
            column,
            column,
            pl.BlockSpec((3, 8, span), lambda i: (0, 0, i)),
            pl.BlockSpec((3, taps.shape[1], span), lambda i: (0, 0, i)),
            pl.BlockSpec((1, span), lambda i: (0, i)),
        ],
        out_specs=[column, column],
        out_shape=[jax.ShapeDtypeStruct((rows, width), F32)] * 2,
        scratch_shapes=[pltpu.VMEM((rows + 8, span), F32)] * 3,
        cost_estimate=pl.CostEstimate(flops=20 * rows * width, bytes_accessed=14 * rows * width, transcendentals=0),
    )(out_gate, in_gate, values, rims, taps, skip_gain.reshape(1, width))


def pair_of(ref, at):
    return jnp.concatenate([ref[at], ref[at + 1]], axis=1)


def forward_into(table_ref, signal_ref, out_ref):
    blocks, _, lanes = signal_ref.shape

    @pl.loop(0, blocks // 2)
    def _(step):
        pair = pair_of(signal_ref, 2 * step)
        spectra = jnp.dot(table_ref[...], jnp.concatenate([pair, pair], axis=0), preferred_element_type=F32)
        out_ref[2 * step] = spectra[:, :lanes]
        out_ref[2 * step + 1] = spectra[:, lanes:]


def forward_kernel(table_ref, signal_ref, out_ref):
    forward_into(table_ref, signal_ref, out_ref)


def forward(table, signal):
    blocks, rows, lanes = signal.shape
    return pl.pallas_call(
        forward_kernel,
        out_shape=jax.ShapeDtypeStruct((blocks, 2 * rows, lanes), F32),
        compiler_params=pltpu.CompilerParams(vmem_limit_bytes=60 << 20),
        cost_estimate=pl.CostEstimate(flops=8 * blocks * rows * rows * lanes, bytes_accessed=10 * blocks * rows * lanes, transcendentals=0),
    )(table, signal)


def conv_kernel(table_ref, inverse_ref, signal_ref, filter_ref, *rest):
    out_refs, (spectra_ref, high_ref, low_ref) = rest[:-3], rest[-3:]
    blocks, rows, lanes = signal_ref.shape
    forward_into(table_ref, signal_ref, spectra_ref)
    half = rows // 2
    tile = 16

    def multiply(base, turn):
        def body(step, carry):
            start = pl.multiple_of(base + step * tile, tile)
            real, imag = pl.ds(start, tile), pl.ds(rows + start, tile)
            before = None
            for at in range(blocks):
                sum_real = sum_imag = None
                for other in range(at + 1):
                    a_real, a_imag = filter_ref[other, real, :], filter_ref[other, imag, :]
                    b_real, b_imag = spectra_ref[at - other, real, :], spectra_ref[at - other, imag, :]
                    part_real = a_real * b_real - a_imag * b_imag
                    part_imag = a_real * b_imag + a_imag * b_real
                    sum_real = part_real if sum_real is None else sum_real + part_real
                    sum_imag = part_imag if sum_imag is None else sum_imag + part_imag
                out_real, out_imag = sum_real, sum_imag
                if before is not None:
                    out_real = sum_real - turn * before[1]
                    out_imag = sum_imag + turn * before[0]
                before = (sum_real, sum_imag)
                for place, value in ((real, out_real), (imag, out_imag)):
                    high = value.astype(BF16)
                    high_ref[at, place, :] = high
                    low_ref[at, place, :] = (value - high.astype(F32)).astype(BF16)
            return carry

        lax.fori_loop(0, half // tile, body, 0)

    multiply(0, 1.0)
    multiply(half, -1.0)

    part_rows = rows // len(out_refs)
    for part, out_ref in enumerate(out_refs):

        @pl.loop(0, blocks // 2)
        def _(step):
            high, low = pair_of(high_ref, 2 * step), pair_of(low_ref, 2 * step)
            result = jnp.dot(
                inverse_ref[pl.ds(part * part_rows, part_rows), :],
                jnp.concatenate([high, high, low], axis=0),
                preferred_element_type=F32,
            ).astype(out_ref.dtype)
            out_ref[2 * step] = result[:, :lanes]
            out_ref[2 * step + 1] = result[:, lanes:]


def block_conv(table, inverse, signal, filter_spectra, parts):
    blocks, rows, lanes = signal.shape
    return pl.pallas_call(
        conv_kernel,
        out_shape=[jax.ShapeDtypeStruct((blocks, rows // parts, lanes), BF16)] * parts,
        scratch_shapes=[
            pltpu.VMEM((blocks, 2 * rows, lanes), F32),
            pltpu.VMEM((blocks, 2 * rows, lanes), BF16),
            pltpu.VMEM((blocks, 2 * rows, lanes), BF16),
        ],
        compiler_params=pltpu.CompilerParams(vmem_limit_bytes=60 << 20),
        cost_estimate=pl.CostEstimate(flops=20 * blocks * rows * rows * lanes, bytes_accessed=10 * blocks * rows * lanes, transcendentals=0),
    )(table, inverse, signal, filter_spectra)


def gate_kernel(long_ref, late_ref, skip_ref, out_ref):
    out_ref[...] = (late_ref[...] * (long_ref[0].astype(F32) + skip_ref[...])).astype(out_ref.dtype)


def gate_rows(long_part, late, skip, part):
    blocks, rows, lanes = long_part.shape
    column = pl.BlockSpec((rows, lanes), lambda i: (part, i))
    return pl.pallas_call(
        gate_kernel,
        grid=(blocks,),
        in_specs=[pl.BlockSpec((1, rows, lanes), lambda i: (i, 0, 0)), column, column],
        out_specs=pl.BlockSpec((rows, lanes), lambda i: (0, i)),
        out_shape=jax.ShapeDtypeStruct((rows, blocks * lanes), BF16),
        cost_estimate=pl.CostEstimate(flops=3 * blocks * rows * lanes, bytes_accessed=12 * blocks * rows * lanes, transcendentals=0),
    )(long_part, late, skip)


def project_kernel(order_ref, *refs):
    del order_ref
    *mixed_refs, weight_ref, out_ref, total_ref = refs
    step = pl.program_id(0)
    for at, mixed_ref in enumerate(mixed_refs):

        @pl.when(step == at)
        def _():
            product = jnp.dot(mixed_ref[...], weight_ref[...], preferred_element_type=F32)
            total_ref[...] = product if at == 0 else total_ref[...] + product

    @pl.when(step == len(mixed_refs) - 1)
    def _():
        out_ref[...] = total_ref[...].astype(out_ref.dtype)


def project(pieces, weight, order):
    rows, depth = pieces[0].shape
    width = weight.shape[1]
    count = len(pieces)
    whole = pl.BlockSpec((rows, depth), lambda i, order: (0, 0))
    return pl.pallas_call(
        project_kernel,
        grid_spec=pltpu.PrefetchScalarGridSpec(
            num_scalar_prefetch=1,
            grid=(count,),
            in_specs=[whole] * count + [pl.BlockSpec((depth, width), lambda i, order: (order[i], 0))],
            out_specs=pl.BlockSpec((rows, width), lambda i, order: (0, 0)),
            scratch_shapes=[pltpu.VMEM((rows, width), F32)],
        ),
        out_shape=jax.ShapeDtypeStruct((rows, width), BF16),
        compiler_params=pltpu.CompilerParams(vmem_limit_bytes=40 << 20),
        cost_estimate=pl.CostEstimate(flops=2 * rows * depth * count * width, bytes_accessed=2 * depth * count * width, transcendentals=0),
    )(order, *pieces, weight)


def gather_channels(block):
    count = lax.axis_size("ch")
    held = {0: block}
    bit = count // 2
    while bit:
        route = [(i, i ^ bit) for i in range(count)]
        held.update({at ^ bit: lax.ppermute(part, "ch", route) for at, part in list(held.items())})
        bit //= 2
    return [held[at] for at in range(count)]


def exchange(blocks):
    return lax.all_to_all(blocks, "seq", split_axis=0, concat_axis=0, tiled=True)


def send_spans(slices):
    count, rows, lanes = slices.shape
    devices = lax.axis_size("seq")
    cut = devices // count
    if cut > 1:
        slices = slices.reshape(count, rows, cut, lanes // cut).transpose(0, 2, 1, 3).reshape(devices, rows, lanes // cut)
    blocks = exchange(slices)
    return jnp.pad(blocks, ((0, 0), (0, 0), (0, lanes - lanes // cut))) if cut > 1 else blocks


def return_spans(blocks, count):
    devices, rows, lanes = blocks.shape
    cut = devices // count
    if cut == 1:
        return exchange(blocks)
    arrived = exchange(blocks[:, :, : lanes // cut])
    return arrived.reshape(count, cut, rows, lanes // cut).transpose(0, 2, 1, 3).reshape(count, rows, lanes)


def on_device(out_gate, in_gate, values, short_filter, long_filter, skip_gain, out_weight):
    rows, width = out_gate.shape
    devices = lax.axis_size("seq")
    slices = width // LANES
    taps = short_filter.shape[1]
    table, inverse = transform_tables(rows)

    rim = jnp.stack([a[rows - (taps - 1) :] for a in (out_gate, in_gate, values)])
    rim = lax.ppermute(rim, "seq", [(i, i + 1) for i in range(devices - 1)])
    rims = jnp.pad(rim.astype(F32), ((0, 0), (8 - (taps - 1), 0), (0, 0)))

    filter_slices = long_filter.astype(BF16).reshape(rows, slices, LANES).transpose(1, 0, 2)
    filter_whole = send_spans(filter_slices)
    mixed_whole = send_spans(mix_inputs(in_gate, values, rims, short_filter))

    filter_spectra = forward(table, filter_whole)
    late, skip = side_terms(out_gate, in_gate, values, rims, short_filter, skip_gain)
    long_parts = block_conv(table, inverse, mixed_whole, filter_spectra, ROW_PARTS)
    channel = lax.axis_index("ch")
    order = jnp.bitwise_xor(channel, jnp.arange(lax.axis_size("ch"), dtype=jnp.int32))
    outs = []
    for part, long_part in enumerate(long_parts):
        returned = return_spans(long_part, slices)
        mixed = gate_rows(returned, late, skip, part)
        outs.append(project(gather_channels(mixed), out_weight, order))
    return jnp.concatenate(outs, axis=0)


def solution(mesh):
    return jax.shard_map(
        on_device,
        mesh=mesh,
        in_specs=(
            P("seq", "ch"),
            P("seq", "ch"),
            P("seq", "ch"),
            P(None, None, "ch"),
            P("seq", "ch"),
            P("ch"),
            P(None, "ch"),
        ),
        out_specs=P("seq", "ch"),
        check_vma=False,
    )
```

```python
import functools
import math

import jax
import jax.numpy as jnp
import ml_dtypes
import numpy as np
from jax import lax
from jax.experimental import pallas as pl
from jax.experimental.pallas import tpu as pltpu
from jax.sharding import PartitionSpec as P

LANES = 128
ROW_PARTS = 2
BF16 = jnp.bfloat16
F32 = jnp.float32


def two_terms(table):
    high = table.astype(ml_dtypes.bfloat16)
    low = (table - high.astype(np.float64)).astype(ml_dtypes.bfloat16)
    return high, low


def transform_tables(rows):
    order = np.concatenate([np.arange(0, rows, 2), np.arange(1, rows, 2)])
    product = (2 * order[:, None] + 1) * np.arange(rows)[None, :] % (4 * rows)
    angles = product * (math.pi / (2 * rows))
    forward = np.concatenate([np.cos(angles), -np.sin(angles)])
    fwd_high, fwd_low = two_terms(forward)
    inv_high, inv_low = two_terms(forward.T / rows)
    return (
        np.concatenate([fwd_high, fwd_low], axis=1),
        np.concatenate([inv_high, inv_low, inv_high], axis=1),
    )


def short_conv(pad_ref, block, rim, taps):
    rows = block.shape[0]
    pad_ref[pl.ds(8 - rim.shape[0], rim.shape[0]), :] = rim
    pad_ref[pl.ds(8, rows), :] = block
    total = taps[0:1] * block
    for offset in range(1, taps.shape[0]):
        total = total + taps[offset : offset + 1] * pad_ref[pl.ds(8 - offset, rows), :]
    return total


def mix_kernel(gate_ref, value_ref, rim_ref, taps_ref, out_ref, pad_a, pad_b):
    first = short_conv(pad_a, gate_ref[...].astype(F32), rim_ref[1], taps_ref[1])
    second = short_conv(pad_b, value_ref[...].astype(F32), rim_ref[2], taps_ref[2])
    out_ref[0] = (first * second).astype(out_ref.dtype)


def mix_inputs(in_gate, values, rims, taps):
    rows, width = in_gate.shape
    span = LANES
    parts = width // span
    return pl.pallas_call(
        mix_kernel,
        grid=(parts,),
        in_specs=[
            pl.BlockSpec((rows, span), lambda i: (0, i)),
            pl.BlockSpec((rows, span), lambda i: (0, i)),
            pl.BlockSpec((3, taps.shape[1] - 1, span), lambda i: (0, 0, i)),
            pl.BlockSpec((3, taps.shape[1], span), lambda i: (0, 0, i)),
        ],
        out_specs=pl.BlockSpec((1, rows, span), lambda i: (i, 0, 0)),
        out_shape=jax.ShapeDtypeStruct((parts, rows, span), BF16),
        scratch_shapes=[pltpu.VMEM((rows + 8, span), F32)] * 2,
        cost_estimate=pl.CostEstimate(flops=12 * rows * width, bytes_accessed=6 * rows * width, transcendentals=0),
    )(in_gate, values, rims, taps)


def side_kernel(late_ref, gate_ref, value_ref, rim_ref, taps_ref, skip_ref, late_out, skip_out, pad_a, pad_b, pad_c):
    late_out[...] = short_conv(pad_a, late_ref[...].astype(F32), rim_ref[0], taps_ref[0])
    first = short_conv(pad_b, gate_ref[...].astype(F32), rim_ref[1], taps_ref[1])
    second = short_conv(pad_c, value_ref[...].astype(F32), rim_ref[2], taps_ref[2])
    skip_out[...] = skip_ref[...] * (first * second)


def side_terms(out_gate, in_gate, values, rims, taps, skip_gain):
    rows, width = in_gate.shape
    span = min(width, 128)
    column = pl.BlockSpec((rows, span), lambda i: (0, i))
    return pl.pallas_call(
        side_kernel,
        grid=(width // span,),
        in_specs=[
            column,
            column,
            column,
            pl.BlockSpec((3, taps.shape[1] - 1, span), lambda i: (0, 0, i)),
            pl.BlockSpec((3, taps.shape[1], span), lambda i: (0, 0, i)),
            pl.BlockSpec((1, span), lambda i: (0, i)),
        ],
        out_specs=[column, column],
        out_shape=[jax.ShapeDtypeStruct((rows, width), F32)] * 2,
        scratch_shapes=[pltpu.VMEM((rows + 8, span), F32)] * 3,
        cost_estimate=pl.CostEstimate(flops=20 * rows * width, bytes_accessed=14 * rows * width, transcendentals=0),
    )(out_gate, in_gate, values, rims, taps, skip_gain.reshape(1, width))


def pair_of(ref, at):
    return jnp.concatenate([ref[at], ref[at + 1]], axis=1)


def forward_into(table_ref, signal_ref, out_ref):
    blocks, _, lanes = signal_ref.shape

    @pl.loop(0, blocks // 2)
    def _(step):
        pair = pair_of(signal_ref, 2 * step)
        spectra = jnp.dot(table_ref[...], jnp.concatenate([pair, pair], axis=0), preferred_element_type=F32)
        out_ref[2 * step] = spectra[:, :lanes]
        out_ref[2 * step + 1] = spectra[:, lanes:]


def forward_kernel(table_ref, signal_ref, out_ref):
    forward_into(table_ref, signal_ref, out_ref)


def forward(table, signal):
    blocks, rows, lanes = signal.shape
    return pl.pallas_call(
        forward_kernel,
        out_shape=jax.ShapeDtypeStruct((blocks, 2 * rows, lanes), F32),
        compiler_params=pltpu.CompilerParams(vmem_limit_bytes=60 << 20),
        cost_estimate=pl.CostEstimate(flops=8 * blocks * rows * rows * lanes, bytes_accessed=10 * blocks * rows * lanes, transcendentals=0),
    )(table, signal)


def conv_kernel(table_ref, inverse_ref, signal_ref, filter_ref, *rest):
    out_refs, (spectra_ref, high_ref, low_ref) = rest[:-3], rest[-3:]
    blocks, rows, lanes = signal_ref.shape
    forward_into(table_ref, signal_ref, spectra_ref)
    half = rows // 2
    tile = 16

    def multiply(base, turn):
        def body(step, carry):
            start = pl.multiple_of(base + step * tile, tile)
            real, imag = pl.ds(start, tile), pl.ds(rows + start, tile)
            before = None
            for at in range(blocks):
                sum_real = sum_imag = None
                for other in range(at + 1):
                    a_real, a_imag = filter_ref[other, real, :], filter_ref[other, imag, :]
                    b_real, b_imag = spectra_ref[at - other, real, :], spectra_ref[at - other, imag, :]
                    part_real = a_real * b_real - a_imag * b_imag
                    part_imag = a_real * b_imag + a_imag * b_real
                    sum_real = part_real if sum_real is None else sum_real + part_real
                    sum_imag = part_imag if sum_imag is None else sum_imag + part_imag
                out_real, out_imag = sum_real, sum_imag
                if before is not None:
                    out_real = sum_real - turn * before[1]
                    out_imag = sum_imag + turn * before[0]
                before = (sum_real, sum_imag)
                for place, value in ((real, out_real), (imag, out_imag)):
                    high = value.astype(BF16)
                    high_ref[at, place, :] = high
                    low_ref[at, place, :] = (value - high.astype(F32)).astype(BF16)
            return carry

        lax.fori_loop(0, half // tile, body, 0)

    multiply(0, 1.0)
    multiply(half, -1.0)

    part_rows = rows // len(out_refs)
    for part, out_ref in enumerate(out_refs):

        @pl.loop(0, blocks // 2)
        def _(step):
            high, low = pair_of(high_ref, 2 * step), pair_of(low_ref, 2 * step)
            result = jnp.dot(
                inverse_ref[pl.ds(part * part_rows, part_rows), :],
                jnp.concatenate([high, high, low], axis=0),
                preferred_element_type=F32,
            ).astype(out_ref.dtype)
            out_ref[2 * step] = result[:, :lanes]
            out_ref[2 * step + 1] = result[:, lanes:]


def block_conv(table, inverse, signal, filter_spectra, parts):
    blocks, rows, lanes = signal.shape
    return pl.pallas_call(
        conv_kernel,
        out_shape=[jax.ShapeDtypeStruct((blocks, rows // parts, lanes), BF16)] * parts,
        scratch_shapes=[
            pltpu.VMEM((blocks, 2 * rows, lanes), F32),
            pltpu.VMEM((blocks, 2 * rows, lanes), BF16),
            pltpu.VMEM((blocks, 2 * rows, lanes), BF16),
        ],
        compiler_params=pltpu.CompilerParams(vmem_limit_bytes=60 << 20),
        cost_estimate=pl.CostEstimate(flops=20 * blocks * rows * rows * lanes, bytes_accessed=10 * blocks * rows * lanes, transcendentals=0),
    )(table, inverse, signal, filter_spectra)


def gate_kernel(long_ref, late_ref, skip_ref, out_ref):
    out_ref[...] = (late_ref[...] * (long_ref[0].astype(F32) + skip_ref[...])).astype(out_ref.dtype)


def gate_rows(long_part, late, skip, part):
    blocks, rows, lanes = long_part.shape
    column = pl.BlockSpec((rows, lanes), lambda i: (part, i))
    return pl.pallas_call(
        gate_kernel,
        grid=(blocks,),
        in_specs=[pl.BlockSpec((1, rows, lanes), lambda i: (i, 0, 0)), column, column],
        out_specs=pl.BlockSpec((rows, lanes), lambda i: (0, i)),
        out_shape=jax.ShapeDtypeStruct((rows, blocks * lanes), BF16),
        cost_estimate=pl.CostEstimate(flops=3 * blocks * rows * lanes, bytes_accessed=12 * blocks * rows * lanes, transcendentals=0),
    )(long_part, late, skip)


def project_kernel(order_ref, *refs):
    del order_ref
    *mixed_refs, weight_ref, out_ref, total_ref = refs
    step = pl.program_id(0)
    for at, mixed_ref in enumerate(mixed_refs):

        @pl.when(step == at)
        def _():
            product = jnp.dot(mixed_ref[...], weight_ref[...], preferred_element_type=F32)
            total_ref[...] = product if at == 0 else total_ref[...] + product

    @pl.when(step == len(mixed_refs) - 1)
    def _():
        out_ref[...] = total_ref[...].astype(out_ref.dtype)


def project(pieces, weight, order):
    rows, depth = pieces[0].shape
    width = weight.shape[1]
    count = len(pieces)
    whole = pl.BlockSpec((rows, depth), lambda i, order: (0, 0))
    return pl.pallas_call(
        project_kernel,
        grid_spec=pltpu.PrefetchScalarGridSpec(
            num_scalar_prefetch=1,
            grid=(count,),
            in_specs=[whole] * count + [pl.BlockSpec((depth, width), lambda i, order: (order[i], 0))],
            out_specs=pl.BlockSpec((rows, width), lambda i, order: (0, 0)),
            scratch_shapes=[pltpu.VMEM((rows, width), F32)],
        ),
        out_shape=jax.ShapeDtypeStruct((rows, width), BF16),
        compiler_params=pltpu.CompilerParams(vmem_limit_bytes=40 << 20),
        cost_estimate=pl.CostEstimate(flops=2 * rows * depth * count * width, bytes_accessed=2 * depth * count * width, transcendentals=0),
    )(order, *pieces, weight)


def gather_channels(block):
    count = lax.axis_size("ch")
    held = {0: block}
    bit = count // 2
    while bit:
        route = [(i, i ^ bit) for i in range(count)]
        held.update({at ^ bit: lax.ppermute(part, "ch", route) for at, part in list(held.items())})
        bit //= 2
    return [held[at] for at in range(count)]


def exchange(blocks):
    return lax.all_to_all(blocks, "seq", split_axis=0, concat_axis=0, tiled=True)


def send_spans(slices):
    count, rows, lanes = slices.shape
    devices = lax.axis_size("seq")
    cut = devices // count
    if cut > 1:
        slices = slices.reshape(count, rows, cut, lanes // cut).transpose(0, 2, 1, 3).reshape(devices, rows, lanes // cut)
    blocks = exchange(slices)
    return jnp.pad(blocks, ((0, 0), (0, 0), (0, lanes - lanes // cut))) if cut > 1 else blocks


def return_spans(blocks, count):
    devices, rows, lanes = blocks.shape
    cut = devices // count
    if cut == 1:
        return exchange(blocks)
    arrived = exchange(blocks[:, :, : lanes // cut])
    return arrived.reshape(count, cut, rows, lanes // cut).transpose(0, 2, 1, 3).reshape(count, rows, lanes)


OFFSETS = (0, 4, 1, 2, 3, 5, 6, 7)
FILTER_ORDER = (4, 1, 5, 2, 6, 3, 7)
SIGNAL_ORDER = (4, 1, 5, 2, 6, 3, 7)
EARLY = (0, 4, 1, 5)
LATE = (2, 6, 3, 7)
GROUP = 4
PER = 2
PIECE_ORDER = (0, 2, 1, 3)


def cost(flops, scale=0):
    return pl.CostEstimate(flops=scale * flops, bytes_accessed=scale * flops // 128, transcendentals=0)


def lanes_at(order_ref, place):
    return pl.ds(pl.multiple_of(order_ref[place] * LANES, LANES), LANES)


def whole_specs(count):
    return [pl.BlockSpec(memory_space=pltpu.VMEM)] * count


def cut_kernel(order_ref, filter_ref, *out_refs):
    for place, out_ref in enumerate(out_refs):
        out_ref[...] = filter_ref[:, lanes_at(order_ref, place)].astype(BF16)


def cut_filter(order, long_filter):
    rows, width = long_filter.shape
    count = width // LANES
    return pl.pallas_call(
        cut_kernel,
        in_specs=[pl.BlockSpec(memory_space=pltpu.SMEM)] + whole_specs(1),
        out_specs=whole_specs(count),
        out_shape=[jax.ShapeDtypeStruct((rows, LANES), BF16)] * count,
        compiler_params=pltpu.CompilerParams(vmem_limit_bytes=8 << 20),
        cost_estimate=cost(rows * width),
    )(order, long_filter)


def rim_kernel(count, order_ref, *refs):
    del order_ref
    ends = [ref[...].astype(F32)[-count:] for ref in refs[:3]]
    refs[-1][...] = jnp.concatenate(ends, axis=0).astype(BF16)


def rim_rows(order, arrays, count):
    rows, width = arrays[0].shape
    last = pl.BlockSpec((16, width), lambda i: (rows // 16 - 1, 0))
    return pl.pallas_call(
        functools.partial(rim_kernel, count),
        grid=(1,),
        in_specs=[pl.BlockSpec(memory_space=pl.ANY)] + [last] * 3,
        out_specs=pl.BlockSpec((3 * count, width), lambda i: (0, 0)),
        out_shape=jax.ShapeDtypeStruct((3 * count, width), BF16),
        compiler_params=pltpu.CompilerParams(vmem_limit_bytes=56 << 20),
        cost_estimate=pl.CostEstimate(flops=0, bytes_accessed=100 * width, transcendentals=0),
    )(order, *arrays)


def rim_of(rim_ref, which, at):
    count = rim_ref.shape[0] // 3
    return rim_ref[:, at].astype(F32)[which * count : (which + 1) * count]


def mix_slices_kernel(order_ref, gate_ref, value_ref, rim_ref, taps_ref, gain_ref, *rest):
    out_refs, skip_ref, (pad_a, pad_b) = rest[:-3], rest[-3], rest[-2:]
    for place, out_ref in enumerate(out_refs):
        at = lanes_at(order_ref, place)
        first = short_conv(pad_a.at[place % 2], gate_ref[:, at].astype(F32), rim_of(rim_ref, 1, at), taps_ref[1, :, at])
        second = short_conv(pad_b.at[place % 2], value_ref[:, at].astype(F32), rim_of(rim_ref, 2, at), taps_ref[2, :, at])
        mixed = first * second
        out_ref[...] = mixed.astype(BF16)
        skip_ref[place] = gain_ref[:, at] * mixed


def mix_slices(order, in_gate, values, rims, taps, skip_gain):
    rows, width = in_gate.shape
    count = width // LANES
    return pl.pallas_call(
        mix_slices_kernel,
        in_specs=[pl.BlockSpec(memory_space=pltpu.SMEM)] + whole_specs(5),
        out_specs=whole_specs(count + 1),
        out_shape=[jax.ShapeDtypeStruct((rows, LANES), BF16)] * count + [jax.ShapeDtypeStruct((count, rows, LANES), F32)],
        scratch_shapes=[pltpu.VMEM((2, rows + 8, LANES), F32)] * 2,
        compiler_params=pltpu.CompilerParams(vmem_limit_bytes=12 << 20),
        cost_estimate=pl.CostEstimate(flops=14 * rows * width, bytes_accessed=10 * rows * width, transcendentals=0),
    )(order, in_gate, values, rims, taps, skip_gain.reshape(1, width))


def late_kernel(order_ref, late_ref, rim_ref, taps_ref, out_ref, pad):
    for place in range(out_ref.shape[0]):
        at = lanes_at(order_ref, place)
        out_ref[place] = short_conv(pad.at[place % 2], late_ref[:, at].astype(F32), rim_of(rim_ref, 0, at), taps_ref[0, :, at])


def late_slices(order, out_gate, rims, taps):
    rows, width = out_gate.shape
    count = width // LANES
    return pl.pallas_call(
        late_kernel,
        in_specs=[pl.BlockSpec(memory_space=pltpu.SMEM)] + whole_specs(3),
        out_specs=pl.BlockSpec(memory_space=pltpu.VMEM),
        out_shape=jax.ShapeDtypeStruct((count, rows, LANES), F32),
        scratch_shapes=[pltpu.VMEM((2, rows + 8, LANES), F32)],
        compiler_params=pltpu.CompilerParams(vmem_limit_bytes=8 << 20),
        cost_estimate=pl.CostEstimate(flops=6 * rows * width, bytes_accessed=6 * rows * width, transcendentals=0),
    )(order, out_gate, rims, taps)


def spectra_into(order_ref, places, table, signal_refs, out_ref):
    columns = jnp.concatenate([ref[...] for ref in signal_refs], axis=1)
    spectra = jnp.dot(table, jnp.concatenate([columns, columns], axis=0), preferred_element_type=F32)
    for at, place in enumerate(places):
        out_ref[order_ref[place]] = spectra[:, at * LANES : (at + 1) * LANES]


def spectra_kernel(places, order_ref, table_ref, weight_ref, *refs):
    del weight_ref
    signal_refs, out_ref = refs[:-1], refs[-1]
    for base in range(0, len(signal_refs), GROUP):
        end = base + GROUP
        spectra_into(order_ref, places[base:end], table_ref[...], signal_refs[base:end], out_ref)


def spectra_of(order, table, weight, blocks, places, count):
    rows, lanes = blocks[0].shape
    given = len(places)
    return pl.pallas_call(
        functools.partial(spectra_kernel, places),
        in_specs=[pl.BlockSpec(memory_space=pltpu.SMEM)] + whole_specs(1) + [pl.BlockSpec(memory_space=pl.ANY)] + whole_specs(given),
        out_specs=pl.BlockSpec(memory_space=pltpu.VMEM),
        out_shape=jax.ShapeDtypeStruct((count, 2 * rows, lanes), F32),
        compiler_params=pltpu.CompilerParams(vmem_limit_bytes=12 << 20),
        cost_estimate=pl.CostEstimate(flops=8 * given * rows * rows * lanes, bytes_accessed=10 * given * rows * lanes, transcendentals=0),
    )(order, table, weight, *[blocks[place] for place in places])


def multiply_spectra(filter_ref, spectra_ref, high_ref, low_ref):
    blocks, depth, _ = spectra_ref.shape
    rows = depth // 2
    half, tile = rows // 2, 16

    def multiply(base, turn):
        def body(step, carry):
            start = pl.multiple_of(base + step * tile, tile)
            real, imag = pl.ds(start, tile), pl.ds(rows + start, tile)
            before = None
            for at in range(blocks):
                sum_real = sum_imag = None
                for other in range(at + 1):
                    a_real, a_imag = filter_ref[other, real, :], filter_ref[other, imag, :]
                    b_real, b_imag = spectra_ref[at - other, real, :], spectra_ref[at - other, imag, :]
                    part_real = a_real * b_real - a_imag * b_imag
                    part_imag = a_real * b_imag + a_imag * b_real
                    sum_real = part_real if sum_real is None else sum_real + part_real
                    sum_imag = part_imag if sum_imag is None else sum_imag + part_imag
                out_real, out_imag = sum_real, sum_imag
                if before is not None:
                    out_real = sum_real - turn * before[1]
                    out_imag = sum_imag + turn * before[0]
                before = (sum_real, sum_imag)
                for place, value in ((real, out_real), (imag, out_imag)):
                    high = value.astype(BF16)
                    high_ref[at, place, :] = high
                    low_ref[at, place, :] = (value - high.astype(F32)).astype(BF16)
            return carry

        lax.fori_loop(0, half // tile, body, 0)

    multiply(0, 1.0)
    multiply(half, -1.0)


def inverse_into(order_ref, base, inverse, high_ref, low_ref, out_refs):
    places = [order_ref[base + at] for at in range(len(out_refs))]
    high = jnp.concatenate([high_ref[place] for place in places], axis=1)
    low = jnp.concatenate([low_ref[place] for place in places], axis=1)
    result = jnp.dot(inverse, jnp.concatenate([high, high, low], axis=0), preferred_element_type=F32).astype(BF16)
    for at, out_ref in enumerate(out_refs):
        out_ref[...] = result[:, at * LANES : (at + 1) * LANES]


def conv_slices_kernel(places, order_ref, table_ref, inverse_ref, filter_ref, early_ref, *refs):
    del early_ref
    count = filter_ref.shape[0]
    signal_refs = refs[: len(places)]
    spectra_ref, *out_refs, high_ref, low_ref = refs[-count - 3 :]
    spectra_into(order_ref, places, table_ref[...], signal_refs, spectra_ref)
    multiply_spectra(filter_ref, spectra_ref, high_ref, low_ref)
    for base in range(0, count, GROUP):
        inverse_into(order_ref, base, inverse_ref[...], high_ref, low_ref, out_refs[base : base + GROUP])


def conv_slices(order, table, inverse, filter_spectra, early_spectra, blocks, places, after):
    rows, lanes = blocks[0].shape
    count = filter_spectra.shape[0]
    _, *outs = pl.pallas_call(
        functools.partial(conv_slices_kernel, places),
        in_specs=[pl.BlockSpec(memory_space=pltpu.SMEM)] + whole_specs(4 + len(places)) + [pl.BlockSpec(memory_space=pl.ANY)] * len(after),
        out_specs=whole_specs(1 + count),
        out_shape=[jax.ShapeDtypeStruct((count, 2 * rows, lanes), F32)]
        + [jax.ShapeDtypeStruct((rows, lanes), BF16)] * count,
        input_output_aliases={4: 0},
        scratch_shapes=[pltpu.VMEM((count, 2 * rows, lanes), BF16)] * 2,
        compiler_params=pltpu.CompilerParams(vmem_limit_bytes=20 << 20),
        cost_estimate=cost(14 * count * rows * rows * lanes, 1),
    )(order, table, inverse, filter_spectra, early_spectra, *[blocks[place] for place in places], *after)
    return outs


def gate_chunk_kernel(first, late_ref, skip_ref, *refs):
    out_ref = refs[-1]
    for at, long_ref in enumerate(refs[:-1]):
        mixed = late_ref[first + at] * (long_ref[...].astype(F32) + skip_ref[first + at])
        out_ref[:, at * LANES : (at + 1) * LANES] = mixed.astype(BF16)


def gate_chunk(late, skip, long_blocks, first):
    rows, lanes = long_blocks[0].shape
    count = len(long_blocks)
    return pl.pallas_call(
        functools.partial(gate_chunk_kernel, first),
        in_specs=whole_specs(2 + count),
        out_specs=pl.BlockSpec(memory_space=pltpu.VMEM),
        out_shape=jax.ShapeDtypeStruct((rows, count * lanes), BF16),
        compiler_params=pltpu.CompilerParams(vmem_limit_bytes=8 << 20),
        cost_estimate=cost(3 * count * rows * lanes),
    )(late, skip, *long_blocks)


def weight_kernel(order_ref, channel_ref, weight_ref, out_ref, arrived):
    count, owners = out_ref.shape[:2]
    depth = weight_ref.shape[0] // owners
    copies = []
    for place in range(count):
        for offset in range(owners):
            start = pl.multiple_of((channel_ref[0] ^ offset) * depth + order_ref[place] * LANES, LANES)
            rows = weight_ref.at[pl.ds(start, LANES), :]
            copies.append(pltpu.make_async_copy(rows, out_ref.at[place, offset], arrived.at[place, offset]))
    for copy in copies:
        copy.start()
    for copy in copies:
        copy.wait()


def weight_rows_of(order, channel, weight):
    depth, width = weight.shape
    count, owners = order.shape[0], len(PIECE_ORDER)
    return pl.pallas_call(
        weight_kernel,
        in_specs=[pl.BlockSpec(memory_space=pltpu.SMEM)] * 2 + [pl.BlockSpec(memory_space=pl.ANY)],
        out_specs=pl.BlockSpec(memory_space=pltpu.VMEM),
        out_shape=jax.ShapeDtypeStruct((count, owners, LANES, width), BF16),
        scratch_shapes=[pltpu.SemaphoreType.DMA((count, owners))],
        compiler_params=pltpu.CompilerParams(vmem_limit_bytes=10 << 20),
        cost_estimate=pl.CostEstimate(flops=0, bytes_accessed=4 * depth * width, transcendentals=0),
    )(order, channel, weight)


def add_chunk(chunk, rows_ref, piece_refs, total):
    pieces = jnp.concatenate([ref[...] for ref in piece_refs], axis=1)
    rows = [rows_ref[chunk * PER + at, offset] for offset in PIECE_ORDER for at in range(PER)]
    product = jnp.dot(pieces, jnp.concatenate(rows, axis=0), preferred_element_type=F32)
    return product if total is None else total + product


def join_kernel(*refs):
    refs[-1][...] = jnp.concatenate([ref[...] for ref in refs[:-1]], axis=1)


def join(blocks):
    rows, lanes = blocks[0].shape
    count = len(blocks)
    return pl.pallas_call(
        join_kernel,
        in_specs=whole_specs(count),
        out_specs=pl.BlockSpec(memory_space=pltpu.VMEM),
        out_shape=jax.ShapeDtypeStruct((rows, count * lanes), blocks[0].dtype),
        compiler_params=pltpu.CompilerParams(vmem_limit_bytes=8 << 20),
        cost_estimate=cost(4 * rows * lanes),
    )(*blocks)


def project_kernel_slices(chunks, rows_ref, *refs):
    refs, more, out_ref = refs[: 2 * len(chunks)], refs[2 * len(chunks) : -1], refs[-1]
    total = more[0][...] if more else None
    for at, chunk in enumerate(chunks):
        total = add_chunk(chunk, rows_ref, refs[2 * at : 2 * at + 2], total)
    out_ref[...] = total.astype(out_ref.dtype)


def project_slices(weight_rows, chunks, pieces, total, out_type):
    rows, depth = pieces[0].shape
    width = weight_rows.shape[3]
    more = () if total is None else (total,)
    return pl.pallas_call(
        functools.partial(project_kernel_slices, chunks),
        in_specs=whole_specs(1 + len(pieces) + len(more)),
        out_specs=pl.BlockSpec(memory_space=pltpu.VMEM),
        out_shape=jax.ShapeDtypeStruct((rows, width), out_type),
        compiler_params=pltpu.CompilerParams(vmem_limit_bytes=14 << 20),
        cost_estimate=cost(0),
    )(weight_rows, *pieces, *more)


def swap_blocks(blocks, sequence):
    count = lax.axis_size("seq")
    arrived = list(blocks)
    for offset in sequence:
        place = OFFSETS.index(offset)
        arrived[place] = lax.ppermute(blocks[place], "seq", [(i, i ^ offset) for i in range(count)])
    return arrived


def on_device_slices(out_gate, in_gate, values, short_filter, long_filter, skip_gain, out_weight):
    rows, width = out_gate.shape
    devices = lax.axis_size("seq")
    taps = short_filter.shape[1]
    table, inverse = transform_tables(rows)
    order = jnp.bitwise_xor(lax.axis_index("seq"), jnp.array(OFFSETS, jnp.int32))
    channel = lax.axis_index("ch").reshape(1)

    rim = rim_rows(order, (out_gate, in_gate, values), taps - 1)
    filter_blocks = swap_blocks(cut_filter(order, long_filter), FILTER_ORDER)
    rims = lax.ppermute(rim, "seq", [(i, i + 1) for i in range(devices - 1)])
    *mixed_slices, skip = mix_slices(order, in_gate, values, rims, short_filter, skip_gain)
    mixed_blocks = swap_blocks(mixed_slices, SIGNAL_ORDER)
    late = late_slices(order, out_gate, rims, short_filter)
    weight_rows = weight_rows_of(order, channel, out_weight)
    sent = (0, *(OFFSETS.index(offset) for offset in FILTER_ORDER))
    filter_spectra = spectra_of(order, table, weight_rows, filter_blocks, sent, devices)
    early, last = (tuple(OFFSETS.index(offset) for offset in group) for group in (EARLY, LATE))
    early_spectra = spectra_of(order, table, weight_rows, mixed_blocks, early, devices)
    long_blocks = conv_slices(order, table, inverse, filter_spectra, early_spectra, mixed_blocks, last, (late, weight_rows))
    arrived = swap_blocks(long_blocks, OFFSETS[1:])

    pieces = []
    for chunk in range(devices // PER):
        start = chunk * PER
        mixed = gate_chunk(late, skip, arrived[start : start + PER], start)
        across = lax.ppermute(mixed, "ch", [(i, i ^ 2) for i in range(4)])
        joined = join([mixed, across])
        pieces += [joined, lax.ppermute(joined, "ch", [(i, i ^ 1) for i in range(4)])]
    total = project_slices(weight_rows, (0, 1, 2), pieces[:-2], None, F32)
    return project_slices(weight_rows, (3,), pieces[-2:], total, BF16)


def on_device_spans(out_gate, in_gate, values, short_filter, long_filter, skip_gain, out_weight):
    rows, width = out_gate.shape
    devices = lax.axis_size("seq")
    slices = width // LANES
    taps = short_filter.shape[1]
    table, inverse = transform_tables(rows)

    rim = jnp.stack([a[rows - (taps - 1) :] for a in (out_gate, in_gate, values)])
    rim = lax.ppermute(rim, "seq", [(i, i + 1) for i in range(devices - 1)])
    rims = rim.astype(F32)

    filter_slices = long_filter.astype(BF16).reshape(rows, slices, LANES).transpose(1, 0, 2)
    filter_whole = send_spans(filter_slices)
    mixed_whole = send_spans(mix_inputs(in_gate, values, rims, short_filter))

    filter_spectra = forward(table, filter_whole)
    late, skip = side_terms(out_gate, in_gate, values, rims, short_filter, skip_gain)
    long_parts = block_conv(table, inverse, mixed_whole, filter_spectra, ROW_PARTS)
    channel = lax.axis_index("ch")
    order = jnp.bitwise_xor(channel, jnp.arange(lax.axis_size("ch"), dtype=jnp.int32))
    outs = []
    for part, long_part in enumerate(long_parts):
        returned = return_spans(long_part, slices)
        mixed = gate_rows(returned, late, skip, part)
        outs.append(project(gather_channels(mixed), out_weight, order))
    return jnp.concatenate(outs, axis=0)


def solution(mesh):
    devices = mesh.shape["seq"]

    def on_device(*arrays):
        width = arrays[0].shape[1]
        sliced = devices == len(OFFSETS) and width == devices * LANES and mesh.shape["ch"] == len(PIECE_ORDER)
        return (on_device_slices if sliced else on_device_spans)(*arrays)

    return jax.shard_map(
        on_device,
        mesh=mesh,
        in_specs=(
            P("seq", "ch"),
            P("seq", "ch"),
            P("seq", "ch"),
            P(None, None, "ch"),
            P("seq", "ch"),
            P("ch"),
            P(None, "ch"),
        ),
        out_specs=P("seq", "ch"),
        check_vma=False,
    )
```

```python
import functools
import math

import jax
import jax.numpy as jnp
import ml_dtypes
import numpy as np
from jax import lax
from jax.experimental import pallas as pl
from jax.experimental.pallas import tpu as pltpu
from jax.sharding import PartitionSpec as P

LANES = 128
TILE = 16
CUT_VMEM = 56
ROW_PARTS = 2
BF16 = jnp.bfloat16
F32 = jnp.float32


def two_terms(table):
    high = table.astype(ml_dtypes.bfloat16)
    low = (table - high.astype(np.float64)).astype(ml_dtypes.bfloat16)
    return high, low


def transform_tables(rows):
    order = np.concatenate([np.arange(0, rows, 2), np.arange(1, rows, 2)])
    product = (2 * order[:, None] + 1) * np.arange(rows)[None, :] % (4 * rows)
    angles = product * (math.pi / (2 * rows))
    forward = np.concatenate([np.cos(angles), -np.sin(angles)])
    fwd_high, fwd_low = two_terms(forward)
    inv_high, inv_low = two_terms(forward.T / rows)
    return (
        np.concatenate([fwd_high, fwd_low], axis=1),
        np.concatenate([inv_high, inv_low, inv_high], axis=1),
    )


def short_conv(pad_ref, block, rim, taps):
    rows = block.shape[0]
    pad_ref[pl.ds(8 - rim.shape[0], rim.shape[0]), :] = rim
    pad_ref[pl.ds(8, rows), :] = block
    total = taps[0:1] * block
    for offset in range(1, taps.shape[0]):
        total = total + taps[offset : offset + 1] * pad_ref[pl.ds(8 - offset, rows), :]
    return total


def mix_kernel(gate_ref, value_ref, rim_ref, taps_ref, out_ref, pad_a, pad_b):
    first = short_conv(pad_a, gate_ref[...].astype(F32), rim_ref[1], taps_ref[1])
    second = short_conv(pad_b, value_ref[...].astype(F32), rim_ref[2], taps_ref[2])
    out_ref[0] = (first * second).astype(out_ref.dtype)


def mix_inputs(in_gate, values, rims, taps):
    rows, width = in_gate.shape
    span = LANES
    parts = width // span
    return pl.pallas_call(
        mix_kernel,
        grid=(parts,),
        in_specs=[
            pl.BlockSpec((rows, span), lambda i: (0, i)),
            pl.BlockSpec((rows, span), lambda i: (0, i)),
            pl.BlockSpec((3, taps.shape[1] - 1, span), lambda i: (0, 0, i)),
            pl.BlockSpec((3, taps.shape[1], span), lambda i: (0, 0, i)),
        ],
        out_specs=pl.BlockSpec((1, rows, span), lambda i: (i, 0, 0)),
        out_shape=jax.ShapeDtypeStruct((parts, rows, span), BF16),
        scratch_shapes=[pltpu.VMEM((rows + 8, span), F32)] * 2,
        cost_estimate=pl.CostEstimate(flops=12 * rows * width, bytes_accessed=6 * rows * width, transcendentals=0),
    )(in_gate, values, rims, taps)


def side_kernel(late_ref, gate_ref, value_ref, rim_ref, taps_ref, skip_ref, late_out, skip_out, pad_a, pad_b, pad_c):
    late_out[...] = short_conv(pad_a, late_ref[...].astype(F32), rim_ref[0], taps_ref[0])
    first = short_conv(pad_b, gate_ref[...].astype(F32), rim_ref[1], taps_ref[1])
    second = short_conv(pad_c, value_ref[...].astype(F32), rim_ref[2], taps_ref[2])
    skip_out[...] = skip_ref[...] * (first * second)


def side_terms(out_gate, in_gate, values, rims, taps, skip_gain):
    rows, width = in_gate.shape
    span = min(width, 128)
    column = pl.BlockSpec((rows, span), lambda i: (0, i))
    return pl.pallas_call(
        side_kernel,
        grid=(width // span,),
        in_specs=[
            column,
            column,
            column,
            pl.BlockSpec((3, taps.shape[1] - 1, span), lambda i: (0, 0, i)),
            pl.BlockSpec((3, taps.shape[1], span), lambda i: (0, 0, i)),
            pl.BlockSpec((1, span), lambda i: (0, i)),
        ],
        out_specs=[column, column],
        out_shape=[jax.ShapeDtypeStruct((rows, width), F32)] * 2,
        scratch_shapes=[pltpu.VMEM((rows + 8, span), F32)] * 3,
        cost_estimate=pl.CostEstimate(flops=20 * rows * width, bytes_accessed=14 * rows * width, transcendentals=0),
    )(out_gate, in_gate, values, rims, taps, skip_gain.reshape(1, width))


def pair_of(ref, at):
    return jnp.concatenate([ref[at], ref[at + 1]], axis=1)


def forward_into(table_ref, signal_ref, out_ref):
    blocks, _, lanes = signal_ref.shape

    @pl.loop(0, blocks // 2)
    def _(step):
        pair = pair_of(signal_ref, 2 * step)
        spectra = jnp.dot(table_ref[...], jnp.concatenate([pair, pair], axis=0), preferred_element_type=F32)
        out_ref[2 * step] = spectra[:, :lanes]
        out_ref[2 * step + 1] = spectra[:, lanes:]


def forward_kernel(table_ref, signal_ref, out_ref):
    forward_into(table_ref, signal_ref, out_ref)


def forward(table, signal):
    blocks, rows, lanes = signal.shape
    return pl.pallas_call(
        forward_kernel,
        out_shape=jax.ShapeDtypeStruct((blocks, 2 * rows, lanes), F32),
        compiler_params=pltpu.CompilerParams(vmem_limit_bytes=60 << 20),
        cost_estimate=pl.CostEstimate(flops=8 * blocks * rows * rows * lanes, bytes_accessed=10 * blocks * rows * lanes, transcendentals=0),
    )(table, signal)


def conv_kernel(table_ref, inverse_ref, signal_ref, filter_ref, *rest):
    out_refs, (spectra_ref, high_ref, low_ref) = rest[:-3], rest[-3:]
    blocks, rows, lanes = signal_ref.shape
    forward_into(table_ref, signal_ref, spectra_ref)
    half = rows // 2
    tile = 16

    def multiply(base, turn):
        def body(step, carry):
            start = pl.multiple_of(base + step * tile, tile)
            real, imag = pl.ds(start, tile), pl.ds(rows + start, tile)
            before = None
            for at in range(blocks):
                sum_real = sum_imag = None
                for other in range(at + 1):
                    a_real, a_imag = filter_ref[other, real, :], filter_ref[other, imag, :]
                    b_real, b_imag = spectra_ref[at - other, real, :], spectra_ref[at - other, imag, :]
                    part_real = a_real * b_real - a_imag * b_imag
                    part_imag = a_real * b_imag + a_imag * b_real
                    sum_real = part_real if sum_real is None else sum_real + part_real
                    sum_imag = part_imag if sum_imag is None else sum_imag + part_imag
                out_real, out_imag = sum_real, sum_imag
                if before is not None:
                    out_real = sum_real - turn * before[1]
                    out_imag = sum_imag + turn * before[0]
                before = (sum_real, sum_imag)
                for place, value in ((real, out_real), (imag, out_imag)):
                    high = value.astype(BF16)
                    high_ref[at, place, :] = high
                    low_ref[at, place, :] = (value - high.astype(F32)).astype(BF16)
            return carry

        lax.fori_loop(0, half // tile, body, 0)

    multiply(0, 1.0)
    multiply(half, -1.0)

    part_rows = rows // len(out_refs)
    for part, out_ref in enumerate(out_refs):

        @pl.loop(0, blocks // 2)
        def _(step):
            high, low = pair_of(high_ref, 2 * step), pair_of(low_ref, 2 * step)
            result = jnp.dot(
                inverse_ref[pl.ds(part * part_rows, part_rows), :],
                jnp.concatenate([high, high, low], axis=0),
                preferred_element_type=F32,
            ).astype(out_ref.dtype)
            out_ref[2 * step] = result[:, :lanes]
            out_ref[2 * step + 1] = result[:, lanes:]


def block_conv(table, inverse, signal, filter_spectra, parts):
    blocks, rows, lanes = signal.shape
    return pl.pallas_call(
        conv_kernel,
        out_shape=[jax.ShapeDtypeStruct((blocks, rows // parts, lanes), BF16)] * parts,
        scratch_shapes=[
            pltpu.VMEM((blocks, 2 * rows, lanes), F32),
            pltpu.VMEM((blocks, 2 * rows, lanes), BF16),
            pltpu.VMEM((blocks, 2 * rows, lanes), BF16),
        ],
        compiler_params=pltpu.CompilerParams(vmem_limit_bytes=60 << 20),
        cost_estimate=pl.CostEstimate(flops=20 * blocks * rows * rows * lanes, bytes_accessed=10 * blocks * rows * lanes, transcendentals=0),
    )(table, inverse, signal, filter_spectra)


def gate_kernel(long_ref, late_ref, skip_ref, out_ref):
    out_ref[...] = (late_ref[...] * (long_ref[0].astype(F32) + skip_ref[...])).astype(out_ref.dtype)


def gate_rows(long_part, late, skip, part):
    blocks, rows, lanes = long_part.shape
    column = pl.BlockSpec((rows, lanes), lambda i: (part, i))
    return pl.pallas_call(
        gate_kernel,
        grid=(blocks,),
        in_specs=[pl.BlockSpec((1, rows, lanes), lambda i: (i, 0, 0)), column, column],
        out_specs=pl.BlockSpec((rows, lanes), lambda i: (0, i)),
        out_shape=jax.ShapeDtypeStruct((rows, blocks * lanes), BF16),
        cost_estimate=pl.CostEstimate(flops=3 * blocks * rows * lanes, bytes_accessed=12 * blocks * rows * lanes, transcendentals=0),
    )(long_part, late, skip)


def project_kernel(order_ref, *refs):
    del order_ref
    *mixed_refs, weight_ref, out_ref, total_ref = refs
    step = pl.program_id(0)
    for at, mixed_ref in enumerate(mixed_refs):

        @pl.when(step == at)
        def _():
            product = jnp.dot(mixed_ref[...], weight_ref[...], preferred_element_type=F32)
            total_ref[...] = product if at == 0 else total_ref[...] + product

    @pl.when(step == len(mixed_refs) - 1)
    def _():
        out_ref[...] = total_ref[...].astype(out_ref.dtype)


def project(pieces, weight, order):
    rows, depth = pieces[0].shape
    width = weight.shape[1]
    count = len(pieces)
    whole = pl.BlockSpec((rows, depth), lambda i, order: (0, 0))
    return pl.pallas_call(
        project_kernel,
        grid_spec=pltpu.PrefetchScalarGridSpec(
            num_scalar_prefetch=1,
            grid=(count,),
            in_specs=[whole] * count + [pl.BlockSpec((depth, width), lambda i, order: (order[i], 0))],
            out_specs=pl.BlockSpec((rows, width), lambda i, order: (0, 0)),
            scratch_shapes=[pltpu.VMEM((rows, width), F32)],
        ),
        out_shape=jax.ShapeDtypeStruct((rows, width), BF16),
        compiler_params=pltpu.CompilerParams(vmem_limit_bytes=40 << 20),
        cost_estimate=pl.CostEstimate(flops=2 * rows * depth * count * width, bytes_accessed=2 * depth * count * width, transcendentals=0),
    )(order, *pieces, weight)


def gather_channels(block):
    count = lax.axis_size("ch")
    held = {0: block}
    bit = count // 2
    while bit:
        route = [(i, i ^ bit) for i in range(count)]
        held.update({at ^ bit: lax.ppermute(part, "ch", route) for at, part in list(held.items())})
        bit //= 2
    return [held[at] for at in range(count)]


def exchange(blocks):
    return lax.all_to_all(blocks, "seq", split_axis=0, concat_axis=0, tiled=True)


def send_spans(slices):
    count, rows, lanes = slices.shape
    devices = lax.axis_size("seq")
    cut = devices // count
    if cut > 1:
        slices = slices.reshape(count, rows, cut, lanes // cut).transpose(0, 2, 1, 3).reshape(devices, rows, lanes // cut)
    blocks = exchange(slices)
    return jnp.pad(blocks, ((0, 0), (0, 0), (0, lanes - lanes // cut))) if cut > 1 else blocks


def return_spans(blocks, count):
    devices, rows, lanes = blocks.shape
    cut = devices // count
    if cut == 1:
        return exchange(blocks)
    arrived = exchange(blocks[:, :, : lanes // cut])
    return arrived.reshape(count, cut, rows, lanes // cut).transpose(0, 2, 1, 3).reshape(count, rows, lanes)


OFFSETS = (0, 4, 1, 2, 3, 5, 6, 7)
FILTER_ORDER = (4, 1, 5, 2, 6, 3, 7)
SIGNAL_ORDER = (4, 1, 5, 2, 6, 3, 7)
EARLY = (0, 4, 1, 5)
LATE = (2, 6, 3, 7)
GROUP = 4
NEXT_OFFSETS = (1, 3, 7)
KEEP = 2
MIX_AFTER = 1
CHUNKS = ((0, 2), (2, 4), (4, 6), (6, 8))
PROJECTS = ((0, 1, 2), (3,))
PROJECT_COSTS = (0, 0)
PIECE_ORDER = (0, 2, 1, 3)


def cost(flops, scale=0):
    return pl.CostEstimate(flops=scale * flops, bytes_accessed=scale * flops // 128, transcendentals=0)


def lanes_at(order_ref, place):
    return pl.ds(pl.multiple_of(order_ref[place] * LANES, LANES), LANES)


def whole_specs(count):
    return [pl.BlockSpec(memory_space=pltpu.VMEM)] * count


def cut_kernel(order_ref, filter_ref, *refs):
    last_refs, (gate_top, value_top), out_refs = refs[:3], refs[3:5], refs[5:-1]
    rows, width = filter_ref.shape
    ends_ref = refs[-1]
    ends = [ref[...].astype(F32)[-KEEP:] for ref in last_refs]
    ends += [ref[...].astype(F32)[:KEEP] for ref in (gate_top, value_top)]
    ends.append(jnp.zeros((TILE - 5 * KEEP, width), F32))
    ends_ref[...] = jnp.concatenate(ends, axis=0).astype(BF16)
    for place, out_ref in enumerate(out_refs):
        at = lanes_at(order_ref, place)
        out_ref[:rows] = filter_ref[:, at].astype(BF16)
        out_ref[rows : rows + TILE] = ends_ref[:, at]
        if OFFSETS[place] in NEXT_OFFSETS:
            for part in range(width // LANES):
                out_ref[rows + (1 + part) * TILE : rows + (2 + part) * TILE] = ends_ref[:, part * LANES : (part + 1) * LANES]


def cut_filter(order, long_filter, out_gate, in_gate, values):
    rows, width = long_filter.shape
    count = width // LANES
    heights = [rows + TILE * (1 + count * (offset in NEXT_OFFSETS)) for offset in OFFSETS]
    top = pl.BlockSpec((TILE, width), lambda i: (0, 0))
    last = pl.BlockSpec((TILE, width), lambda i: (rows // TILE - 1, 0))
    return pl.pallas_call(
        cut_kernel,
        grid=(1,),
        in_specs=[pl.BlockSpec(memory_space=pltpu.SMEM), pl.BlockSpec((rows, width), lambda i: (0, 0))] + [last] * 3 + [top] * 2,
        out_specs=[pl.BlockSpec((height, LANES), lambda i: (0, 0)) for height in heights],
        out_shape=[jax.ShapeDtypeStruct((height, LANES), BF16) for height in heights],
        scratch_shapes=[pltpu.VMEM((TILE, width), BF16)],
        compiler_params=pltpu.CompilerParams(vmem_limit_bytes=CUT_VMEM << 20),
        cost_estimate=cost(rows * width),
    )(order, long_filter, out_gate, in_gate, values, in_gate, values)


def mix_slices_kernel(order_ref, gate_ref, value_ref, taps_ref, after_ref, *rest):
    del after_ref
    out_refs, (pad_a, pad_b) = rest[:-2], rest[-2:]
    keep = taps_ref.shape[1] - 1
    for place, out_ref in enumerate(out_refs):
        at = lanes_at(order_ref, place)
        none = jnp.zeros((keep, LANES), F32)
        first = short_conv(pad_a.at[place % 2], gate_ref[:, at].astype(F32), none, taps_ref[1, :, at])
        second = short_conv(pad_b.at[place % 2], value_ref[:, at].astype(F32), none, taps_ref[2, :, at])
        out_ref[...] = (first * second).astype(BF16)


def mix_slices(order, in_gate, values, taps, after):
    rows, width = in_gate.shape
    count = width // LANES
    return pl.pallas_call(
        mix_slices_kernel,
        in_specs=[pl.BlockSpec(memory_space=pltpu.SMEM)] + whole_specs(3) + [pl.BlockSpec(memory_space=pl.ANY)],
        out_specs=whole_specs(count),
        out_shape=[jax.ShapeDtypeStruct((rows, LANES), BF16)] * count,
        scratch_shapes=[pltpu.VMEM((2, rows + 8, LANES), F32)] * 2,
        compiler_params=pltpu.CompilerParams(vmem_limit_bytes=12 << 20),
        cost_estimate=cost(14 * rows * width, 1),
    )(order, in_gate, values, taps, after)


def side_slices_kernel(order_ref, late_ref, gate_ref, value_ref, *refs):
    *before_refs, taps_ref, gain_ref, late_out, skip_out = refs[:-3]
    pads = refs[-3:]
    rows, keep = late_ref.shape[0], taps_ref.shape[1] - 1
    own = order_ref[0]
    for place in range(late_out.shape[0]):
        at = lanes_at(order_ref, place)
        start = pl.multiple_of(rows + (1 + order_ref[place]) * TILE, TILE)
        rim = jnp.zeros((TILE, LANES), F32)
        for offset, ref in zip(NEXT_OFFSETS, before_refs, strict=True):
            given = ref[pl.ds(start, TILE), :].astype(F32)
            rim = jnp.where((own & offset) == (offset + 1) // 2, given, rim)
        late, first, second = (
            short_conv(
                pad.at[place % 2],
                ref[:, at].astype(F32),
                rim[which * keep : (which + 1) * keep],
                taps_ref[which, :, at],
            )
            for which, (pad, ref) in enumerate(zip(pads, (late_ref, gate_ref, value_ref), strict=True))
        )
        late_out[place] = late
        skip_out[place] = gain_ref[:, at] * (first * second)


def side_slices(order, out_gate, in_gate, values, filter_blocks, taps, skip_gain):
    rows, width = out_gate.shape
    count = width // LANES
    before = [filter_blocks[OFFSETS.index(offset)] for offset in NEXT_OFFSETS]
    return pl.pallas_call(
        side_slices_kernel,
        in_specs=[pl.BlockSpec(memory_space=pltpu.SMEM)] + whole_specs(5 + len(before)),
        out_specs=whole_specs(2),
        out_shape=[jax.ShapeDtypeStruct((count, rows, LANES), F32)] * 2,
        scratch_shapes=[pltpu.VMEM((2, rows + 8, LANES), F32)] * 3,
        compiler_params=pltpu.CompilerParams(vmem_limit_bytes=16 << 20),
        cost_estimate=cost(20 * rows * width, 1),
    )(order, out_gate, in_gate, values, *before, taps, skip_gain.reshape(1, width))


def spectra_into(order_ref, places, table, blocks, out_ref):
    columns = jnp.concatenate(blocks, axis=1)
    spectra = jnp.dot(table, jnp.concatenate([columns, columns], axis=0), preferred_element_type=F32)
    for at, place in enumerate(places):
        out_ref[order_ref[place]] = spectra[:, at * LANES : (at + 1) * LANES]


def with_first(order_ref, places, signal_refs, first_ref):
    blocks = []
    for place, ref in zip(places, signal_refs, strict=True):
        top = ref[:TILE].astype(F32)
        row = lax.broadcasted_iota(jnp.int32, top.shape, 0)
        top = jnp.where(row < KEEP, first_ref[order_ref[place]], top).astype(BF16)
        blocks.append(jnp.concatenate([top, ref[TILE:]], axis=0))
    return blocks


def filter_kernel(places, order_ref, table_ref, taps_ref, after_ref, *refs):
    del after_ref
    *block_refs, out_ref, first_ref, ends_ref = refs
    rows = table_ref.shape[0] // 2
    for base in range(0, len(block_refs), GROUP):
        blocks = [ref[:rows] for ref in block_refs[base : base + GROUP]]
        spectra_into(order_ref, places[base : base + GROUP], table_ref[...], blocks, out_ref)
    for place, ref in zip(places, block_refs, strict=True):
        ends_ref[order_ref[place]] = ref[rows : rows + TILE].astype(F32)
    count = taps_ref.shape[1]
    at = lanes_at(order_ref, 0)
    for block in range(len(block_refs)):
        mixed = None
        for which in range(2):
            top = ends_ref[block, (3 + which) * KEEP : (4 + which) * KEEP]
            end = jnp.zeros_like(top)
            if block:
                end = ends_ref[block - 1, (1 + which) * KEEP : (2 + which) * KEEP]
            joined = jnp.concatenate([end, top], axis=0)
            taps = taps_ref[1 + which, :, at]
            total = taps[0:1] * joined[KEEP:]
            for offset in range(1, count):
                total = total + taps[offset : offset + 1] * joined[KEEP - offset : 2 * KEEP - offset]
            mixed = total if mixed is None else mixed * total
        first_ref[block] = jnp.concatenate([mixed, jnp.zeros((TILE - KEEP, LANES), F32)], axis=0)


def filter_spectra_of(order, table, taps, blocks, places, after):
    rows, lanes = table.shape[0] // 2, blocks[0].shape[1]
    count = len(blocks)
    return pl.pallas_call(
        functools.partial(filter_kernel, places),
        in_specs=[pl.BlockSpec(memory_space=pltpu.SMEM)] + whole_specs(2) + [pl.BlockSpec(memory_space=pl.ANY)] + whole_specs(count),
        out_specs=whole_specs(2),
        out_shape=[
            jax.ShapeDtypeStruct((count, 2 * rows, lanes), F32),
            jax.ShapeDtypeStruct((count, TILE, lanes), F32),
        ],
        scratch_shapes=[pltpu.VMEM((count, TILE, lanes), F32)],
        compiler_params=pltpu.CompilerParams(vmem_limit_bytes=12 << 20),
        cost_estimate=cost(8 * count * rows * rows * lanes, 1),
    )(order, table, taps, after, *[blocks[place] for place in places])


def early_kernel(places, order_ref, table_ref, first_ref, *refs):
    blocks = with_first(order_ref, places, refs[:-1], first_ref)
    spectra_into(order_ref, places, table_ref[...], blocks, refs[-1])


def early_spectra_of(order, table, first, blocks, places):
    rows, lanes = blocks[0].shape
    given = len(places)
    return pl.pallas_call(
        functools.partial(early_kernel, places),
        in_specs=[pl.BlockSpec(memory_space=pltpu.SMEM)] + whole_specs(2 + given),
        out_specs=pl.BlockSpec(memory_space=pltpu.VMEM),
        out_shape=jax.ShapeDtypeStruct((len(blocks), 2 * rows, lanes), F32),
        compiler_params=pltpu.CompilerParams(vmem_limit_bytes=12 << 20),
        cost_estimate=cost(8 * given * rows * rows * lanes, 1),
    )(order, table, first, *[blocks[place] for place in places])


def multiply_spectra(filter_ref, spectra_ref, high_ref, low_ref):
    blocks, depth, _ = spectra_ref.shape
    rows = depth // 2
    half, tile = rows // 2, 16

    def multiply(base, turn):
        def body(step, carry):
            start = pl.multiple_of(base + step * tile, tile)
            real, imag = pl.ds(start, tile), pl.ds(rows + start, tile)
            before = None
            for at in range(blocks):
                sum_real = sum_imag = None
                for other in range(at + 1):
                    a_real, a_imag = filter_ref[other, real, :], filter_ref[other, imag, :]
                    b_real, b_imag = spectra_ref[at - other, real, :], spectra_ref[at - other, imag, :]
                    part_real = a_real * b_real - a_imag * b_imag
                    part_imag = a_real * b_imag + a_imag * b_real
                    sum_real = part_real if sum_real is None else sum_real + part_real
                    sum_imag = part_imag if sum_imag is None else sum_imag + part_imag
                out_real, out_imag = sum_real, sum_imag
                if before is not None:
                    out_real = sum_real - turn * before[1]
                    out_imag = sum_imag + turn * before[0]
                before = (sum_real, sum_imag)
                for place, value in ((real, out_real), (imag, out_imag)):
                    high = value.astype(BF16)
                    high_ref[at, place, :] = high
                    low_ref[at, place, :] = (value - high.astype(F32)).astype(BF16)
            return carry

        lax.fori_loop(0, half // tile, body, 0)

    multiply(0, 1.0)
    multiply(half, -1.0)


def inverse_into(order_ref, base, inverse, high_ref, low_ref, out_refs):
    places = [order_ref[base + at] for at in range(len(out_refs))]
    high = jnp.concatenate([high_ref[place] for place in places], axis=1)
    low = jnp.concatenate([low_ref[place] for place in places], axis=1)
    result = jnp.dot(inverse, jnp.concatenate([high, high, low], axis=0), preferred_element_type=F32).astype(BF16)
    for at, out_ref in enumerate(out_refs):
        out_ref[...] = result[:, at * LANES : (at + 1) * LANES]


def conv_slices_kernel(places, order_ref, table_ref, inverse_ref, filter_ref, early_ref, first_ref, *refs):
    del early_ref
    count = filter_ref.shape[0]
    signal_refs = refs[: len(places)]
    spectra_ref, *out_refs, high_ref, low_ref = refs[-count - 3 :]
    blocks = with_first(order_ref, places, signal_refs, first_ref)
    spectra_into(order_ref, places, table_ref[...], blocks, spectra_ref)
    multiply_spectra(filter_ref, spectra_ref, high_ref, low_ref)
    for base in range(0, count, GROUP):
        inverse_into(order_ref, base, inverse_ref[...], high_ref, low_ref, out_refs[base : base + GROUP])


def conv_slices(order, table, inverse, filter_spectra, early_spectra, first, blocks, places, after):
    rows, lanes = blocks[0].shape
    count = filter_spectra.shape[0]
    _, *outs = pl.pallas_call(
        functools.partial(conv_slices_kernel, places),
        in_specs=[pl.BlockSpec(memory_space=pltpu.SMEM)] + whole_specs(5 + len(places)) + [pl.BlockSpec(memory_space=pl.ANY)] * len(after),
        out_specs=whole_specs(1 + count),
        out_shape=[jax.ShapeDtypeStruct((count, 2 * rows, lanes), F32)]
        + [jax.ShapeDtypeStruct((rows, lanes), BF16)] * count,
        input_output_aliases={4: 0},
        scratch_shapes=[pltpu.VMEM((count, 2 * rows, lanes), BF16)] * 2,
        compiler_params=pltpu.CompilerParams(vmem_limit_bytes=20 << 20),
        cost_estimate=cost(14 * count * rows * rows * lanes, 1),
    )(order, table, inverse, filter_spectra, early_spectra, first, *[blocks[place] for place in places], *after)
    return outs


def gate_chunk_kernel(first, late_ref, skip_ref, *refs):
    out_ref = refs[-1]
    for at, long_ref in enumerate(refs[:-1]):
        mixed = late_ref[first + at] * (long_ref[...].astype(F32) + skip_ref[first + at])
        out_ref[:, at * LANES : (at + 1) * LANES] = mixed.astype(BF16)


def gate_chunk(late, skip, long_blocks, first):
    rows, lanes = long_blocks[0].shape
    count = len(long_blocks)
    return pl.pallas_call(
        functools.partial(gate_chunk_kernel, first),
        in_specs=whole_specs(2 + count),
        out_specs=pl.BlockSpec(memory_space=pltpu.VMEM),
        out_shape=jax.ShapeDtypeStruct((rows, count * lanes), BF16),
        compiler_params=pltpu.CompilerParams(vmem_limit_bytes=8 << 20),
        cost_estimate=cost(3 * count * rows * lanes),
    )(late, skip, *long_blocks)


def weight_kernel(order_ref, channel_ref, weight_ref, out_ref, arrived):
    count, owners = out_ref.shape[:2]
    depth = weight_ref.shape[0] // owners
    copies = []
    for place in range(count):
        for offset in range(owners):
            start = pl.multiple_of((channel_ref[0] ^ offset) * depth + order_ref[place] * LANES, LANES)
            rows = weight_ref.at[pl.ds(start, LANES), :]
            copies.append(pltpu.make_async_copy(rows, out_ref.at[place, offset], arrived.at[place, offset]))
    for copy in copies:
        copy.start()
    for copy in copies:
        copy.wait()


def weight_rows_of(order, channel, weight):
    depth, width = weight.shape
    count, owners = order.shape[0], len(PIECE_ORDER)
    return pl.pallas_call(
        weight_kernel,
        in_specs=[pl.BlockSpec(memory_space=pltpu.SMEM)] * 2 + [pl.BlockSpec(memory_space=pl.ANY)],
        out_specs=pl.BlockSpec(memory_space=pltpu.VMEM),
        out_shape=jax.ShapeDtypeStruct((count, owners, LANES, width), BF16),
        scratch_shapes=[pltpu.SemaphoreType.DMA((count, owners))],
        compiler_params=pltpu.CompilerParams(vmem_limit_bytes=10 << 20),
        cost_estimate=pl.CostEstimate(flops=0, bytes_accessed=4 * depth * width, transcendentals=0),
    )(order, channel, weight)


def add_chunk(chunk, rows_ref, piece_refs, total):
    pieces = jnp.concatenate([ref[...] for ref in piece_refs], axis=1)
    rows = [rows_ref[place, offset] for offset in PIECE_ORDER for place in range(*CHUNKS[chunk])]
    product = jnp.dot(pieces, jnp.concatenate(rows, axis=0), preferred_element_type=F32)
    return product if total is None else total + product


def join_kernel(*refs):
    refs[-1][...] = jnp.concatenate([ref[...] for ref in refs[:-1]], axis=1)


def join(blocks):
    rows, lanes = blocks[0].shape
    count = len(blocks)
    return pl.pallas_call(
        join_kernel,
        in_specs=whole_specs(count),
        out_specs=pl.BlockSpec(memory_space=pltpu.VMEM),
        out_shape=jax.ShapeDtypeStruct((rows, count * lanes), blocks[0].dtype),
        compiler_params=pltpu.CompilerParams(vmem_limit_bytes=8 << 20),
        cost_estimate=cost(4 * rows * lanes),
    )(*blocks)


def project_kernel_slices(chunks, rows_ref, *refs):
    refs, more, out_ref = refs[: 2 * len(chunks)], refs[2 * len(chunks) : -1], refs[-1]
    total = more[0][...] if more else None
    for at, chunk in enumerate(chunks):
        total = add_chunk(chunk, rows_ref, refs[2 * at : 2 * at + 2], total)
    out_ref[...] = total.astype(out_ref.dtype)


def project_slices(weight_rows, chunks, pieces, total, out_type, scale):
    rows = pieces[0].shape[0]
    width = weight_rows.shape[3]
    more = () if total is None else (total,)
    return pl.pallas_call(
        functools.partial(project_kernel_slices, chunks),
        in_specs=whole_specs(1 + len(pieces) + len(more)),
        out_specs=pl.BlockSpec(memory_space=pltpu.VMEM),
        out_shape=jax.ShapeDtypeStruct((rows, width), out_type),
        compiler_params=pltpu.CompilerParams(vmem_limit_bytes=14 << 20),
        cost_estimate=cost(2 * rows * sum(piece.shape[1] for piece in pieces) * width, scale),
    )(weight_rows, *pieces, *more)


def swap_blocks(blocks, sequence):
    count = lax.axis_size("seq")
    arrived = list(blocks)
    for offset in sequence:
        place = OFFSETS.index(offset)
        arrived[place] = lax.ppermute(blocks[place], "seq", [(i, i ^ offset) for i in range(count)])
    return arrived


def on_device_slices(out_gate, in_gate, values, short_filter, long_filter, skip_gain, out_weight):
    rows, width = out_gate.shape
    devices = lax.axis_size("seq")
    table, inverse = transform_tables(rows)
    order = jnp.bitwise_xor(lax.axis_index("seq"), jnp.array(OFFSETS, jnp.int32))
    channel = lax.axis_index("ch").reshape(1)

    filter_blocks = swap_blocks(cut_filter(order, long_filter, out_gate, in_gate, values), FILTER_ORDER)
    sent = (0, *(OFFSETS.index(offset) for offset in FILTER_ORDER))
    mixed_blocks = swap_blocks(
        mix_slices(order, in_gate, values, short_filter, filter_blocks[OFFSETS.index(MIX_AFTER)]), SIGNAL_ORDER
    )
    late, skip = side_slices(order, out_gate, in_gate, values, filter_blocks, short_filter, skip_gain)
    weight_rows = weight_rows_of(order, channel, out_weight)
    filter_spectra, first = filter_spectra_of(order, table, short_filter, filter_blocks, sent, weight_rows)
    early, last = (tuple(OFFSETS.index(offset) for offset in group) for group in (EARLY, LATE))
    early_spectra = early_spectra_of(order, table, first, mixed_blocks, early)
    long_blocks = conv_slices(order, table, inverse, filter_spectra, early_spectra, first, mixed_blocks, last, (late, weight_rows))
    arrived = swap_blocks(long_blocks, OFFSETS[1:])

    pieces = []
    for start, stop in CHUNKS:
        mixed = gate_chunk(late, skip, arrived[start:stop], start)
        across = lax.ppermute(mixed, "ch", [(i, i ^ 2) for i in range(4)])
        joined = join([mixed, across])
        pieces.append((joined, lax.ppermute(joined, "ch", [(i, i ^ 1) for i in range(4)])))
    total = None
    for chunks, scale in zip(PROJECTS, PROJECT_COSTS, strict=True):
        kind = BF16 if chunks == PROJECTS[-1] else F32
        total = project_slices(weight_rows, chunks, [piece for chunk in chunks for piece in pieces[chunk]], total, kind, scale)
    return total


def on_device_spans(out_gate, in_gate, values, short_filter, long_filter, skip_gain, out_weight):
    rows, width = out_gate.shape
    devices = lax.axis_size("seq")
    slices = width // LANES
    taps = short_filter.shape[1]
    table, inverse = transform_tables(rows)

    rim = jnp.stack([a[rows - (taps - 1) :] for a in (out_gate, in_gate, values)])
    rim = lax.ppermute(rim, "seq", [(i, i + 1) for i in range(devices - 1)])
    rims = rim.astype(F32)

    filter_slices = long_filter.astype(BF16).reshape(rows, slices, LANES).transpose(1, 0, 2)
    filter_whole = send_spans(filter_slices)
    mixed_whole = send_spans(mix_inputs(in_gate, values, rims, short_filter))

    filter_spectra = forward(table, filter_whole)
    late, skip = side_terms(out_gate, in_gate, values, rims, short_filter, skip_gain)
    long_parts = block_conv(table, inverse, mixed_whole, filter_spectra, ROW_PARTS)
    channel = lax.axis_index("ch")
    order = jnp.bitwise_xor(channel, jnp.arange(lax.axis_size("ch"), dtype=jnp.int32))
    outs = []
    for part, long_part in enumerate(long_parts):
        returned = return_spans(long_part, slices)
        mixed = gate_rows(returned, late, skip, part)
        outs.append(project(gather_channels(mixed), out_weight, order))
    return jnp.concatenate(outs, axis=0)


def solution(mesh):
    devices = mesh.shape["seq"]

    def on_device(*arrays):
        width = arrays[0].shape[1]
        taps = arrays[3].shape[1]
        sliced = taps == KEEP + 1 and devices == len(OFFSETS) and width == devices * LANES and mesh.shape["ch"] == len(PIECE_ORDER)
        return (on_device_slices if sliced else on_device_spans)(*arrays)

    return jax.shard_map(
        on_device,
        mesh=mesh,
        in_specs=(
            P("seq", "ch"),
            P("seq", "ch"),
            P("seq", "ch"),
            P(None, None, "ch"),
            P("seq", "ch"),
            P("ch"),
            P(None, "ch"),
        ),
        out_specs=P("seq", "ch"),
        check_vma=False,
    )
```

```python
import functools
import math

import jax
import jax.numpy as jnp
import ml_dtypes
import numpy as np
from jax import lax
from jax.experimental import pallas as pl
from jax.experimental.pallas import tpu as pltpu
from jax.sharding import PartitionSpec as P

LANES = 128
TILE = 16
CUT_VMEM = 56
ROW_PARTS = 2
BF16 = jnp.bfloat16
F32 = jnp.float32


def two_terms(table):
    high = table.astype(ml_dtypes.bfloat16)
    low = (table - high.astype(np.float64)).astype(ml_dtypes.bfloat16)
    return high, low


def transform_tables(rows):
    order = np.concatenate([np.arange(0, rows, 2), np.arange(1, rows, 2)])
    product = (2 * order[:, None] + 1) * np.arange(rows)[None, :] % (4 * rows)
    angles = product * (math.pi / (2 * rows))
    forward = np.concatenate([np.cos(angles), -np.sin(angles)])
    fwd_high, fwd_low = two_terms(forward)
    inv_high, inv_low = two_terms(forward.T / rows)
    return (
        np.concatenate([fwd_high, fwd_low], axis=1),
        np.concatenate([inv_high, inv_low, inv_high], axis=1),
    )


def short_conv(pad_ref, block, rim, taps):
    rows = block.shape[0]
    pad_ref[pl.ds(8 - rim.shape[0], rim.shape[0]), :] = rim
    pad_ref[pl.ds(8, rows), :] = block
    total = taps[0:1] * block
    for offset in range(1, taps.shape[0]):
        total = total + taps[offset : offset + 1] * pad_ref[pl.ds(8 - offset, rows), :]
    return total


def mix_kernel(gate_ref, value_ref, rim_ref, taps_ref, out_ref, pad_a, pad_b):
    first = short_conv(pad_a, gate_ref[...].astype(F32), rim_ref[1], taps_ref[1])
    second = short_conv(pad_b, value_ref[...].astype(F32), rim_ref[2], taps_ref[2])
    out_ref[0] = (first * second).astype(out_ref.dtype)


def mix_inputs(in_gate, values, rims, taps):
    rows, width = in_gate.shape
    span = LANES
    parts = width // span
    return pl.pallas_call(
        mix_kernel,
        grid=(parts,),
        in_specs=[
            pl.BlockSpec((rows, span), lambda i: (0, i)),
            pl.BlockSpec((rows, span), lambda i: (0, i)),
            pl.BlockSpec((3, taps.shape[1] - 1, span), lambda i: (0, 0, i)),
            pl.BlockSpec((3, taps.shape[1], span), lambda i: (0, 0, i)),
        ],
        out_specs=pl.BlockSpec((1, rows, span), lambda i: (i, 0, 0)),
        out_shape=jax.ShapeDtypeStruct((parts, rows, span), BF16),
        scratch_shapes=[pltpu.VMEM((rows + 8, span), F32)] * 2,
        cost_estimate=pl.CostEstimate(flops=12 * rows * width, bytes_accessed=6 * rows * width, transcendentals=0),
    )(in_gate, values, rims, taps)


def side_kernel(late_ref, gate_ref, value_ref, rim_ref, taps_ref, skip_ref, late_out, skip_out, pad_a, pad_b, pad_c):
    late_out[...] = short_conv(pad_a, late_ref[...].astype(F32), rim_ref[0], taps_ref[0])
    first = short_conv(pad_b, gate_ref[...].astype(F32), rim_ref[1], taps_ref[1])
    second = short_conv(pad_c, value_ref[...].astype(F32), rim_ref[2], taps_ref[2])
    skip_out[...] = skip_ref[...] * (first * second)


def side_terms(out_gate, in_gate, values, rims, taps, skip_gain):
    rows, width = in_gate.shape
    span = min(width, 128)
    column = pl.BlockSpec((rows, span), lambda i: (0, i))
    return pl.pallas_call(
        side_kernel,
        grid=(width // span,),
        in_specs=[
            column,
            column,
            column,
            pl.BlockSpec((3, taps.shape[1] - 1, span), lambda i: (0, 0, i)),
            pl.BlockSpec((3, taps.shape[1], span), lambda i: (0, 0, i)),
            pl.BlockSpec((1, span), lambda i: (0, i)),
        ],
        out_specs=[column, column],
        out_shape=[jax.ShapeDtypeStruct((rows, width), F32)] * 2,
        scratch_shapes=[pltpu.VMEM((rows + 8, span), F32)] * 3,
        cost_estimate=pl.CostEstimate(flops=20 * rows * width, bytes_accessed=14 * rows * width, transcendentals=0),
    )(out_gate, in_gate, values, rims, taps, skip_gain.reshape(1, width))


def pair_of(ref, at):
    return jnp.concatenate([ref[at], ref[at + 1]], axis=1)


def forward_into(table_ref, signal_ref, out_ref):
    blocks, _, lanes = signal_ref.shape

    @pl.loop(0, blocks // 2)
    def _(step):
        pair = pair_of(signal_ref, 2 * step)
        spectra = jnp.dot(table_ref[...], jnp.concatenate([pair, pair], axis=0), preferred_element_type=F32)
        out_ref[2 * step] = spectra[:, :lanes]
        out_ref[2 * step + 1] = spectra[:, lanes:]


def forward_kernel(table_ref, signal_ref, out_ref):
    forward_into(table_ref, signal_ref, out_ref)


def forward(table, signal):
    blocks, rows, lanes = signal.shape
    return pl.pallas_call(
        forward_kernel,
        out_shape=jax.ShapeDtypeStruct((blocks, 2 * rows, lanes), F32),
        compiler_params=pltpu.CompilerParams(vmem_limit_bytes=60 << 20),
        cost_estimate=pl.CostEstimate(flops=8 * blocks * rows * rows * lanes, bytes_accessed=10 * blocks * rows * lanes, transcendentals=0),
    )(table, signal)


def conv_kernel(table_ref, inverse_ref, signal_ref, filter_ref, *rest):
    out_refs, (spectra_ref, high_ref, low_ref) = rest[:-3], rest[-3:]
    blocks, rows, lanes = signal_ref.shape
    forward_into(table_ref, signal_ref, spectra_ref)
    half = rows // 2
    tile = 16

    def multiply(base, turn):
        def body(step, carry):
            start = pl.multiple_of(base + step * tile, tile)
            real, imag = pl.ds(start, tile), pl.ds(rows + start, tile)
            before = None
            for at in range(blocks):
                sum_real = sum_imag = None
                for other in range(at + 1):
                    a_real, a_imag = filter_ref[other, real, :], filter_ref[other, imag, :]
                    b_real, b_imag = spectra_ref[at - other, real, :], spectra_ref[at - other, imag, :]
                    part_real = a_real * b_real - a_imag * b_imag
                    part_imag = a_real * b_imag + a_imag * b_real
                    sum_real = part_real if sum_real is None else sum_real + part_real
                    sum_imag = part_imag if sum_imag is None else sum_imag + part_imag
                out_real, out_imag = sum_real, sum_imag
                if before is not None:
                    out_real = sum_real - turn * before[1]
                    out_imag = sum_imag + turn * before[0]
                before = (sum_real, sum_imag)
                for place, value in ((real, out_real), (imag, out_imag)):
                    high = value.astype(BF16)
                    high_ref[at, place, :] = high
                    low_ref[at, place, :] = (value - high.astype(F32)).astype(BF16)
            return carry

        lax.fori_loop(0, half // tile, body, 0)

    multiply(0, 1.0)
    multiply(half, -1.0)

    part_rows = rows // len(out_refs)
    for part, out_ref in enumerate(out_refs):

        @pl.loop(0, blocks // 2)
        def _(step):
            high, low = pair_of(high_ref, 2 * step), pair_of(low_ref, 2 * step)
            result = jnp.dot(
                inverse_ref[pl.ds(part * part_rows, part_rows), :],
                jnp.concatenate([high, high, low], axis=0),
                preferred_element_type=F32,
            ).astype(out_ref.dtype)
            out_ref[2 * step] = result[:, :lanes]
            out_ref[2 * step + 1] = result[:, lanes:]


def block_conv(table, inverse, signal, filter_spectra, parts):
    blocks, rows, lanes = signal.shape
    return pl.pallas_call(
        conv_kernel,
        out_shape=[jax.ShapeDtypeStruct((blocks, rows // parts, lanes), BF16)] * parts,
        scratch_shapes=[
            pltpu.VMEM((blocks, 2 * rows, lanes), F32),
            pltpu.VMEM((blocks, 2 * rows, lanes), BF16),
            pltpu.VMEM((blocks, 2 * rows, lanes), BF16),
        ],
        compiler_params=pltpu.CompilerParams(vmem_limit_bytes=60 << 20),
        cost_estimate=pl.CostEstimate(flops=20 * blocks * rows * rows * lanes, bytes_accessed=10 * blocks * rows * lanes, transcendentals=0),
    )(table, inverse, signal, filter_spectra)


def gate_kernel(long_ref, late_ref, skip_ref, out_ref):
    out_ref[...] = (late_ref[...] * (long_ref[0].astype(F32) + skip_ref[...])).astype(out_ref.dtype)


def gate_rows(long_part, late, skip, part):
    blocks, rows, lanes = long_part.shape
    column = pl.BlockSpec((rows, lanes), lambda i: (part, i))
    return pl.pallas_call(
        gate_kernel,
        grid=(blocks,),
        in_specs=[pl.BlockSpec((1, rows, lanes), lambda i: (i, 0, 0)), column, column],
        out_specs=pl.BlockSpec((rows, lanes), lambda i: (0, i)),
        out_shape=jax.ShapeDtypeStruct((rows, blocks * lanes), BF16),
        cost_estimate=pl.CostEstimate(flops=3 * blocks * rows * lanes, bytes_accessed=12 * blocks * rows * lanes, transcendentals=0),
    )(long_part, late, skip)


def project_kernel(order_ref, *refs):
    del order_ref
    *mixed_refs, weight_ref, out_ref, total_ref = refs
    step = pl.program_id(0)
    for at, mixed_ref in enumerate(mixed_refs):

        @pl.when(step == at)
        def _():
            product = jnp.dot(mixed_ref[...], weight_ref[...], preferred_element_type=F32)
            total_ref[...] = product if at == 0 else total_ref[...] + product

    @pl.when(step == len(mixed_refs) - 1)
    def _():
        out_ref[...] = total_ref[...].astype(out_ref.dtype)


def project(pieces, weight, order):
    rows, depth = pieces[0].shape
    width = weight.shape[1]
    count = len(pieces)
    whole = pl.BlockSpec((rows, depth), lambda i, order: (0, 0))
    return pl.pallas_call(
        project_kernel,
        grid_spec=pltpu.PrefetchScalarGridSpec(
            num_scalar_prefetch=1,
            grid=(count,),
            in_specs=[whole] * count + [pl.BlockSpec((depth, width), lambda i, order: (order[i], 0))],
            out_specs=pl.BlockSpec((rows, width), lambda i, order: (0, 0)),
            scratch_shapes=[pltpu.VMEM((rows, width), F32)],
        ),
        out_shape=jax.ShapeDtypeStruct((rows, width), BF16),
        compiler_params=pltpu.CompilerParams(vmem_limit_bytes=40 << 20),
        cost_estimate=pl.CostEstimate(flops=2 * rows * depth * count * width, bytes_accessed=2 * depth * count * width, transcendentals=0),
    )(order, *pieces, weight)


def gather_channels(block):
    count = lax.axis_size("ch")
    held = {0: block}
    bit = count // 2
    while bit:
        route = [(i, i ^ bit) for i in range(count)]
        held.update({at ^ bit: lax.ppermute(part, "ch", route) for at, part in list(held.items())})
        bit //= 2
    return [held[at] for at in range(count)]


def exchange(blocks):
    return lax.all_to_all(blocks, "seq", split_axis=0, concat_axis=0, tiled=True)


def send_spans(slices):
    count, rows, lanes = slices.shape
    devices = lax.axis_size("seq")
    cut = devices // count
    if cut > 1:
        slices = slices.reshape(count, rows, cut, lanes // cut).transpose(0, 2, 1, 3).reshape(devices, rows, lanes // cut)
    blocks = exchange(slices)
    return jnp.pad(blocks, ((0, 0), (0, 0), (0, lanes - lanes // cut))) if cut > 1 else blocks


def return_spans(blocks, count):
    devices, rows, lanes = blocks.shape
    cut = devices // count
    if cut == 1:
        return exchange(blocks)
    arrived = exchange(blocks[:, :, : lanes // cut])
    return arrived.reshape(count, cut, rows, lanes // cut).transpose(0, 2, 1, 3).reshape(count, rows, lanes)


OFFSETS = (0, 4, 1, 2, 3, 5, 6, 7)
FILTER_ORDER = (4, 1, 5, 2, 6, 3, 7)
SIGNAL_ORDER = (4, 1, 5, 2, 6, 3, 7)
RESULT_ORDER = (4, 1, 2, 3, 5, 6, 7)
EARLY = (0, 4, 1, 5)
LATE = (2, 6, 3, 7)
GROUP = 4
NEXT_OFFSETS = (1, 3, 7)
KEEP = 2
MIX_AFTER = 1
CHUNKS = ((0, 2), (2, 4), (4, 6), (6, 8))
PROJECTS = ((0, 1, 2), (3,))
PROJECT_COSTS = (0, 0)
PIECE_ORDER = (0, 2, 1, 3)


def cost(flops, scale=0):
    return pl.CostEstimate(flops=scale * flops, bytes_accessed=scale * flops // 128, transcendentals=0)


def lanes_at(order_ref, place):
    return pl.ds(pl.multiple_of(order_ref[place] * LANES, LANES), LANES)


def whole_specs(count):
    return [pl.BlockSpec(memory_space=pltpu.VMEM)] * count


def cut_kernel(filter_ref, *refs):
    own = lax.axis_index("seq")
    last_refs, (gate_top, value_top), out_refs = refs[:3], refs[3:5], refs[5:-1]
    rows, width = filter_ref.shape
    ends_ref = refs[-1]
    ends = [ref[...].astype(F32)[-KEEP:] for ref in last_refs]
    ends += [ref[...].astype(F32)[:KEEP] for ref in (gate_top, value_top)]
    ends.append(jnp.zeros((TILE - 5 * KEEP, width), F32))
    ends_ref[...] = jnp.concatenate(ends, axis=0).astype(BF16)
    for place, out_ref in enumerate(out_refs):
        at = pl.ds(pl.multiple_of((own ^ OFFSETS[place]) * LANES, LANES), LANES)
        out_ref[:rows] = filter_ref[:, at].astype(BF16)
        out_ref[rows : rows + TILE] = ends_ref[:, at]
        if OFFSETS[place] in NEXT_OFFSETS:
            for part in range(width // LANES):
                out_ref[rows + (1 + part) * TILE : rows + (2 + part) * TILE] = ends_ref[:, part * LANES : (part + 1) * LANES]


def cut_filter(long_filter, out_gate, in_gate, values):
    rows, width = long_filter.shape
    count = width // LANES
    heights = [rows + TILE * (1 + count * (offset in NEXT_OFFSETS)) for offset in OFFSETS]
    top = pl.BlockSpec((TILE, width), lambda i: (0, 0))
    last = pl.BlockSpec((TILE, width), lambda i: (rows // TILE - 1, 0))
    return pl.pallas_call(
        cut_kernel,
        grid=(1,),
        in_specs=[pl.BlockSpec((rows, width), lambda i: (0, 0))] + [last] * 3 + [top] * 2,
        out_specs=[pl.BlockSpec((height, LANES), lambda i: (0, 0)) for height in heights],
        out_shape=[jax.ShapeDtypeStruct((height, LANES), BF16) for height in heights],
        scratch_shapes=[pltpu.VMEM((TILE, width), BF16)],
        compiler_params=pltpu.CompilerParams(vmem_limit_bytes=CUT_VMEM << 20),
        cost_estimate=cost(rows * width),
    )(long_filter, out_gate, in_gate, values, in_gate, values)


def mix_slices_kernel(order_ref, gate_ref, value_ref, taps_ref, after_ref, *rest):
    del after_ref
    out_refs, (pad_a, pad_b) = rest[:-2], rest[-2:]
    keep = taps_ref.shape[1] - 1
    for place, out_ref in enumerate(out_refs):
        at = lanes_at(order_ref, place)
        none = jnp.zeros((keep, LANES), F32)
        first = short_conv(pad_a.at[place % 2], gate_ref[:, at].astype(F32), none, taps_ref[1, :, at])
        second = short_conv(pad_b.at[place % 2], value_ref[:, at].astype(F32), none, taps_ref[2, :, at])
        out_ref[...] = (first * second).astype(BF16)


def mix_slices(order, in_gate, values, taps, after):
    rows, width = in_gate.shape
    count = width // LANES
    return pl.pallas_call(
        mix_slices_kernel,
        in_specs=[pl.BlockSpec(memory_space=pltpu.SMEM)] + whole_specs(3) + [pl.BlockSpec(memory_space=pl.ANY)],
        out_specs=whole_specs(count),
        out_shape=[jax.ShapeDtypeStruct((rows, LANES), BF16)] * count,
        scratch_shapes=[pltpu.VMEM((2, rows + 8, LANES), F32)] * 2,
        compiler_params=pltpu.CompilerParams(vmem_limit_bytes=12 << 20),
        cost_estimate=cost(14 * rows * width, 1),
    )(order, in_gate, values, taps, after)


def side_slices_kernel(order_ref, late_ref, gate_ref, value_ref, *refs):
    *before_refs, taps_ref, gain_ref, late_out, skip_out = refs[:-3]
    pads = refs[-3:]
    rows, keep = late_ref.shape[0], taps_ref.shape[1] - 1
    own = order_ref[0]
    for place in range(late_out.shape[0]):
        at = lanes_at(order_ref, place)
        start = pl.multiple_of(rows + (1 + order_ref[place]) * TILE, TILE)
        rim = jnp.zeros((TILE, LANES), F32)
        for offset, ref in zip(NEXT_OFFSETS, before_refs, strict=True):
            given = ref[pl.ds(start, TILE), :].astype(F32)
            rim = jnp.where((own & offset) == (offset + 1) // 2, given, rim)
        late, first, second = (
            short_conv(
                pad.at[place % 2],
                ref[:, at].astype(F32),
                rim[which * keep : (which + 1) * keep],
                taps_ref[which, :, at],
            )
            for which, (pad, ref) in enumerate(zip(pads, (late_ref, gate_ref, value_ref), strict=True))
        )
        late_out[place] = late
        skip_out[place] = gain_ref[:, at] * (first * second)


def side_slices(order, out_gate, in_gate, values, filter_blocks, taps, skip_gain):
    rows, width = out_gate.shape
    count = width // LANES
    before = [filter_blocks[OFFSETS.index(offset)] for offset in NEXT_OFFSETS]
    return pl.pallas_call(
        side_slices_kernel,
        in_specs=[pl.BlockSpec(memory_space=pltpu.SMEM)] + whole_specs(5 + len(before)),
        out_specs=whole_specs(2),
        out_shape=[jax.ShapeDtypeStruct((count, rows, LANES), F32)] * 2,
        scratch_shapes=[pltpu.VMEM((2, rows + 8, LANES), F32)] * 3,
        compiler_params=pltpu.CompilerParams(vmem_limit_bytes=16 << 20),
        cost_estimate=cost(20 * rows * width, 1),
    )(order, out_gate, in_gate, values, *before, taps, skip_gain.reshape(1, width))


def spectra_into(order_ref, places, table, blocks, out_ref):
    columns = jnp.concatenate(blocks, axis=1)
    spectra = jnp.dot(table, jnp.concatenate([columns, columns], axis=0), preferred_element_type=F32)
    for at, place in enumerate(places):
        out_ref[order_ref[place]] = spectra[:, at * LANES : (at + 1) * LANES]


def with_first(order_ref, places, signal_refs, first_ref):
    blocks = []
    for place, ref in zip(places, signal_refs, strict=True):
        top = ref[:TILE].astype(F32)
        row = lax.broadcasted_iota(jnp.int32, top.shape, 0)
        top = jnp.where(row < KEEP, first_ref[order_ref[place]], top).astype(BF16)
        blocks.append(jnp.concatenate([top, ref[TILE:]], axis=0))
    return blocks


def filter_kernel(places, order_ref, table_ref, taps_ref, after_ref, *refs):
    del after_ref
    *block_refs, out_ref, first_ref, ends_ref = refs
    rows = table_ref.shape[0] // 2
    for base in range(0, len(block_refs), GROUP):
        blocks = [ref[:rows] for ref in block_refs[base : base + GROUP]]
        spectra_into(order_ref, places[base : base + GROUP], table_ref[...], blocks, out_ref)
    for place, ref in zip(places, block_refs, strict=True):
        ends_ref[order_ref[place]] = ref[rows : rows + TILE].astype(F32)
    count = taps_ref.shape[1]
    at = lanes_at(order_ref, 0)
    for block in range(len(block_refs)):
        mixed = None
        for which in range(2):
            top = ends_ref[block, (3 + which) * KEEP : (4 + which) * KEEP]
            end = jnp.zeros_like(top)
            if block:
                end = ends_ref[block - 1, (1 + which) * KEEP : (2 + which) * KEEP]
            joined = jnp.concatenate([end, top], axis=0)
            taps = taps_ref[1 + which, :, at]
            total = taps[0:1] * joined[KEEP:]
            for offset in range(1, count):
                total = total + taps[offset : offset + 1] * joined[KEEP - offset : 2 * KEEP - offset]
            mixed = total if mixed is None else mixed * total
        first_ref[block] = jnp.concatenate([mixed, jnp.zeros((TILE - KEEP, LANES), F32)], axis=0)


def filter_spectra_of(order, table, taps, blocks, places, after):
    rows, lanes = table.shape[0] // 2, blocks[0].shape[1]
    count = len(blocks)
    return pl.pallas_call(
        functools.partial(filter_kernel, places),
        in_specs=[pl.BlockSpec(memory_space=pltpu.SMEM)] + whole_specs(2) + [pl.BlockSpec(memory_space=pl.ANY)] + whole_specs(count),
        out_specs=whole_specs(2),
        out_shape=[
            jax.ShapeDtypeStruct((count, 2 * rows, lanes), F32),
            jax.ShapeDtypeStruct((count, TILE, lanes), F32),
        ],
        scratch_shapes=[pltpu.VMEM((count, TILE, lanes), F32)],
        compiler_params=pltpu.CompilerParams(vmem_limit_bytes=12 << 20),
        cost_estimate=cost(8 * count * rows * rows * lanes, 1),
    )(order, table, taps, after, *[blocks[place] for place in places])


def early_kernel(places, order_ref, table_ref, first_ref, *refs):
    blocks = with_first(order_ref, places, refs[:-1], first_ref)
    spectra_into(order_ref, places, table_ref[...], blocks, refs[-1])


def early_spectra_of(order, table, first, blocks, places):
    rows, lanes = blocks[0].shape
    given = len(places)
    return pl.pallas_call(
        functools.partial(early_kernel, places),
        in_specs=[pl.BlockSpec(memory_space=pltpu.SMEM)] + whole_specs(2 + given),
        out_specs=pl.BlockSpec(memory_space=pltpu.VMEM),
        out_shape=jax.ShapeDtypeStruct((len(blocks), 2 * rows, lanes), F32),
        compiler_params=pltpu.CompilerParams(vmem_limit_bytes=12 << 20),
        cost_estimate=cost(8 * given * rows * rows * lanes, 1),
    )(order, table, first, *[blocks[place] for place in places])


def multiply_spectra(filter_ref, spectra_ref, high_ref, low_ref):
    blocks, depth, _ = spectra_ref.shape
    rows = depth // 2
    half, tile = rows // 2, 16

    def multiply(base, turn):
        def body(step, carry):
            start = pl.multiple_of(base + step * tile, tile)
            real, imag = pl.ds(start, tile), pl.ds(rows + start, tile)
            before = None
            for at in range(blocks):
                sum_real = sum_imag = None
                for other in range(at + 1):
                    a_real, a_imag = filter_ref[other, real, :], filter_ref[other, imag, :]
                    b_real, b_imag = spectra_ref[at - other, real, :], spectra_ref[at - other, imag, :]
                    part_real = a_real * b_real - a_imag * b_imag
                    part_imag = a_real * b_imag + a_imag * b_real
                    sum_real = part_real if sum_real is None else sum_real + part_real
                    sum_imag = part_imag if sum_imag is None else sum_imag + part_imag
                out_real, out_imag = sum_real, sum_imag
                if before is not None:
                    out_real = sum_real - turn * before[1]
                    out_imag = sum_imag + turn * before[0]
                before = (sum_real, sum_imag)
                for place, value in ((real, out_real), (imag, out_imag)):
                    high = value.astype(BF16)
                    high_ref[at, place, :] = high
                    low_ref[at, place, :] = (value - high.astype(F32)).astype(BF16)
            return carry

        lax.fori_loop(0, half // tile, body, 0)

    multiply(0, 1.0)
    multiply(half, -1.0)


def inverse_into(order_ref, base, inverse, high_ref, low_ref, out_refs):
    places = [order_ref[base + at] for at in range(len(out_refs))]
    high = jnp.concatenate([high_ref[place] for place in places], axis=1)
    low = jnp.concatenate([low_ref[place] for place in places], axis=1)
    result = jnp.dot(inverse, jnp.concatenate([high, high, low], axis=0), preferred_element_type=F32).astype(BF16)
    for at, out_ref in enumerate(out_refs):
        out_ref[...] = result[:, at * LANES : (at + 1) * LANES]


def conv_slices_kernel(places, order_ref, table_ref, inverse_ref, filter_ref, early_ref, first_ref, *refs):
    del early_ref
    count = filter_ref.shape[0]
    signal_refs = refs[: len(places)]
    spectra_ref, *out_refs, high_ref, low_ref = refs[-count - 3 :]
    blocks = with_first(order_ref, places, signal_refs, first_ref)
    spectra_into(order_ref, places, table_ref[...], blocks, spectra_ref)
    multiply_spectra(filter_ref, spectra_ref, high_ref, low_ref)
    for base in range(0, count, GROUP):
        inverse_into(order_ref, base, inverse_ref[...], high_ref, low_ref, out_refs[base : base + GROUP])


def conv_slices(order, table, inverse, filter_spectra, early_spectra, first, blocks, places, after):
    rows, lanes = blocks[0].shape
    count = filter_spectra.shape[0]
    _, *outs = pl.pallas_call(
        functools.partial(conv_slices_kernel, places),
        in_specs=[pl.BlockSpec(memory_space=pltpu.SMEM)] + whole_specs(5 + len(places)) + [pl.BlockSpec(memory_space=pl.ANY)] * len(after),
        out_specs=whole_specs(1 + count),
        out_shape=[jax.ShapeDtypeStruct((count, 2 * rows, lanes), F32)]
        + [jax.ShapeDtypeStruct((rows, lanes), BF16)] * count,
        input_output_aliases={4: 0},
        scratch_shapes=[pltpu.VMEM((count, 2 * rows, lanes), BF16)] * 2,
        compiler_params=pltpu.CompilerParams(vmem_limit_bytes=20 << 20),
        cost_estimate=cost(14 * count * rows * rows * lanes, 1),
    )(order, table, inverse, filter_spectra, early_spectra, first, *[blocks[place] for place in places], *after)
    return outs


def gate_chunk_kernel(first, late_ref, skip_ref, *refs):
    out_ref = refs[-1]
    for at, long_ref in enumerate(refs[:-1]):
        mixed = late_ref[first + at] * (long_ref[...].astype(F32) + skip_ref[first + at])
        out_ref[:, at * LANES : (at + 1) * LANES] = mixed.astype(BF16)


def gate_chunk(late, skip, long_blocks, first):
    rows, lanes = long_blocks[0].shape
    count = len(long_blocks)
    return pl.pallas_call(
        functools.partial(gate_chunk_kernel, first),
        in_specs=whole_specs(2 + count),
        out_specs=pl.BlockSpec(memory_space=pltpu.VMEM),
        out_shape=jax.ShapeDtypeStruct((rows, count * lanes), BF16),
        compiler_params=pltpu.CompilerParams(vmem_limit_bytes=8 << 20),
        cost_estimate=cost(3 * count * rows * lanes),
    )(late, skip, *long_blocks)


def weight_kernel(order_ref, channel_ref, weight_ref, out_ref, arrived):
    count, owners = out_ref.shape[:2]
    depth = weight_ref.shape[0] // owners
    copies = []
    for place in range(count):
        for offset in range(owners):
            start = pl.multiple_of((channel_ref[0] ^ offset) * depth + order_ref[place] * LANES, LANES)
            rows = weight_ref.at[pl.ds(start, LANES), :]
            copies.append(pltpu.make_async_copy(rows, out_ref.at[place, offset], arrived.at[place, offset]))
    for copy in copies:
        copy.start()
    for copy in copies:
        copy.wait()


def weight_rows_of(order, channel, weight):
    depth, width = weight.shape
    count, owners = order.shape[0], len(PIECE_ORDER)
    return pl.pallas_call(
        weight_kernel,
        in_specs=[pl.BlockSpec(memory_space=pltpu.SMEM)] * 2 + [pl.BlockSpec(memory_space=pl.ANY)],
        out_specs=pl.BlockSpec(memory_space=pltpu.VMEM),
        out_shape=jax.ShapeDtypeStruct((count, owners, LANES, width), BF16),
        scratch_shapes=[pltpu.SemaphoreType.DMA((count, owners))],
        compiler_params=pltpu.CompilerParams(vmem_limit_bytes=10 << 20),
        cost_estimate=pl.CostEstimate(flops=0, bytes_accessed=4 * depth * width, transcendentals=0),
    )(order, channel, weight)


def add_chunk(chunk, rows_ref, piece_refs, total):
    pieces = jnp.concatenate([ref[...] for ref in piece_refs], axis=1)
    rows = [rows_ref[place, offset] for offset in PIECE_ORDER for place in range(*CHUNKS[chunk])]
    product = jnp.dot(pieces, jnp.concatenate(rows, axis=0), preferred_element_type=F32)
    return product if total is None else total + product


def join_kernel(*refs):
    refs[-1][...] = jnp.concatenate([ref[...] for ref in refs[:-1]], axis=1)


def join(blocks):
    rows, lanes = blocks[0].shape
    count = len(blocks)
    return pl.pallas_call(
        join_kernel,
        in_specs=whole_specs(count),
        out_specs=pl.BlockSpec(memory_space=pltpu.VMEM),
        out_shape=jax.ShapeDtypeStruct((rows, count * lanes), blocks[0].dtype),
        compiler_params=pltpu.CompilerParams(vmem_limit_bytes=8 << 20),
        cost_estimate=cost(4 * rows * lanes),
    )(*blocks)


def project_kernel_slices(chunks, rows_ref, *refs):
    refs, more, out_ref = refs[: 2 * len(chunks)], refs[2 * len(chunks) : -1], refs[-1]
    total = more[0][...] if more else None
    for at, chunk in enumerate(chunks):
        total = add_chunk(chunk, rows_ref, refs[2 * at : 2 * at + 2], total)
    out_ref[...] = total.astype(out_ref.dtype)


def project_slices(weight_rows, chunks, pieces, total, out_type, scale):
    rows = pieces[0].shape[0]
    width = weight_rows.shape[3]
    more = () if total is None else (total,)
    return pl.pallas_call(
        functools.partial(project_kernel_slices, chunks),
        in_specs=whole_specs(1 + len(pieces) + len(more)),
        out_specs=pl.BlockSpec(memory_space=pltpu.VMEM),
        out_shape=jax.ShapeDtypeStruct((rows, width), out_type),
        compiler_params=pltpu.CompilerParams(vmem_limit_bytes=14 << 20),
        cost_estimate=cost(2 * rows * sum(piece.shape[1] for piece in pieces) * width, scale),
    )(weight_rows, *pieces, *more)


def swap_blocks(blocks, sequence):
    count = lax.axis_size("seq")
    arrived = list(blocks)
    for offset in sequence:
        place = OFFSETS.index(offset)
        arrived[place] = lax.ppermute(blocks[place], "seq", [(i, i ^ offset) for i in range(count)])
    return arrived


def on_device_slices(out_gate, in_gate, values, short_filter, long_filter, skip_gain, out_weight):
    rows, width = out_gate.shape
    devices = lax.axis_size("seq")
    table, inverse = transform_tables(rows)
    order = jnp.bitwise_xor(lax.axis_index("seq"), jnp.array(OFFSETS, jnp.int32))
    channel = lax.axis_index("ch").reshape(1)

    filter_blocks = swap_blocks(cut_filter(long_filter, out_gate, in_gate, values), FILTER_ORDER)
    sent = (0, *(OFFSETS.index(offset) for offset in FILTER_ORDER))
    mixed_blocks = swap_blocks(
        mix_slices(order, in_gate, values, short_filter, filter_blocks[OFFSETS.index(MIX_AFTER)]), SIGNAL_ORDER
    )
    late, skip = side_slices(order, out_gate, in_gate, values, filter_blocks, short_filter, skip_gain)
    weight_rows = weight_rows_of(order, channel, out_weight)
    filter_spectra, first = filter_spectra_of(order, table, short_filter, filter_blocks, sent, weight_rows)
    early, last = (tuple(OFFSETS.index(offset) for offset in group) for group in (EARLY, LATE))
    early_spectra = early_spectra_of(order, table, first, mixed_blocks, early)
    long_blocks = conv_slices(order, table, inverse, filter_spectra, early_spectra, first, mixed_blocks, last, (late, weight_rows))
    arrived = swap_blocks(long_blocks, RESULT_ORDER)

    pieces = []
    for start, stop in CHUNKS:
        mixed = gate_chunk(late, skip, arrived[start:stop], start)
        across = lax.ppermute(mixed, "ch", [(i, i ^ 2) for i in range(4)])
        joined = join([mixed, across])
        pieces.append((joined, lax.ppermute(joined, "ch", [(i, i ^ 1) for i in range(4)])))
    total = None
    for chunks, scale in zip(PROJECTS, PROJECT_COSTS, strict=True):
        kind = BF16 if chunks == PROJECTS[-1] else F32
        total = project_slices(weight_rows, chunks, [piece for chunk in chunks for piece in pieces[chunk]], total, kind, scale)
    return total


def on_device_spans(out_gate, in_gate, values, short_filter, long_filter, skip_gain, out_weight):
    rows, width = out_gate.shape
    devices = lax.axis_size("seq")
    slices = width // LANES
    taps = short_filter.shape[1]
    table, inverse = transform_tables(rows)

    rim = jnp.stack([a[rows - (taps - 1) :] for a in (out_gate, in_gate, values)])
    rim = lax.ppermute(rim, "seq", [(i, i + 1) for i in range(devices - 1)])
    rims = rim.astype(F32)

    filter_slices = long_filter.astype(BF16).reshape(rows, slices, LANES).transpose(1, 0, 2)
    filter_whole = send_spans(filter_slices)
    mixed_whole = send_spans(mix_inputs(in_gate, values, rims, short_filter))

    filter_spectra = forward(table, filter_whole)
    late, skip = side_terms(out_gate, in_gate, values, rims, short_filter, skip_gain)
    long_parts = block_conv(table, inverse, mixed_whole, filter_spectra, ROW_PARTS)
    channel = lax.axis_index("ch")
    order = jnp.bitwise_xor(channel, jnp.arange(lax.axis_size("ch"), dtype=jnp.int32))
    outs = []
    for part, long_part in enumerate(long_parts):
        returned = return_spans(long_part, slices)
        mixed = gate_rows(returned, late, skip, part)
        outs.append(project(gather_channels(mixed), out_weight, order))
    return jnp.concatenate(outs, axis=0)


def solution(mesh):
    devices = mesh.shape["seq"]

    def on_device(*arrays):
        width = arrays[0].shape[1]
        taps = arrays[3].shape[1]
        sliced = taps == KEEP + 1 and devices == len(OFFSETS) and width == devices * LANES and mesh.shape["ch"] == len(PIECE_ORDER)
        return (on_device_slices if sliced else on_device_spans)(*arrays)

    return jax.shard_map(
        on_device,
        mesh=mesh,
        in_specs=(
            P("seq", "ch"),
            P("seq", "ch"),
            P("seq", "ch"),
            P(None, None, "ch"),
            P("seq", "ch"),
            P("ch"),
            P(None, "ch"),
        ),
        out_specs=P("seq", "ch"),
        check_vma=False,
    )
```

```python
import functools
import math

import jax
import jax.numpy as jnp
import ml_dtypes
import numpy as np
from jax import lax
from jax.experimental import pallas as pl
from jax.experimental.pallas import tpu as pltpu
from jax.sharding import PartitionSpec as P

LANES = 128
TILE = 16
CUT_VMEM = 56
ROW_PARTS = 2
BF16 = jnp.bfloat16
F32 = jnp.float32


def two_terms(table):
    high = table.astype(ml_dtypes.bfloat16)
    low = (table - high.astype(np.float64)).astype(ml_dtypes.bfloat16)
    return high, low


def transform_tables(rows):
    order = np.concatenate([np.arange(0, rows, 2), np.arange(1, rows, 2)])
    product = (2 * order[:, None] + 1) * np.arange(rows)[None, :] % (4 * rows)
    angles = product * (math.pi / (2 * rows))
    forward = np.concatenate([np.cos(angles), -np.sin(angles)])
    fwd_high, fwd_low = two_terms(forward)
    inv_high, inv_low = two_terms(forward.T / rows)
    return (
        np.concatenate([fwd_high, fwd_low], axis=1),
        np.concatenate([inv_high, inv_low, inv_high], axis=1),
    )


def short_conv(pad_ref, block, rim, taps):
    rows = block.shape[0]
    pad_ref[pl.ds(8 - rim.shape[0], rim.shape[0]), :] = rim
    pad_ref[pl.ds(8, rows), :] = block
    total = taps[0:1] * block
    for offset in range(1, taps.shape[0]):
        total = total + taps[offset : offset + 1] * pad_ref[pl.ds(8 - offset, rows), :]
    return total


def mix_kernel(gate_ref, value_ref, rim_ref, taps_ref, out_ref, pad_a, pad_b):
    first = short_conv(pad_a, gate_ref[...].astype(F32), rim_ref[1], taps_ref[1])
    second = short_conv(pad_b, value_ref[...].astype(F32), rim_ref[2], taps_ref[2])
    out_ref[0] = (first * second).astype(out_ref.dtype)


def mix_inputs(in_gate, values, rims, taps):
    rows, width = in_gate.shape
    span = LANES
    parts = width // span
    return pl.pallas_call(
        mix_kernel,
        grid=(parts,),
        in_specs=[
            pl.BlockSpec((rows, span), lambda i: (0, i)),
            pl.BlockSpec((rows, span), lambda i: (0, i)),
            pl.BlockSpec((3, taps.shape[1] - 1, span), lambda i: (0, 0, i)),
            pl.BlockSpec((3, taps.shape[1], span), lambda i: (0, 0, i)),
        ],
        out_specs=pl.BlockSpec((1, rows, span), lambda i: (i, 0, 0)),
        out_shape=jax.ShapeDtypeStruct((parts, rows, span), BF16),
        scratch_shapes=[pltpu.VMEM((rows + 8, span), F32)] * 2,
        cost_estimate=pl.CostEstimate(flops=12 * rows * width, bytes_accessed=6 * rows * width, transcendentals=0),
    )(in_gate, values, rims, taps)


def side_kernel(late_ref, gate_ref, value_ref, rim_ref, taps_ref, skip_ref, late_out, skip_out, pad_a, pad_b, pad_c):
    late_out[...] = short_conv(pad_a, late_ref[...].astype(F32), rim_ref[0], taps_ref[0])
    first = short_conv(pad_b, gate_ref[...].astype(F32), rim_ref[1], taps_ref[1])
    second = short_conv(pad_c, value_ref[...].astype(F32), rim_ref[2], taps_ref[2])
    skip_out[...] = skip_ref[...] * (first * second)


def side_terms(out_gate, in_gate, values, rims, taps, skip_gain):
    rows, width = in_gate.shape
    span = min(width, 128)
    column = pl.BlockSpec((rows, span), lambda i: (0, i))
    return pl.pallas_call(
        side_kernel,
        grid=(width // span,),
        in_specs=[
            column,
            column,
            column,
            pl.BlockSpec((3, taps.shape[1] - 1, span), lambda i: (0, 0, i)),
            pl.BlockSpec((3, taps.shape[1], span), lambda i: (0, 0, i)),
            pl.BlockSpec((1, span), lambda i: (0, i)),
        ],
        out_specs=[column, column],
        out_shape=[jax.ShapeDtypeStruct((rows, width), F32)] * 2,
        scratch_shapes=[pltpu.VMEM((rows + 8, span), F32)] * 3,
        cost_estimate=pl.CostEstimate(flops=20 * rows * width, bytes_accessed=14 * rows * width, transcendentals=0),
    )(out_gate, in_gate, values, rims, taps, skip_gain.reshape(1, width))


def pair_of(ref, at):
    return jnp.concatenate([ref[at], ref[at + 1]], axis=1)


def forward_into(table_ref, signal_ref, out_ref):
    blocks, _, lanes = signal_ref.shape

    @pl.loop(0, blocks // 2)
    def _(step):
        pair = pair_of(signal_ref, 2 * step)
        spectra = jnp.dot(table_ref[...], jnp.concatenate([pair, pair], axis=0), preferred_element_type=F32)
        out_ref[2 * step] = spectra[:, :lanes]
        out_ref[2 * step + 1] = spectra[:, lanes:]


def forward_kernel(table_ref, signal_ref, out_ref):
    forward_into(table_ref, signal_ref, out_ref)


def forward(table, signal):
    blocks, rows, lanes = signal.shape
    return pl.pallas_call(
        forward_kernel,
        out_shape=jax.ShapeDtypeStruct((blocks, 2 * rows, lanes), F32),
        compiler_params=pltpu.CompilerParams(vmem_limit_bytes=60 << 20),
        cost_estimate=pl.CostEstimate(flops=8 * blocks * rows * rows * lanes, bytes_accessed=10 * blocks * rows * lanes, transcendentals=0),
    )(table, signal)


def conv_kernel(table_ref, inverse_ref, signal_ref, filter_ref, *rest):
    out_refs, (spectra_ref, high_ref, low_ref) = rest[:-3], rest[-3:]
    blocks, rows, lanes = signal_ref.shape
    forward_into(table_ref, signal_ref, spectra_ref)
    half = rows // 2
    tile = 16

    def multiply(base, turn):
        def body(step, carry):
            start = pl.multiple_of(base + step * tile, tile)
            real, imag = pl.ds(start, tile), pl.ds(rows + start, tile)
            before = None
            for at in range(blocks):
                sum_real = sum_imag = None
                for other in range(at + 1):
                    a_real, a_imag = filter_ref[other, real, :], filter_ref[other, imag, :]
                    b_real, b_imag = spectra_ref[at - other, real, :], spectra_ref[at - other, imag, :]
                    part_real = a_real * b_real - a_imag * b_imag
                    part_imag = a_real * b_imag + a_imag * b_real
                    sum_real = part_real if sum_real is None else sum_real + part_real
                    sum_imag = part_imag if sum_imag is None else sum_imag + part_imag
                out_real, out_imag = sum_real, sum_imag
                if before is not None:
                    out_real = sum_real - turn * before[1]
                    out_imag = sum_imag + turn * before[0]
                before = (sum_real, sum_imag)
                for place, value in ((real, out_real), (imag, out_imag)):
                    high = value.astype(BF16)
                    high_ref[at, place, :] = high
                    low_ref[at, place, :] = (value - high.astype(F32)).astype(BF16)
            return carry

        lax.fori_loop(0, half // tile, body, 0)

    multiply(0, 1.0)
    multiply(half, -1.0)

    part_rows = rows // len(out_refs)
    for part, out_ref in enumerate(out_refs):

        @pl.loop(0, blocks // 2)
        def _(step):
            high, low = pair_of(high_ref, 2 * step), pair_of(low_ref, 2 * step)
            result = jnp.dot(
                inverse_ref[pl.ds(part * part_rows, part_rows), :],
                jnp.concatenate([high, high, low], axis=0),
                preferred_element_type=F32,
            ).astype(out_ref.dtype)
            out_ref[2 * step] = result[:, :lanes]
            out_ref[2 * step + 1] = result[:, lanes:]


def block_conv(table, inverse, signal, filter_spectra, parts):
    blocks, rows, lanes = signal.shape
    return pl.pallas_call(
        conv_kernel,
        out_shape=[jax.ShapeDtypeStruct((blocks, rows // parts, lanes), BF16)] * parts,
        scratch_shapes=[
            pltpu.VMEM((blocks, 2 * rows, lanes), F32),
            pltpu.VMEM((blocks, 2 * rows, lanes), BF16),
            pltpu.VMEM((blocks, 2 * rows, lanes), BF16),
        ],
        compiler_params=pltpu.CompilerParams(vmem_limit_bytes=60 << 20),
        cost_estimate=pl.CostEstimate(flops=20 * blocks * rows * rows * lanes, bytes_accessed=10 * blocks * rows * lanes, transcendentals=0),
    )(table, inverse, signal, filter_spectra)


def gate_kernel(long_ref, late_ref, skip_ref, out_ref):
    out_ref[...] = (late_ref[...] * (long_ref[0].astype(F32) + skip_ref[...])).astype(out_ref.dtype)


def gate_rows(long_part, late, skip, part):
    blocks, rows, lanes = long_part.shape
    column = pl.BlockSpec((rows, lanes), lambda i: (part, i))
    return pl.pallas_call(
        gate_kernel,
        grid=(blocks,),
        in_specs=[pl.BlockSpec((1, rows, lanes), lambda i: (i, 0, 0)), column, column],
        out_specs=pl.BlockSpec((rows, lanes), lambda i: (0, i)),
        out_shape=jax.ShapeDtypeStruct((rows, blocks * lanes), BF16),
        cost_estimate=pl.CostEstimate(flops=3 * blocks * rows * lanes, bytes_accessed=12 * blocks * rows * lanes, transcendentals=0),
    )(long_part, late, skip)


def project_kernel(order_ref, *refs):
    del order_ref
    *mixed_refs, weight_ref, out_ref, total_ref = refs
    step = pl.program_id(0)
    for at, mixed_ref in enumerate(mixed_refs):

        @pl.when(step == at)
        def _():
            product = jnp.dot(mixed_ref[...], weight_ref[...], preferred_element_type=F32)
            total_ref[...] = product if at == 0 else total_ref[...] + product

    @pl.when(step == len(mixed_refs) - 1)
    def _():
        out_ref[...] = total_ref[...].astype(out_ref.dtype)


def project(pieces, weight, order):
    rows, depth = pieces[0].shape
    width = weight.shape[1]
    count = len(pieces)
    whole = pl.BlockSpec((rows, depth), lambda i, order: (0, 0))
    return pl.pallas_call(
        project_kernel,
        grid_spec=pltpu.PrefetchScalarGridSpec(
            num_scalar_prefetch=1,
            grid=(count,),
            in_specs=[whole] * count + [pl.BlockSpec((depth, width), lambda i, order: (order[i], 0))],
            out_specs=pl.BlockSpec((rows, width), lambda i, order: (0, 0)),
            scratch_shapes=[pltpu.VMEM((rows, width), F32)],
        ),
        out_shape=jax.ShapeDtypeStruct((rows, width), BF16),
        compiler_params=pltpu.CompilerParams(vmem_limit_bytes=40 << 20),
        cost_estimate=pl.CostEstimate(flops=2 * rows * depth * count * width, bytes_accessed=2 * depth * count * width, transcendentals=0),
    )(order, *pieces, weight)


def gather_channels(block):
    count = lax.axis_size("ch")
    held = {0: block}
    bit = count // 2
    while bit:
        route = [(i, i ^ bit) for i in range(count)]
        held.update({at ^ bit: lax.ppermute(part, "ch", route) for at, part in list(held.items())})
        bit //= 2
    return [held[at] for at in range(count)]


def exchange(blocks):
    return lax.all_to_all(blocks, "seq", split_axis=0, concat_axis=0, tiled=True)


def send_spans(slices):
    count, rows, lanes = slices.shape
    devices = lax.axis_size("seq")
    cut = devices // count
    if cut > 1:
        slices = slices.reshape(count, rows, cut, lanes // cut).transpose(0, 2, 1, 3).reshape(devices, rows, lanes // cut)
    blocks = exchange(slices)
    return jnp.pad(blocks, ((0, 0), (0, 0), (0, lanes - lanes // cut))) if cut > 1 else blocks


def return_spans(blocks, count):
    devices, rows, lanes = blocks.shape
    cut = devices // count
    if cut == 1:
        return exchange(blocks)
    arrived = exchange(blocks[:, :, : lanes // cut])
    return arrived.reshape(count, cut, rows, lanes // cut).transpose(0, 2, 1, 3).reshape(count, rows, lanes)


OFFSETS = (0, 4, 1, 2, 3, 5, 6, 7)
FILTER_ORDER = (4, 1, 5, 2, 6, 3, 7)
SIGNAL_ORDER = (4, 1, 5, 2, 6, 3, 7)
RESULT_ORDER = (4, 1, 2, 3, 5, 6, 7)
EARLY = (0, 4, 1, 5)
LATE = (2, 6, 3, 7)
GROUP = 4
NEXT_OFFSETS = (1, 3, 7)
KEEP = 2
MIX_AFTER = 1
CHUNKS = ((0, 2), (2, 4), (4, 6), (6, 8))
PROJECTS = ((0, 1, 2), (3,))
PROJECT_COSTS = (0, 0)
PIECE_ORDER = (0, 2, 1, 3)


def cost(flops, scale=0):
    return pl.CostEstimate(flops=scale * flops, bytes_accessed=scale * flops // 128, transcendentals=0)


def lanes_at(order_ref, place):
    return pl.ds(pl.multiple_of(order_ref[place] * LANES, LANES), LANES)


def whole_specs(count):
    return [pl.BlockSpec(memory_space=pltpu.VMEM)] * count


def cut_kernel(filter_ref, *refs):
    own = lax.axis_index("seq")
    last_refs, (gate_top, value_top), out_refs = refs[:3], refs[3:5], refs[5:-1]
    rows, width = filter_ref.shape
    ends_ref = refs[-1]
    ends = [ref[...].astype(F32)[-KEEP:] for ref in last_refs]
    ends += [ref[...].astype(F32)[:KEEP] for ref in (gate_top, value_top)]
    ends.append(jnp.zeros((TILE - 5 * KEEP, width), F32))
    ends_ref[...] = jnp.concatenate(ends, axis=0)
    for place, out_ref in enumerate(out_refs):
        at = pl.ds(pl.multiple_of((own ^ OFFSETS[place]) * LANES, LANES), LANES)
        out_ref[:rows] = filter_ref[:, at].astype(BF16)
        out_ref[rows : rows + TILE] = ends_ref[:, at].astype(BF16)
        if OFFSETS[place] in NEXT_OFFSETS:
            for part in range(width // (2 * LANES)):
                pair = [ends_ref[: TILE // 2, q * LANES : (q + 1) * LANES] for q in (2 * part, 2 * part + 1)]
                out_ref[rows + (1 + part) * TILE : rows + (2 + part) * TILE] = jnp.concatenate(pair, axis=0).astype(BF16)


def cut_filter(long_filter, out_gate, in_gate, values):
    rows, width = long_filter.shape
    count = width // LANES
    heights = [rows + TILE * (1 + count // 2 * (offset in NEXT_OFFSETS)) for offset in OFFSETS]
    top = pl.BlockSpec((TILE, width), lambda i: (0, 0))
    last = pl.BlockSpec((TILE, width), lambda i: (rows // TILE - 1, 0))
    return pl.pallas_call(
        cut_kernel,
        grid=(1,),
        in_specs=[pl.BlockSpec((rows, width), lambda i: (0, 0))] + [last] * 3 + [top] * 2,
        out_specs=[pl.BlockSpec((height, LANES), lambda i: (0, 0)) for height in heights],
        out_shape=[jax.ShapeDtypeStruct((height, LANES), BF16) for height in heights],
        scratch_shapes=[pltpu.VMEM((TILE, width), F32)],
        compiler_params=pltpu.CompilerParams(vmem_limit_bytes=CUT_VMEM << 20),
        cost_estimate=cost(rows * width),
    )(long_filter, out_gate, in_gate, values, in_gate, values)


def mix_slices_kernel(order_ref, gate_ref, value_ref, taps_ref, after_ref, *rest):
    del after_ref
    out_refs, (pad_a, pad_b) = rest[:-2], rest[-2:]
    keep = taps_ref.shape[1] - 1
    for place, out_ref in enumerate(out_refs):
        at = lanes_at(order_ref, place)
        none = jnp.zeros((keep, LANES), F32)
        first = short_conv(pad_a.at[place % 2], gate_ref[:, at].astype(F32), none, taps_ref[1, :, at])
        second = short_conv(pad_b.at[place % 2], value_ref[:, at].astype(F32), none, taps_ref[2, :, at])
        out_ref[...] = (first * second).astype(BF16)


def mix_slices(order, in_gate, values, taps, after):
    rows, width = in_gate.shape
    count = width // LANES
    return pl.pallas_call(
        mix_slices_kernel,
        in_specs=[pl.BlockSpec(memory_space=pltpu.SMEM)] + whole_specs(3) + [pl.BlockSpec(memory_space=pl.ANY)],
        out_specs=whole_specs(count),
        out_shape=[jax.ShapeDtypeStruct((rows, LANES), BF16)] * count,
        scratch_shapes=[pltpu.VMEM((2, rows + 8, LANES), F32)] * 2,
        compiler_params=pltpu.CompilerParams(vmem_limit_bytes=12 << 20),
        cost_estimate=cost(14 * rows * width, 1),
    )(order, in_gate, values, taps, after)


def side_slices_kernel(order_ref, late_ref, gate_ref, value_ref, *refs):
    *before_refs, taps_ref, gain_ref, late_out, skip_out = refs[:-3]
    pads = refs[-3:]
    rows, keep = late_ref.shape[0], taps_ref.shape[1] - 1
    own = order_ref[0]
    for place in range(late_out.shape[0]):
        at = lanes_at(order_ref, place)
        start = pl.multiple_of(rows + (1 + order_ref[place] // 2) * TILE, TILE)
        rim = jnp.zeros((TILE // 2, LANES), F32)
        for offset, ref in zip(NEXT_OFFSETS, before_refs, strict=True):
            given = ref[pl.ds(start, TILE), :].astype(F32)
            given = jnp.where(order_ref[place] % 2 == 1, given[TILE // 2 :], given[: TILE // 2])
            rim = jnp.where((own & offset) == (offset + 1) // 2, given, rim)
        late, first, second = (
            short_conv(
                pad.at[place % 2],
                ref[:, at].astype(F32),
                rim[which * keep : (which + 1) * keep],
                taps_ref[which, :, at],
            )
            for which, (pad, ref) in enumerate(zip(pads, (late_ref, gate_ref, value_ref), strict=True))
        )
        late_out[place] = late
        skip_out[place] = gain_ref[:, at] * (first * second)


def side_slices(order, out_gate, in_gate, values, filter_blocks, taps, skip_gain):
    rows, width = out_gate.shape
    count = width // LANES
    before = [filter_blocks[OFFSETS.index(offset)] for offset in NEXT_OFFSETS]
    return pl.pallas_call(
        side_slices_kernel,
        in_specs=[pl.BlockSpec(memory_space=pltpu.SMEM)] + whole_specs(5 + len(before)),
        out_specs=whole_specs(2),
        out_shape=[jax.ShapeDtypeStruct((count, rows, LANES), F32)] * 2,
        scratch_shapes=[pltpu.VMEM((2, rows + 8, LANES), F32)] * 3,
        compiler_params=pltpu.CompilerParams(vmem_limit_bytes=16 << 20),
        cost_estimate=cost(20 * rows * width, 1),
    )(order, out_gate, in_gate, values, *before, taps, skip_gain.reshape(1, width))


def spectra_into(order_ref, places, table, blocks, out_ref):
    columns = jnp.concatenate(blocks, axis=1)
    spectra = jnp.dot(table, jnp.concatenate([columns, columns], axis=0), preferred_element_type=F32)
    for at, place in enumerate(places):
        out_ref[order_ref[place]] = spectra[:, at * LANES : (at + 1) * LANES]


def with_first(order_ref, places, signal_refs, first_ref):
    blocks = []
    for place, ref in zip(places, signal_refs, strict=True):
        top = ref[:TILE].astype(F32)
        row = lax.broadcasted_iota(jnp.int32, top.shape, 0)
        top = jnp.where(row < KEEP, first_ref[order_ref[place]], top).astype(BF16)
        blocks.append(jnp.concatenate([top, ref[TILE:]], axis=0))
    return blocks


def filter_kernel(places, order_ref, table_ref, taps_ref, after_ref, *refs):
    del after_ref
    *block_refs, out_ref, first_ref, ends_ref = refs
    rows = table_ref.shape[0] // 2
    for base in range(0, len(block_refs), GROUP):
        blocks = [ref[:rows] for ref in block_refs[base : base + GROUP]]
        spectra_into(order_ref, places[base : base + GROUP], table_ref[...], blocks, out_ref)
    for place, ref in zip(places, block_refs, strict=True):
        ends_ref[order_ref[place]] = ref[rows : rows + TILE].astype(F32)
    count = taps_ref.shape[1]
    at = lanes_at(order_ref, 0)
    for block in range(len(block_refs)):
        mixed = None
        for which in range(2):
            top = ends_ref[block, (3 + which) * KEEP : (4 + which) * KEEP]
            end = jnp.zeros_like(top)
            if block:
                end = ends_ref[block - 1, (1 + which) * KEEP : (2 + which) * KEEP]
            joined = jnp.concatenate([end, top], axis=0)
            taps = taps_ref[1 + which, :, at]
            total = taps[0:1] * joined[KEEP:]
            for offset in range(1, count):
                total = total + taps[offset : offset + 1] * joined[KEEP - offset : 2 * KEEP - offset]
            mixed = total if mixed is None else mixed * total
        first_ref[block] = jnp.concatenate([mixed, jnp.zeros((TILE - KEEP, LANES), F32)], axis=0)


def filter_spectra_of(order, table, taps, blocks, places, after):
    rows, lanes = table.shape[0] // 2, blocks[0].shape[1]
    count = len(blocks)
    return pl.pallas_call(
        functools.partial(filter_kernel, places),
        in_specs=[pl.BlockSpec(memory_space=pltpu.SMEM)] + whole_specs(2) + [pl.BlockSpec(memory_space=pl.ANY)] + whole_specs(count),
        out_specs=whole_specs(2),
        out_shape=[
            jax.ShapeDtypeStruct((count, 2 * rows, lanes), F32),
            jax.ShapeDtypeStruct((count, TILE, lanes), F32),
        ],
        scratch_shapes=[pltpu.VMEM((count, TILE, lanes), F32)],
        compiler_params=pltpu.CompilerParams(vmem_limit_bytes=12 << 20),
        cost_estimate=cost(8 * count * rows * rows * lanes, 1),
    )(order, table, taps, after, *[blocks[place] for place in places])


def early_kernel(places, order_ref, table_ref, first_ref, *refs):
    blocks = with_first(order_ref, places, refs[:-1], first_ref)
    spectra_into(order_ref, places, table_ref[...], blocks, refs[-1])


def early_spectra_of(order, table, first, blocks, places):
    rows, lanes = blocks[0].shape
    given = len(places)
    return pl.pallas_call(
        functools.partial(early_kernel, places),
        in_specs=[pl.BlockSpec(memory_space=pltpu.SMEM)] + whole_specs(2 + given),
        out_specs=pl.BlockSpec(memory_space=pltpu.VMEM),
        out_shape=jax.ShapeDtypeStruct((len(blocks), 2 * rows, lanes), F32),
        compiler_params=pltpu.CompilerParams(vmem_limit_bytes=12 << 20),
        cost_estimate=cost(8 * given * rows * rows * lanes, 1),
    )(order, table, first, *[blocks[place] for place in places])


def multiply_spectra(filter_ref, spectra_ref, high_ref, low_ref):
    blocks, depth, _ = spectra_ref.shape
    rows = depth // 2
    half, tile = rows // 2, 16

    def multiply(base, turn):
        def body(step, carry):
            start = pl.multiple_of(base + step * tile, tile)
            real, imag = pl.ds(start, tile), pl.ds(rows + start, tile)
            before = None
            for at in range(blocks):
                sum_real = sum_imag = None
                for other in range(at + 1):
                    a_real, a_imag = filter_ref[other, real, :], filter_ref[other, imag, :]
                    b_real, b_imag = spectra_ref[at - other, real, :], spectra_ref[at - other, imag, :]
                    part_real = a_real * b_real - a_imag * b_imag
                    part_imag = a_real * b_imag + a_imag * b_real
                    sum_real = part_real if sum_real is None else sum_real + part_real
                    sum_imag = part_imag if sum_imag is None else sum_imag + part_imag
                out_real, out_imag = sum_real, sum_imag
                if before is not None:
                    out_real = sum_real - turn * before[1]
                    out_imag = sum_imag + turn * before[0]
                before = (sum_real, sum_imag)
                for place, value in ((real, out_real), (imag, out_imag)):
                    high = value.astype(BF16)
                    high_ref[at, place, :] = high
                    low_ref[at, place, :] = (value - high.astype(F32)).astype(BF16)
            return carry

        lax.fori_loop(0, half // tile, body, 0)

    multiply(0, 1.0)
    multiply(half, -1.0)


def inverse_into(order_ref, base, inverse, high_ref, low_ref, out_refs):
    places = [order_ref[base + at] for at in range(len(out_refs))]
    high = jnp.concatenate([high_ref[place] for place in places], axis=1)
    low = jnp.concatenate([low_ref[place] for place in places], axis=1)
    result = jnp.dot(inverse, jnp.concatenate([high, high, low], axis=0), preferred_element_type=F32).astype(BF16)
    for at, out_ref in enumerate(out_refs):
        out_ref[...] = result[:, at * LANES : (at + 1) * LANES]


def conv_slices_kernel(places, order_ref, table_ref, inverse_ref, filter_ref, early_ref, first_ref, *refs):
    del early_ref
    count = filter_ref.shape[0]
    signal_refs = refs[: len(places)]
    spectra_ref, *out_refs, high_ref, low_ref = refs[-count - 3 :]
    blocks = with_first(order_ref, places, signal_refs, first_ref)
    spectra_into(order_ref, places, table_ref[...], blocks, spectra_ref)
    multiply_spectra(filter_ref, spectra_ref, high_ref, low_ref)
    for base in range(0, count, GROUP):
        inverse_into(order_ref, base, inverse_ref[...], high_ref, low_ref, out_refs[base : base + GROUP])


def conv_slices(order, table, inverse, filter_spectra, early_spectra, first, blocks, places, after):
    rows, lanes = blocks[0].shape
    count = filter_spectra.shape[0]
    _, *outs = pl.pallas_call(
        functools.partial(conv_slices_kernel, places),
        in_specs=[pl.BlockSpec(memory_space=pltpu.SMEM)] + whole_specs(5 + len(places)) + [pl.BlockSpec(memory_space=pl.ANY)] * len(after),
        out_specs=whole_specs(1 + count),
        out_shape=[jax.ShapeDtypeStruct((count, 2 * rows, lanes), F32)]
        + [jax.ShapeDtypeStruct((rows, lanes), BF16)] * count,
        input_output_aliases={4: 0},
        scratch_shapes=[pltpu.VMEM((count, 2 * rows, lanes), BF16)] * 2,
        compiler_params=pltpu.CompilerParams(vmem_limit_bytes=20 << 20),
        cost_estimate=cost(14 * count * rows * rows * lanes, 1),
    )(order, table, inverse, filter_spectra, early_spectra, first, *[blocks[place] for place in places], *after)
    return outs


def gate_chunk_kernel(first, late_ref, skip_ref, *refs):
    out_ref = refs[-1]
    for at, long_ref in enumerate(refs[:-1]):
        mixed = late_ref[first + at] * (long_ref[...].astype(F32) + skip_ref[first + at])
        out_ref[:, at * LANES : (at + 1) * LANES] = mixed.astype(BF16)


def gate_chunk(late, skip, long_blocks, first):
    rows, lanes = long_blocks[0].shape
    count = len(long_blocks)
    return pl.pallas_call(
        functools.partial(gate_chunk_kernel, first),
        in_specs=whole_specs(2 + count),
        out_specs=pl.BlockSpec(memory_space=pltpu.VMEM),
        out_shape=jax.ShapeDtypeStruct((rows, count * lanes), BF16),
        compiler_params=pltpu.CompilerParams(vmem_limit_bytes=8 << 20),
        cost_estimate=cost(3 * count * rows * lanes),
    )(late, skip, *long_blocks)


def weight_kernel(order_ref, channel_ref, weight_ref, out_ref, arrived):
    count, owners = out_ref.shape[:2]
    depth = weight_ref.shape[0] // owners
    copies = []
    for place in range(count):
        for offset in range(owners):
            start = pl.multiple_of((channel_ref[0] ^ offset) * depth + order_ref[place] * LANES, LANES)
            rows = weight_ref.at[pl.ds(start, LANES), :]
            copies.append(pltpu.make_async_copy(rows, out_ref.at[place, offset], arrived.at[place, offset]))
    for copy in copies:
        copy.start()
    for copy in copies:
        copy.wait()


def weight_rows_of(order, channel, weight):
    depth, width = weight.shape
    count, owners = order.shape[0], len(PIECE_ORDER)
    return pl.pallas_call(
        weight_kernel,
        in_specs=[pl.BlockSpec(memory_space=pltpu.SMEM)] * 2 + [pl.BlockSpec(memory_space=pl.ANY)],
        out_specs=pl.BlockSpec(memory_space=pltpu.VMEM),
        out_shape=jax.ShapeDtypeStruct((count, owners, LANES, width), BF16),
        scratch_shapes=[pltpu.SemaphoreType.DMA((count, owners))],
        compiler_params=pltpu.CompilerParams(vmem_limit_bytes=10 << 20),
        cost_estimate=pl.CostEstimate(flops=0, bytes_accessed=4 * depth * width, transcendentals=0),
    )(order, channel, weight)


def add_chunk(chunk, rows_ref, piece_refs, total):
    pieces = jnp.concatenate([ref[...] for ref in piece_refs], axis=1)
    rows = [rows_ref[place, offset] for offset in PIECE_ORDER for place in range(*CHUNKS[chunk])]
    product = jnp.dot(pieces, jnp.concatenate(rows, axis=0), preferred_element_type=F32)
    return product if total is None else total + product


def join_kernel(*refs):
    refs[-1][...] = jnp.concatenate([ref[...] for ref in refs[:-1]], axis=1)


def join(blocks):
    rows, lanes = blocks[0].shape
    count = len(blocks)
    return pl.pallas_call(
        join_kernel,
        in_specs=whole_specs(count),
        out_specs=pl.BlockSpec(memory_space=pltpu.VMEM),
        out_shape=jax.ShapeDtypeStruct((rows, count * lanes), blocks[0].dtype),
        compiler_params=pltpu.CompilerParams(vmem_limit_bytes=8 << 20),
        cost_estimate=cost(4 * rows * lanes),
    )(*blocks)


def project_kernel_slices(chunks, rows_ref, *refs):
    refs, more, out_ref = refs[: 2 * len(chunks)], refs[2 * len(chunks) : -1], refs[-1]
    total = more[0][...] if more else None
    for at, chunk in enumerate(chunks):
        total = add_chunk(chunk, rows_ref, refs[2 * at : 2 * at + 2], total)
    out_ref[...] = total.astype(out_ref.dtype)


def project_slices(weight_rows, chunks, pieces, total, out_type, scale):
    rows = pieces[0].shape[0]
    width = weight_rows.shape[3]
    more = () if total is None else (total,)
    return pl.pallas_call(
        functools.partial(project_kernel_slices, chunks),
        in_specs=whole_specs(1 + len(pieces) + len(more)),
        out_specs=pl.BlockSpec(memory_space=pltpu.VMEM),
        out_shape=jax.ShapeDtypeStruct((rows, width), out_type),
        compiler_params=pltpu.CompilerParams(vmem_limit_bytes=14 << 20),
        cost_estimate=cost(2 * rows * sum(piece.shape[1] for piece in pieces) * width, scale),
    )(weight_rows, *pieces, *more)


def swap_blocks(blocks, sequence):
    count = lax.axis_size("seq")
    arrived = list(blocks)
    for offset in sequence:
        place = OFFSETS.index(offset)
        arrived[place] = lax.ppermute(blocks[place], "seq", [(i, i ^ offset) for i in range(count)])
    return arrived


def on_device_slices(out_gate, in_gate, values, short_filter, long_filter, skip_gain, out_weight):
    rows, width = out_gate.shape
    devices = lax.axis_size("seq")
    table, inverse = transform_tables(rows)
    order = jnp.bitwise_xor(lax.axis_index("seq"), jnp.array(OFFSETS, jnp.int32))
    channel = lax.axis_index("ch").reshape(1)

    filter_blocks = swap_blocks(cut_filter(long_filter, out_gate, in_gate, values), FILTER_ORDER)
    sent = (0, *(OFFSETS.index(offset) for offset in FILTER_ORDER))
    mixed_blocks = swap_blocks(
        mix_slices(order, in_gate, values, short_filter, filter_blocks[OFFSETS.index(MIX_AFTER)]), SIGNAL_ORDER
    )
    late, skip = side_slices(order, out_gate, in_gate, values, filter_blocks, short_filter, skip_gain)
    weight_rows = weight_rows_of(order, channel, out_weight)
    filter_spectra, first = filter_spectra_of(order, table, short_filter, filter_blocks, sent, weight_rows)
    early, last = (tuple(OFFSETS.index(offset) for offset in group) for group in (EARLY, LATE))
    early_spectra = early_spectra_of(order, table, first, mixed_blocks, early)
    long_blocks = conv_slices(order, table, inverse, filter_spectra, early_spectra, first, mixed_blocks, last, (late, weight_rows))
    arrived = swap_blocks(long_blocks, RESULT_ORDER)

    pieces = []
    for start, stop in CHUNKS:
        mixed = gate_chunk(late, skip, arrived[start:stop], start)
        across = lax.ppermute(mixed, "ch", [(i, i ^ 2) for i in range(4)])
        joined = join([mixed, across])
        pieces.append((joined, lax.ppermute(joined, "ch", [(i, i ^ 1) for i in range(4)])))
    total = None
    for chunks, scale in zip(PROJECTS, PROJECT_COSTS, strict=True):
        kind = BF16 if chunks == PROJECTS[-1] else F32
        total = project_slices(weight_rows, chunks, [piece for chunk in chunks for piece in pieces[chunk]], total, kind, scale)
    return total


def on_device_spans(out_gate, in_gate, values, short_filter, long_filter, skip_gain, out_weight):
    rows, width = out_gate.shape
    devices = lax.axis_size("seq")
    slices = width // LANES
    taps = short_filter.shape[1]
    table, inverse = transform_tables(rows)

    rim = jnp.stack([a[rows - (taps - 1) :] for a in (out_gate, in_gate, values)])
    rim = lax.ppermute(rim, "seq", [(i, i + 1) for i in range(devices - 1)])
    rims = rim.astype(F32)

    filter_slices = long_filter.astype(BF16).reshape(rows, slices, LANES).transpose(1, 0, 2)
    filter_whole = send_spans(filter_slices)
    mixed_whole = send_spans(mix_inputs(in_gate, values, rims, short_filter))

    filter_spectra = forward(table, filter_whole)
    late, skip = side_terms(out_gate, in_gate, values, rims, short_filter, skip_gain)
    long_parts = block_conv(table, inverse, mixed_whole, filter_spectra, ROW_PARTS)
    channel = lax.axis_index("ch")
    order = jnp.bitwise_xor(channel, jnp.arange(lax.axis_size("ch"), dtype=jnp.int32))
    outs = []
    for part, long_part in enumerate(long_parts):
        returned = return_spans(long_part, slices)
        mixed = gate_rows(returned, late, skip, part)
        outs.append(project(gather_channels(mixed), out_weight, order))
    return jnp.concatenate(outs, axis=0)


def solution(mesh):
    devices = mesh.shape["seq"]

    def on_device(*arrays):
        width = arrays[0].shape[1]
        taps = arrays[3].shape[1]
        sliced = taps == KEEP + 1 and devices == len(OFFSETS) and width == devices * LANES and mesh.shape["ch"] == len(PIECE_ORDER)
        return (on_device_slices if sliced else on_device_spans)(*arrays)

    return jax.shard_map(
        on_device,
        mesh=mesh,
        in_specs=(
            P("seq", "ch"),
            P("seq", "ch"),
            P("seq", "ch"),
            P(None, None, "ch"),
            P("seq", "ch"),
            P("ch"),
            P(None, "ch"),
        ),
        out_specs=P("seq", "ch"),
        check_vma=False,
    )
```

```python
import functools
import math

import jax
import jax.numpy as jnp
import ml_dtypes
import numpy as np
from jax import lax
from jax.experimental import pallas as pl
from jax.experimental.pallas import tpu as pltpu
from jax.sharding import PartitionSpec as P

LANES = 128
TILE = 16
CUT_VMEM = 56
ROW_PARTS = 2
BF16 = jnp.bfloat16
F32 = jnp.float32


def two_terms(table):
    high = table.astype(ml_dtypes.bfloat16)
    low = (table - high.astype(np.float64)).astype(ml_dtypes.bfloat16)
    return high, low


def transform_tables(rows):
    order = np.concatenate([np.arange(0, rows, 2), np.arange(1, rows, 2)])
    product = (2 * order[:, None] + 1) * np.arange(rows)[None, :] % (4 * rows)
    angles = product * (math.pi / (2 * rows))
    forward = np.concatenate([np.cos(angles), -np.sin(angles)])
    fwd_high, fwd_low = two_terms(forward)
    inv_high, inv_low = two_terms(forward.T / rows)
    return (
        np.concatenate([fwd_high, fwd_low], axis=1),
        np.concatenate([inv_high, inv_low, inv_high], axis=1),
    )


def short_conv(pad_ref, block, rim, taps):
    rows = block.shape[0]
    pad_ref[pl.ds(8 - rim.shape[0], rim.shape[0]), :] = rim
    pad_ref[pl.ds(8, rows), :] = block
    total = taps[0:1] * block
    for offset in range(1, taps.shape[0]):
        total = total + taps[offset : offset + 1] * pad_ref[pl.ds(8 - offset, rows), :]
    return total


def mix_kernel(gate_ref, value_ref, rim_ref, taps_ref, out_ref, pad_a, pad_b):
    first = short_conv(pad_a, gate_ref[...].astype(F32), rim_ref[1], taps_ref[1])
    second = short_conv(pad_b, value_ref[...].astype(F32), rim_ref[2], taps_ref[2])
    out_ref[0] = (first * second).astype(out_ref.dtype)


def mix_inputs(in_gate, values, rims, taps):
    rows, width = in_gate.shape
    span = LANES
    parts = width // span
    return pl.pallas_call(
        mix_kernel,
        grid=(parts,),
        in_specs=[
            pl.BlockSpec((rows, span), lambda i: (0, i)),
            pl.BlockSpec((rows, span), lambda i: (0, i)),
            pl.BlockSpec((3, taps.shape[1] - 1, span), lambda i: (0, 0, i)),
            pl.BlockSpec((3, taps.shape[1], span), lambda i: (0, 0, i)),
        ],
        out_specs=pl.BlockSpec((1, rows, span), lambda i: (i, 0, 0)),
        out_shape=jax.ShapeDtypeStruct((parts, rows, span), BF16),
        scratch_shapes=[pltpu.VMEM((rows + 8, span), F32)] * 2,
        cost_estimate=pl.CostEstimate(flops=12 * rows * width, bytes_accessed=6 * rows * width, transcendentals=0),
    )(in_gate, values, rims, taps)


def side_kernel(late_ref, gate_ref, value_ref, rim_ref, taps_ref, skip_ref, late_out, skip_out, pad_a, pad_b, pad_c):
    late_out[...] = short_conv(pad_a, late_ref[...].astype(F32), rim_ref[0], taps_ref[0])
    first = short_conv(pad_b, gate_ref[...].astype(F32), rim_ref[1], taps_ref[1])
    second = short_conv(pad_c, value_ref[...].astype(F32), rim_ref[2], taps_ref[2])
    skip_out[...] = skip_ref[...] * (first * second)


def side_terms(out_gate, in_gate, values, rims, taps, skip_gain):
    rows, width = in_gate.shape
    span = min(width, 128)
    column = pl.BlockSpec((rows, span), lambda i: (0, i))
    return pl.pallas_call(
        side_kernel,
        grid=(width // span,),
        in_specs=[
            column,
            column,
            column,
            pl.BlockSpec((3, taps.shape[1] - 1, span), lambda i: (0, 0, i)),
            pl.BlockSpec((3, taps.shape[1], span), lambda i: (0, 0, i)),
            pl.BlockSpec((1, span), lambda i: (0, i)),
        ],
        out_specs=[column, column],
        out_shape=[jax.ShapeDtypeStruct((rows, width), F32)] * 2,
        scratch_shapes=[pltpu.VMEM((rows + 8, span), F32)] * 3,
        cost_estimate=pl.CostEstimate(flops=20 * rows * width, bytes_accessed=14 * rows * width, transcendentals=0),
    )(out_gate, in_gate, values, rims, taps, skip_gain.reshape(1, width))


def pair_of(ref, at):
    return jnp.concatenate([ref[at], ref[at + 1]], axis=1)


def forward_into(table_ref, signal_ref, out_ref):
    blocks, _, lanes = signal_ref.shape

    @pl.loop(0, blocks // 2)
    def _(step):
        pair = pair_of(signal_ref, 2 * step)
        spectra = jnp.dot(table_ref[...], jnp.concatenate([pair, pair], axis=0), preferred_element_type=F32)
        out_ref[2 * step] = spectra[:, :lanes]
        out_ref[2 * step + 1] = spectra[:, lanes:]


def forward_kernel(table_ref, signal_ref, out_ref):
    forward_into(table_ref, signal_ref, out_ref)


def forward(table, signal):
    blocks, rows, lanes = signal.shape
    return pl.pallas_call(
        forward_kernel,
        out_shape=jax.ShapeDtypeStruct((blocks, 2 * rows, lanes), F32),
        compiler_params=pltpu.CompilerParams(vmem_limit_bytes=60 << 20),
        cost_estimate=pl.CostEstimate(flops=8 * blocks * rows * rows * lanes, bytes_accessed=10 * blocks * rows * lanes, transcendentals=0),
    )(table, signal)


def conv_kernel(table_ref, inverse_ref, signal_ref, filter_ref, *rest):
    out_refs, (spectra_ref, high_ref, low_ref) = rest[:-3], rest[-3:]
    blocks, rows, lanes = signal_ref.shape
    forward_into(table_ref, signal_ref, spectra_ref)
    half = rows // 2
    tile = 16

    def multiply(base, turn):
        def body(step, carry):
            start = pl.multiple_of(base + step * tile, tile)
            real, imag = pl.ds(start, tile), pl.ds(rows + start, tile)
            before = None
            for at in range(blocks):
                sum_real = sum_imag = None
                for other in range(at + 1):
                    a_real, a_imag = filter_ref[other, real, :], filter_ref[other, imag, :]
                    b_real, b_imag = spectra_ref[at - other, real, :], spectra_ref[at - other, imag, :]
                    part_real = a_real * b_real - a_imag * b_imag
                    part_imag = a_real * b_imag + a_imag * b_real
                    sum_real = part_real if sum_real is None else sum_real + part_real
                    sum_imag = part_imag if sum_imag is None else sum_imag + part_imag
                out_real, out_imag = sum_real, sum_imag
                if before is not None:
                    out_real = sum_real - turn * before[1]
                    out_imag = sum_imag + turn * before[0]
                before = (sum_real, sum_imag)
                for place, value in ((real, out_real), (imag, out_imag)):
                    high = value.astype(BF16)
                    high_ref[at, place, :] = high
                    low_ref[at, place, :] = (value - high.astype(F32)).astype(BF16)
            return carry

        lax.fori_loop(0, half // tile, body, 0)

    multiply(0, 1.0)
    multiply(half, -1.0)

    part_rows = rows // len(out_refs)
    for part, out_ref in enumerate(out_refs):

        @pl.loop(0, blocks // 2)
        def _(step):
            high, low = pair_of(high_ref, 2 * step), pair_of(low_ref, 2 * step)
            result = jnp.dot(
                inverse_ref[pl.ds(part * part_rows, part_rows), :],
                jnp.concatenate([high, high, low], axis=0),
                preferred_element_type=F32,
            ).astype(out_ref.dtype)
            out_ref[2 * step] = result[:, :lanes]
            out_ref[2 * step + 1] = result[:, lanes:]


def block_conv(table, inverse, signal, filter_spectra, parts):
    blocks, rows, lanes = signal.shape
    return pl.pallas_call(
        conv_kernel,
        out_shape=[jax.ShapeDtypeStruct((blocks, rows // parts, lanes), BF16)] * parts,
        scratch_shapes=[
            pltpu.VMEM((blocks, 2 * rows, lanes), F32),
            pltpu.VMEM((blocks, 2 * rows, lanes), BF16),
            pltpu.VMEM((blocks, 2 * rows, lanes), BF16),
        ],
        compiler_params=pltpu.CompilerParams(vmem_limit_bytes=60 << 20),
        cost_estimate=pl.CostEstimate(flops=20 * blocks * rows * rows * lanes, bytes_accessed=10 * blocks * rows * lanes, transcendentals=0),
    )(table, inverse, signal, filter_spectra)


def gate_kernel(long_ref, late_ref, skip_ref, out_ref):
    out_ref[...] = (late_ref[...] * (long_ref[0].astype(F32) + skip_ref[...])).astype(out_ref.dtype)


def gate_rows(long_part, late, skip, part):
    blocks, rows, lanes = long_part.shape
    column = pl.BlockSpec((rows, lanes), lambda i: (part, i))
    return pl.pallas_call(
        gate_kernel,
        grid=(blocks,),
        in_specs=[pl.BlockSpec((1, rows, lanes), lambda i: (i, 0, 0)), column, column],
        out_specs=pl.BlockSpec((rows, lanes), lambda i: (0, i)),
        out_shape=jax.ShapeDtypeStruct((rows, blocks * lanes), BF16),
        cost_estimate=pl.CostEstimate(flops=3 * blocks * rows * lanes, bytes_accessed=12 * blocks * rows * lanes, transcendentals=0),
    )(long_part, late, skip)


def project_kernel(order_ref, *refs):
    del order_ref
    *mixed_refs, weight_ref, out_ref, total_ref = refs
    step = pl.program_id(0)
    for at, mixed_ref in enumerate(mixed_refs):

        @pl.when(step == at)
        def _():
            product = jnp.dot(mixed_ref[...], weight_ref[...], preferred_element_type=F32)
            total_ref[...] = product if at == 0 else total_ref[...] + product

    @pl.when(step == len(mixed_refs) - 1)
    def _():
        out_ref[...] = total_ref[...].astype(out_ref.dtype)


def project(pieces, weight, order):
    rows, depth = pieces[0].shape
    width = weight.shape[1]
    count = len(pieces)
    whole = pl.BlockSpec((rows, depth), lambda i, order: (0, 0))
    return pl.pallas_call(
        project_kernel,
        grid_spec=pltpu.PrefetchScalarGridSpec(
            num_scalar_prefetch=1,
            grid=(count,),
            in_specs=[whole] * count + [pl.BlockSpec((depth, width), lambda i, order: (order[i], 0))],
            out_specs=pl.BlockSpec((rows, width), lambda i, order: (0, 0)),
            scratch_shapes=[pltpu.VMEM((rows, width), F32)],
        ),
        out_shape=jax.ShapeDtypeStruct((rows, width), BF16),
        compiler_params=pltpu.CompilerParams(vmem_limit_bytes=40 << 20),
        cost_estimate=pl.CostEstimate(flops=2 * rows * depth * count * width, bytes_accessed=2 * depth * count * width, transcendentals=0),
    )(order, *pieces, weight)


def gather_channels(block):
    count = lax.axis_size("ch")
    held = {0: block}
    bit = count // 2
    while bit:
        route = [(i, i ^ bit) for i in range(count)]
        held.update({at ^ bit: lax.ppermute(part, "ch", route) for at, part in list(held.items())})
        bit //= 2
    return [held[at] for at in range(count)]


def exchange(blocks):
    return lax.all_to_all(blocks, "seq", split_axis=0, concat_axis=0, tiled=True)


def send_spans(slices):
    count, rows, lanes = slices.shape
    devices = lax.axis_size("seq")
    cut = devices // count
    if cut > 1:
        slices = slices.reshape(count, rows, cut, lanes // cut).transpose(0, 2, 1, 3).reshape(devices, rows, lanes // cut)
    blocks = exchange(slices)
    return jnp.pad(blocks, ((0, 0), (0, 0), (0, lanes - lanes // cut))) if cut > 1 else blocks


def return_spans(blocks, count):
    devices, rows, lanes = blocks.shape
    cut = devices // count
    if cut == 1:
        return exchange(blocks)
    arrived = exchange(blocks[:, :, : lanes // cut])
    return arrived.reshape(count, cut, rows, lanes // cut).transpose(0, 2, 1, 3).reshape(count, rows, lanes)


OFFSETS = (0, 4, 1, 2, 3, 6, 5, 7)
FILTER_ORDER = (4, 1, 6, 2, 5, 3, 7)
SIGNAL_ORDER = (4, 1, 5, 2, 6, 3, 7)
RESULT_ORDER = (4, 1, 2, 3, 6, 5, 7)
EARLY = (0, 4, 1, 5)
LATE = (2, 6, 3, 7)
GROUP = 4
NEXT_OFFSETS = (1, 3, 7)
KEEP = 2
MIX_AFTER = 1
CHUNKS = ((0, 2), (2, 4), (4, 6), (6, 8))
PROJECTS = ((0, 1, 2), (3,))
PROJECT_COSTS = (0, 0)
PIECE_ORDER = (0, 2, 1, 3)


def cost(flops, scale=0):
    return pl.CostEstimate(flops=scale * flops, bytes_accessed=scale * flops // 128, transcendentals=0)


def lanes_at(order_ref, place):
    return pl.ds(pl.multiple_of(order_ref[place] * LANES, LANES), LANES)


def whole_specs(count):
    return [pl.BlockSpec(memory_space=pltpu.VMEM)] * count


def cut_kernel(filter_ref, *refs):
    own = lax.axis_index("seq")
    last_refs, (gate_top, value_top), out_refs = refs[:3], refs[3:5], refs[5:-1]
    rows, width = filter_ref.shape
    ends_ref = refs[-1]
    ends = [ref[...].astype(F32)[-KEEP:] for ref in last_refs]
    ends += [ref[...].astype(F32)[:KEEP] for ref in (gate_top, value_top)]
    ends.append(jnp.zeros((TILE - 5 * KEEP, width), F32))
    ends_ref[...] = jnp.concatenate(ends, axis=0)
    for place, out_ref in enumerate(out_refs):
        at = pl.ds(pl.multiple_of((own ^ OFFSETS[place]) * LANES, LANES), LANES)
        out_ref[:rows] = filter_ref[:, at].astype(BF16)
        out_ref[rows : rows + TILE] = ends_ref[:, at].astype(BF16)
        if OFFSETS[place] in NEXT_OFFSETS:
            for part in range(width // (2 * LANES)):
                pair = [ends_ref[: TILE // 2, q * LANES : (q + 1) * LANES] for q in (2 * part, 2 * part + 1)]
                out_ref[rows + (1 + part) * TILE : rows + (2 + part) * TILE] = jnp.concatenate(pair, axis=0).astype(BF16)


def cut_filter(long_filter, out_gate, in_gate, values):
    rows, width = long_filter.shape
    count = width // LANES
    heights = [rows + TILE * (1 + count // 2 * (offset in NEXT_OFFSETS)) for offset in OFFSETS]
    top = pl.BlockSpec((TILE, width), lambda i: (0, 0))
    last = pl.BlockSpec((TILE, width), lambda i: (rows // TILE - 1, 0))
    return pl.pallas_call(
        cut_kernel,
        grid=(1,),
        in_specs=[pl.BlockSpec((rows, width), lambda i: (0, 0))] + [last] * 3 + [top] * 2,
        out_specs=[pl.BlockSpec((height, LANES), lambda i: (0, 0)) for height in heights],
        out_shape=[jax.ShapeDtypeStruct((height, LANES), BF16) for height in heights],
        scratch_shapes=[pltpu.VMEM((TILE, width), F32)],
        compiler_params=pltpu.CompilerParams(vmem_limit_bytes=CUT_VMEM << 20),
        cost_estimate=cost(rows * width),
    )(long_filter, out_gate, in_gate, values, in_gate, values)


def mix_slices_kernel(order_ref, gate_ref, value_ref, taps_ref, after_ref, *rest):
    del after_ref
    out_refs, (pad_a, pad_b) = rest[:-2], rest[-2:]
    keep = taps_ref.shape[1] - 1
    for place, out_ref in enumerate(out_refs):
        at = lanes_at(order_ref, place)
        none = jnp.zeros((keep, LANES), F32)
        first = short_conv(pad_a.at[place % 2], gate_ref[:, at].astype(F32), none, taps_ref[1, :, at])
        second = short_conv(pad_b.at[place % 2], value_ref[:, at].astype(F32), none, taps_ref[2, :, at])
        out_ref[...] = (first * second).astype(BF16)


def mix_slices(order, in_gate, values, taps, after):
    rows, width = in_gate.shape
    count = width // LANES
    return pl.pallas_call(
        mix_slices_kernel,
        in_specs=[pl.BlockSpec(memory_space=pltpu.SMEM)] + whole_specs(3) + [pl.BlockSpec(memory_space=pl.ANY)],
        out_specs=whole_specs(count),
        out_shape=[jax.ShapeDtypeStruct((rows, LANES), BF16)] * count,
        scratch_shapes=[pltpu.VMEM((2, rows + 8, LANES), F32)] * 2,
        compiler_params=pltpu.CompilerParams(vmem_limit_bytes=12 << 20),
        cost_estimate=cost(14 * rows * width, 1),
    )(order, in_gate, values, taps, after)


def side_slices_kernel(order_ref, late_ref, gate_ref, value_ref, *refs):
    *before_refs, taps_ref, gain_ref, late_out, skip_out = refs[:-3]
    pads = refs[-3:]
    rows, keep = late_ref.shape[0], taps_ref.shape[1] - 1
    own = order_ref[0]
    for place in range(late_out.shape[0]):
        at = lanes_at(order_ref, place)
        start = pl.multiple_of(rows + (1 + order_ref[place] // 2) * TILE, TILE)
        rim = jnp.zeros((TILE // 2, LANES), F32)
        for offset, ref in zip(NEXT_OFFSETS, before_refs, strict=True):
            given = ref[pl.ds(start, TILE), :].astype(F32)
            given = jnp.where(order_ref[place] % 2 == 1, given[TILE // 2 :], given[: TILE // 2])
            rim = jnp.where((own & offset) == (offset + 1) // 2, given, rim)
        late, first, second = (
            short_conv(
                pad.at[place % 2],
                ref[:, at].astype(F32),
                rim[which * keep : (which + 1) * keep],
                taps_ref[which, :, at],
            )
            for which, (pad, ref) in enumerate(zip(pads, (late_ref, gate_ref, value_ref), strict=True))
        )
        late_out[place] = late
        skip_out[place] = gain_ref[:, at] * (first * second)


def side_slices(order, out_gate, in_gate, values, filter_blocks, taps, skip_gain):
    rows, width = out_gate.shape
    count = width // LANES
    before = [filter_blocks[OFFSETS.index(offset)] for offset in NEXT_OFFSETS]
    return pl.pallas_call(
        side_slices_kernel,
        in_specs=[pl.BlockSpec(memory_space=pltpu.SMEM)] + whole_specs(5 + len(before)),
        out_specs=whole_specs(2),
        out_shape=[jax.ShapeDtypeStruct((count, rows, LANES), F32)] * 2,
        scratch_shapes=[pltpu.VMEM((2, rows + 8, LANES), F32)] * 3,
        compiler_params=pltpu.CompilerParams(vmem_limit_bytes=16 << 20),
        cost_estimate=cost(20 * rows * width, 1),
    )(order, out_gate, in_gate, values, *before, taps, skip_gain.reshape(1, width))


def spectra_into(order_ref, places, table, blocks, out_ref):
    columns = jnp.concatenate(blocks, axis=1)
    spectra = jnp.dot(table, jnp.concatenate([columns, columns], axis=0), preferred_element_type=F32)
    for at, place in enumerate(places):
        out_ref[order_ref[place]] = spectra[:, at * LANES : (at + 1) * LANES]


def with_first(order_ref, places, signal_refs, first_ref):
    blocks = []
    for place, ref in zip(places, signal_refs, strict=True):
        top = ref[:TILE].astype(F32)
        row = lax.broadcasted_iota(jnp.int32, top.shape, 0)
        top = jnp.where(row < KEEP, first_ref[order_ref[place]], top).astype(BF16)
        blocks.append(jnp.concatenate([top, ref[TILE:]], axis=0))
    return blocks


def filter_kernel(places, order_ref, table_ref, taps_ref, after_ref, *refs):
    del after_ref
    *block_refs, out_ref, first_ref, ends_ref = refs
    rows = table_ref.shape[0] // 2
    for base in range(0, len(block_refs), GROUP):
        blocks = [ref[:rows] for ref in block_refs[base : base + GROUP]]
        spectra_into(order_ref, places[base : base + GROUP], table_ref[...], blocks, out_ref)
    for place, ref in zip(places, block_refs, strict=True):
        ends_ref[order_ref[place]] = ref[rows : rows + TILE].astype(F32)
    count = taps_ref.shape[1]
    at = lanes_at(order_ref, 0)
    for block in range(len(block_refs)):
        mixed = None
        for which in range(2):
            top = ends_ref[block, (3 + which) * KEEP : (4 + which) * KEEP]
            end = jnp.zeros_like(top)
            if block:
                end = ends_ref[block - 1, (1 + which) * KEEP : (2 + which) * KEEP]
            joined = jnp.concatenate([end, top], axis=0)
            taps = taps_ref[1 + which, :, at]
            total = taps[0:1] * joined[KEEP:]
            for offset in range(1, count):
                total = total + taps[offset : offset + 1] * joined[KEEP - offset : 2 * KEEP - offset]
            mixed = total if mixed is None else mixed * total
        first_ref[block] = jnp.concatenate([mixed, jnp.zeros((TILE - KEEP, LANES), F32)], axis=0)


def filter_spectra_of(order, table, taps, blocks, places, after):
    rows, lanes = table.shape[0] // 2, blocks[0].shape[1]
    count = len(blocks)
    return pl.pallas_call(
        functools.partial(filter_kernel, places),
        in_specs=[pl.BlockSpec(memory_space=pltpu.SMEM)] + whole_specs(2) + [pl.BlockSpec(memory_space=pl.ANY)] + whole_specs(count),
        out_specs=whole_specs(2),
        out_shape=[
            jax.ShapeDtypeStruct((count, 2 * rows, lanes), F32),
            jax.ShapeDtypeStruct((count, TILE, lanes), F32),
        ],
        scratch_shapes=[pltpu.VMEM((count, TILE, lanes), F32)],
        compiler_params=pltpu.CompilerParams(vmem_limit_bytes=12 << 20),
        cost_estimate=cost(8 * count * rows * rows * lanes, 1),
    )(order, table, taps, after, *[blocks[place] for place in places])


def early_kernel(places, order_ref, table_ref, first_ref, *refs):
    blocks = with_first(order_ref, places, refs[:-1], first_ref)
    spectra_into(order_ref, places, table_ref[...], blocks, refs[-1])


def early_spectra_of(order, table, first, blocks, places):
    rows, lanes = blocks[0].shape
    given = len(places)
    return pl.pallas_call(
        functools.partial(early_kernel, places),
        in_specs=[pl.BlockSpec(memory_space=pltpu.SMEM)] + whole_specs(2 + given),
        out_specs=pl.BlockSpec(memory_space=pltpu.VMEM),
        out_shape=jax.ShapeDtypeStruct((len(blocks), 2 * rows, lanes), F32),
        compiler_params=pltpu.CompilerParams(vmem_limit_bytes=12 << 20),
        cost_estimate=cost(8 * given * rows * rows * lanes, 1),
    )(order, table, first, *[blocks[place] for place in places])


def multiply_spectra(filter_ref, spectra_ref, high_ref, low_ref):
    blocks, depth, _ = spectra_ref.shape
    rows = depth // 2
    half, tile = rows // 2, 16

    def multiply(base, turn):
        def body(step, carry):
            start = pl.multiple_of(base + step * tile, tile)
            real, imag = pl.ds(start, tile), pl.ds(rows + start, tile)
            before = None
            for at in range(blocks):
                sum_real = sum_imag = None
                for other in range(at + 1):
                    a_real, a_imag = filter_ref[other, real, :], filter_ref[other, imag, :]
                    b_real, b_imag = spectra_ref[at - other, real, :], spectra_ref[at - other, imag, :]
                    part_real = a_real * b_real - a_imag * b_imag
                    part_imag = a_real * b_imag + a_imag * b_real
                    sum_real = part_real if sum_real is None else sum_real + part_real
                    sum_imag = part_imag if sum_imag is None else sum_imag + part_imag
                out_real, out_imag = sum_real, sum_imag
                if before is not None:
                    out_real = sum_real - turn * before[1]
                    out_imag = sum_imag + turn * before[0]
                before = (sum_real, sum_imag)
                for place, value in ((real, out_real), (imag, out_imag)):
                    high = value.astype(BF16)
                    high_ref[at, place, :] = high
                    low_ref[at, place, :] = (value - high.astype(F32)).astype(BF16)
            return carry

        lax.fori_loop(0, half // tile, body, 0)

    multiply(0, 1.0)
    multiply(half, -1.0)


def inverse_into(order_ref, base, inverse, high_ref, low_ref, out_refs):
    places = [order_ref[base + at] for at in range(len(out_refs))]
    high = jnp.concatenate([high_ref[place] for place in places], axis=1)
    low = jnp.concatenate([low_ref[place] for place in places], axis=1)
    result = jnp.dot(inverse, jnp.concatenate([high, high, low], axis=0), preferred_element_type=F32).astype(BF16)
    for at, out_ref in enumerate(out_refs):
        out_ref[...] = result[:, at * LANES : (at + 1) * LANES]


def conv_slices_kernel(places, order_ref, table_ref, inverse_ref, filter_ref, early_ref, first_ref, *refs):
    del early_ref
    count = filter_ref.shape[0]
    signal_refs = refs[: len(places)]
    spectra_ref, *out_refs, high_ref, low_ref = refs[-count - 3 :]
    blocks = with_first(order_ref, places, signal_refs, first_ref)
    spectra_into(order_ref, places, table_ref[...], blocks, spectra_ref)
    multiply_spectra(filter_ref, spectra_ref, high_ref, low_ref)
    for base in range(0, count, GROUP):
        inverse_into(order_ref, base, inverse_ref[...], high_ref, low_ref, out_refs[base : base + GROUP])


def conv_slices(order, table, inverse, filter_spectra, early_spectra, first, blocks, places, after):
    rows, lanes = blocks[0].shape
    count = filter_spectra.shape[0]
    _, *outs = pl.pallas_call(
        functools.partial(conv_slices_kernel, places),
        in_specs=[pl.BlockSpec(memory_space=pltpu.SMEM)] + whole_specs(5 + len(places)) + [pl.BlockSpec(memory_space=pl.ANY)] * len(after),
        out_specs=whole_specs(1 + count),
        out_shape=[jax.ShapeDtypeStruct((count, 2 * rows, lanes), F32)]
        + [jax.ShapeDtypeStruct((rows, lanes), BF16)] * count,
        input_output_aliases={4: 0},
        scratch_shapes=[pltpu.VMEM((count, 2 * rows, lanes), BF16)] * 2,
        compiler_params=pltpu.CompilerParams(vmem_limit_bytes=20 << 20),
        cost_estimate=cost(14 * count * rows * rows * lanes, 1),
    )(order, table, inverse, filter_spectra, early_spectra, first, *[blocks[place] for place in places], *after)
    return outs


def gate_chunk_kernel(first, late_ref, skip_ref, *refs):
    out_ref = refs[-1]
    for at, long_ref in enumerate(refs[:-1]):
        mixed = late_ref[first + at] * (long_ref[...].astype(F32) + skip_ref[first + at])
        out_ref[:, at * LANES : (at + 1) * LANES] = mixed.astype(BF16)


def gate_chunk(late, skip, long_blocks, first):
    rows, lanes = long_blocks[0].shape
    count = len(long_blocks)
    return pl.pallas_call(
        functools.partial(gate_chunk_kernel, first),
        in_specs=whole_specs(2 + count),
        out_specs=pl.BlockSpec(memory_space=pltpu.VMEM),
        out_shape=jax.ShapeDtypeStruct((rows, count * lanes), BF16),
        compiler_params=pltpu.CompilerParams(vmem_limit_bytes=8 << 20),
        cost_estimate=cost(3 * count * rows * lanes),
    )(late, skip, *long_blocks)


def weight_kernel(order_ref, channel_ref, weight_ref, out_ref, arrived):
    count, owners = out_ref.shape[:2]
    depth = weight_ref.shape[0] // owners
    copies = []
    for place in range(count):
        for offset in range(owners):
            start = pl.multiple_of((channel_ref[0] ^ offset) * depth + order_ref[place] * LANES, LANES)
            rows = weight_ref.at[pl.ds(start, LANES), :]
            copies.append(pltpu.make_async_copy(rows, out_ref.at[place, offset], arrived.at[place, offset]))
    for copy in copies:
        copy.start()
    for copy in copies:
        copy.wait()


def weight_rows_of(order, channel, weight):
    depth, width = weight.shape
    count, owners = order.shape[0], len(PIECE_ORDER)
    return pl.pallas_call(
        weight_kernel,
        in_specs=[pl.BlockSpec(memory_space=pltpu.SMEM)] * 2 + [pl.BlockSpec(memory_space=pl.ANY)],
        out_specs=pl.BlockSpec(memory_space=pltpu.VMEM),
        out_shape=jax.ShapeDtypeStruct((count, owners, LANES, width), BF16),
        scratch_shapes=[pltpu.SemaphoreType.DMA((count, owners))],
        compiler_params=pltpu.CompilerParams(vmem_limit_bytes=10 << 20),
        cost_estimate=pl.CostEstimate(flops=0, bytes_accessed=4 * depth * width, transcendentals=0),
    )(order, channel, weight)


def add_chunk(chunk, rows_ref, piece_refs, total):
    pieces = jnp.concatenate([ref[...] for ref in piece_refs], axis=1)
    rows = [rows_ref[place, offset] for offset in PIECE_ORDER for place in range(*CHUNKS[chunk])]
    product = jnp.dot(pieces, jnp.concatenate(rows, axis=0), preferred_element_type=F32)
    return product if total is None else total + product


def join_kernel(*refs):
    refs[-1][...] = jnp.concatenate([ref[...] for ref in refs[:-1]], axis=1)


def join(blocks):
    rows, lanes = blocks[0].shape
    count = len(blocks)
    return pl.pallas_call(
        join_kernel,
        in_specs=whole_specs(count),
        out_specs=pl.BlockSpec(memory_space=pltpu.VMEM),
        out_shape=jax.ShapeDtypeStruct((rows, count * lanes), blocks[0].dtype),
        compiler_params=pltpu.CompilerParams(vmem_limit_bytes=8 << 20),
        cost_estimate=cost(4 * rows * lanes),
    )(*blocks)


def project_kernel_slices(chunks, rows_ref, *refs):
    refs, more, out_ref = refs[: 2 * len(chunks)], refs[2 * len(chunks) : -1], refs[-1]
    total = more[0][...] if more else None
    for at, chunk in enumerate(chunks):
        total = add_chunk(chunk, rows_ref, refs[2 * at : 2 * at + 2], total)
    out_ref[...] = total.astype(out_ref.dtype)


def project_slices(weight_rows, chunks, pieces, total, out_type, scale):
    rows = pieces[0].shape[0]
    width = weight_rows.shape[3]
    more = () if total is None else (total,)
    return pl.pallas_call(
        functools.partial(project_kernel_slices, chunks),
        in_specs=whole_specs(1 + len(pieces) + len(more)),
        out_specs=pl.BlockSpec(memory_space=pltpu.VMEM),
        out_shape=jax.ShapeDtypeStruct((rows, width), out_type),
        compiler_params=pltpu.CompilerParams(vmem_limit_bytes=14 << 20),
        cost_estimate=cost(2 * rows * sum(piece.shape[1] for piece in pieces) * width, scale),
    )(weight_rows, *pieces, *more)


def swap_blocks(blocks, sequence):
    count = lax.axis_size("seq")
    arrived = list(blocks)
    for offset in sequence:
        place = OFFSETS.index(offset)
        arrived[place] = lax.ppermute(blocks[place], "seq", [(i, i ^ offset) for i in range(count)])
    return arrived


def on_device_slices(out_gate, in_gate, values, short_filter, long_filter, skip_gain, out_weight):
    rows, width = out_gate.shape
    devices = lax.axis_size("seq")
    table, inverse = transform_tables(rows)
    order = jnp.bitwise_xor(lax.axis_index("seq"), jnp.array(OFFSETS, jnp.int32))
    channel = lax.axis_index("ch").reshape(1)

    filter_blocks = swap_blocks(cut_filter(long_filter, out_gate, in_gate, values), FILTER_ORDER)
    sent = (0, *(OFFSETS.index(offset) for offset in FILTER_ORDER))
    mixed_blocks = swap_blocks(
        mix_slices(order, in_gate, values, short_filter, filter_blocks[OFFSETS.index(MIX_AFTER)]), SIGNAL_ORDER
    )
    late, skip = side_slices(order, out_gate, in_gate, values, filter_blocks, short_filter, skip_gain)
    weight_rows = weight_rows_of(order, channel, out_weight)
    filter_spectra, first = filter_spectra_of(order, table, short_filter, filter_blocks, sent, weight_rows)
    early, last = (tuple(OFFSETS.index(offset) for offset in group) for group in (EARLY, LATE))
    early_spectra = early_spectra_of(order, table, first, mixed_blocks, early)
    long_blocks = conv_slices(order, table, inverse, filter_spectra, early_spectra, first, mixed_blocks, last, (late, weight_rows))
    arrived = swap_blocks(long_blocks, RESULT_ORDER)

    pieces = []
    for start, stop in CHUNKS:
        mixed = gate_chunk(late, skip, arrived[start:stop], start)
        across = lax.ppermute(mixed, "ch", [(i, i ^ 2) for i in range(4)])
        joined = join([mixed, across])
        pieces.append((joined, lax.ppermute(joined, "ch", [(i, i ^ 1) for i in range(4)])))
    total = None
    for chunks, scale in zip(PROJECTS, PROJECT_COSTS, strict=True):
        kind = BF16 if chunks == PROJECTS[-1] else F32
        total = project_slices(weight_rows, chunks, [piece for chunk in chunks for piece in pieces[chunk]], total, kind, scale)
    return total


def on_device_spans(out_gate, in_gate, values, short_filter, long_filter, skip_gain, out_weight):
    rows, width = out_gate.shape
    devices = lax.axis_size("seq")
    slices = width // LANES
    taps = short_filter.shape[1]
    table, inverse = transform_tables(rows)

    rim = jnp.stack([a[rows - (taps - 1) :] for a in (out_gate, in_gate, values)])
    rim = lax.ppermute(rim, "seq", [(i, i + 1) for i in range(devices - 1)])
    rims = rim.astype(F32)

    filter_slices = long_filter.astype(BF16).reshape(rows, slices, LANES).transpose(1, 0, 2)
    filter_whole = send_spans(filter_slices)
    mixed_whole = send_spans(mix_inputs(in_gate, values, rims, short_filter))

    filter_spectra = forward(table, filter_whole)
    late, skip = side_terms(out_gate, in_gate, values, rims, short_filter, skip_gain)
    long_parts = block_conv(table, inverse, mixed_whole, filter_spectra, ROW_PARTS)
    channel = lax.axis_index("ch")
    order = jnp.bitwise_xor(channel, jnp.arange(lax.axis_size("ch"), dtype=jnp.int32))
    outs = []
    for part, long_part in enumerate(long_parts):
        returned = return_spans(long_part, slices)
        mixed = gate_rows(returned, late, skip, part)
        outs.append(project(gather_channels(mixed), out_weight, order))
    return jnp.concatenate(outs, axis=0)


def solution(mesh):
    devices = mesh.shape["seq"]

    def on_device(*arrays):
        width = arrays[0].shape[1]
        taps = arrays[3].shape[1]
        sliced = taps == KEEP + 1 and devices == len(OFFSETS) and width == devices * LANES and mesh.shape["ch"] == len(PIECE_ORDER)
        return (on_device_slices if sliced else on_device_spans)(*arrays)

    return jax.shard_map(
        on_device,
        mesh=mesh,
        in_specs=(
            P("seq", "ch"),
            P("seq", "ch"),
            P("seq", "ch"),
            P(None, None, "ch"),
            P("seq", "ch"),
            P("ch"),
            P(None, "ch"),
        ),
        out_specs=P("seq", "ch"),
        check_vma=False,
    )
```

```python
import functools
import math

import jax
import jax.numpy as jnp
import ml_dtypes
import numpy as np
from jax import lax
from jax.experimental import pallas as pl
from jax.experimental.pallas import tpu as pltpu
from jax.sharding import PartitionSpec as P

LANES = 128
TILE = 16
CUT_VMEM = 56
ROW_PARTS = 2
BF16 = jnp.bfloat16
F32 = jnp.float32


def two_terms(table):
    high = table.astype(ml_dtypes.bfloat16)
    low = (table - high.astype(np.float64)).astype(ml_dtypes.bfloat16)
    return high, low


def transform_tables(rows):
    order = np.concatenate([np.arange(0, rows, 2), np.arange(1, rows, 2)])
    product = (2 * order[:, None] + 1) * np.arange(rows)[None, :] % (4 * rows)
    angles = product * (math.pi / (2 * rows))
    forward = np.concatenate([np.cos(angles), -np.sin(angles)])
    fwd_high, fwd_low = two_terms(forward)
    inv_high, inv_low = two_terms(forward.T / rows)
    return (
        np.concatenate([fwd_high, fwd_low], axis=1),
        np.concatenate([inv_high, inv_low, inv_high], axis=1),
    )


def short_conv(pad_ref, block, rim, taps):
    rows = block.shape[0]
    pad_ref[pl.ds(8 - rim.shape[0], rim.shape[0]), :] = rim
    pad_ref[pl.ds(8, rows), :] = block
    total = taps[0:1] * block
    for offset in range(1, taps.shape[0]):
        total = total + taps[offset : offset + 1] * pad_ref[pl.ds(8 - offset, rows), :]
    return total


def mix_kernel(gate_ref, value_ref, rim_ref, taps_ref, out_ref, pad_a, pad_b):
    first = short_conv(pad_a, gate_ref[...].astype(F32), rim_ref[1], taps_ref[1])
    second = short_conv(pad_b, value_ref[...].astype(F32), rim_ref[2], taps_ref[2])
    out_ref[0] = (first * second).astype(out_ref.dtype)


def mix_inputs(in_gate, values, rims, taps):
    rows, width = in_gate.shape
    span = LANES
    parts = width // span
    return pl.pallas_call(
        mix_kernel,
        grid=(parts,),
        in_specs=[
            pl.BlockSpec((rows, span), lambda i: (0, i)),
            pl.BlockSpec((rows, span), lambda i: (0, i)),
            pl.BlockSpec((3, taps.shape[1] - 1, span), lambda i: (0, 0, i)),
            pl.BlockSpec((3, taps.shape[1], span), lambda i: (0, 0, i)),
        ],
        out_specs=pl.BlockSpec((1, rows, span), lambda i: (i, 0, 0)),
        out_shape=jax.ShapeDtypeStruct((parts, rows, span), BF16),
        scratch_shapes=[pltpu.VMEM((rows + 8, span), F32)] * 2,
        cost_estimate=pl.CostEstimate(flops=12 * rows * width, bytes_accessed=6 * rows * width, transcendentals=0),
    )(in_gate, values, rims, taps)


def side_kernel(late_ref, gate_ref, value_ref, rim_ref, taps_ref, skip_ref, late_out, skip_out, pad_a, pad_b, pad_c):
    late_out[...] = short_conv(pad_a, late_ref[...].astype(F32), rim_ref[0], taps_ref[0])
    first = short_conv(pad_b, gate_ref[...].astype(F32), rim_ref[1], taps_ref[1])
    second = short_conv(pad_c, value_ref[...].astype(F32), rim_ref[2], taps_ref[2])
    skip_out[...] = skip_ref[...] * (first * second)


def side_terms(out_gate, in_gate, values, rims, taps, skip_gain):
    rows, width = in_gate.shape
    span = min(width, 128)
    column = pl.BlockSpec((rows, span), lambda i: (0, i))
    return pl.pallas_call(
        side_kernel,
        grid=(width // span,),
        in_specs=[
            column,
            column,
            column,
            pl.BlockSpec((3, taps.shape[1] - 1, span), lambda i: (0, 0, i)),
            pl.BlockSpec((3, taps.shape[1], span), lambda i: (0, 0, i)),
            pl.BlockSpec((1, span), lambda i: (0, i)),
        ],
        out_specs=[column, column],
        out_shape=[jax.ShapeDtypeStruct((rows, width), F32)] * 2,
        scratch_shapes=[pltpu.VMEM((rows + 8, span), F32)] * 3,
        cost_estimate=pl.CostEstimate(flops=20 * rows * width, bytes_accessed=14 * rows * width, transcendentals=0),
    )(out_gate, in_gate, values, rims, taps, skip_gain.reshape(1, width))


def pair_of(ref, at):
    return jnp.concatenate([ref[at], ref[at + 1]], axis=1)


def forward_into(table_ref, signal_ref, out_ref):
    blocks, _, lanes = signal_ref.shape

    @pl.loop(0, blocks // 2)
    def _(step):
        pair = pair_of(signal_ref, 2 * step)
        spectra = jnp.dot(table_ref[...], jnp.concatenate([pair, pair], axis=0), preferred_element_type=F32)
        out_ref[2 * step] = spectra[:, :lanes]
        out_ref[2 * step + 1] = spectra[:, lanes:]


def forward_kernel(table_ref, signal_ref, out_ref):
    forward_into(table_ref, signal_ref, out_ref)


def forward(table, signal):
    blocks, rows, lanes = signal.shape
    return pl.pallas_call(
        forward_kernel,
        out_shape=jax.ShapeDtypeStruct((blocks, 2 * rows, lanes), F32),
        compiler_params=pltpu.CompilerParams(vmem_limit_bytes=60 << 20),
        cost_estimate=pl.CostEstimate(flops=8 * blocks * rows * rows * lanes, bytes_accessed=10 * blocks * rows * lanes, transcendentals=0),
    )(table, signal)


def conv_kernel(table_ref, inverse_ref, signal_ref, filter_ref, *rest):
    out_refs, (spectra_ref, high_ref, low_ref) = rest[:-3], rest[-3:]
    blocks, rows, lanes = signal_ref.shape
    forward_into(table_ref, signal_ref, spectra_ref)
    half = rows // 2
    tile = 16

    def multiply(base, turn):
        def body(step, carry):
            start = pl.multiple_of(base + step * tile, tile)
            real, imag = pl.ds(start, tile), pl.ds(rows + start, tile)
            before = None
            for at in range(blocks):
                sum_real = sum_imag = None
                for other in range(at + 1):
                    a_real, a_imag = filter_ref[other, real, :], filter_ref[other, imag, :]
                    b_real, b_imag = spectra_ref[at - other, real, :], spectra_ref[at - other, imag, :]
                    part_real = a_real * b_real - a_imag * b_imag
                    part_imag = a_real * b_imag + a_imag * b_real
                    sum_real = part_real if sum_real is None else sum_real + part_real
                    sum_imag = part_imag if sum_imag is None else sum_imag + part_imag
                out_real, out_imag = sum_real, sum_imag
                if before is not None:
                    out_real = sum_real - turn * before[1]
                    out_imag = sum_imag + turn * before[0]
                before = (sum_real, sum_imag)
                for place, value in ((real, out_real), (imag, out_imag)):
                    high = value.astype(BF16)
                    high_ref[at, place, :] = high
                    low_ref[at, place, :] = (value - high.astype(F32)).astype(BF16)
            return carry

        lax.fori_loop(0, half // tile, body, 0)

    multiply(0, 1.0)
    multiply(half, -1.0)

    part_rows = rows // len(out_refs)
    for part, out_ref in enumerate(out_refs):

        @pl.loop(0, blocks // 2)
        def _(step):
            high, low = pair_of(high_ref, 2 * step), pair_of(low_ref, 2 * step)
            result = jnp.dot(
                inverse_ref[pl.ds(part * part_rows, part_rows), :],
                jnp.concatenate([high, high, low], axis=0),
                preferred_element_type=F32,
            ).astype(out_ref.dtype)
            out_ref[2 * step] = result[:, :lanes]
            out_ref[2 * step + 1] = result[:, lanes:]


def block_conv(table, inverse, signal, filter_spectra, parts):
    blocks, rows, lanes = signal.shape
    return pl.pallas_call(
        conv_kernel,
        out_shape=[jax.ShapeDtypeStruct((blocks, rows // parts, lanes), BF16)] * parts,
        scratch_shapes=[
            pltpu.VMEM((blocks, 2 * rows, lanes), F32),
            pltpu.VMEM((blocks, 2 * rows, lanes), BF16),
            pltpu.VMEM((blocks, 2 * rows, lanes), BF16),
        ],
        compiler_params=pltpu.CompilerParams(vmem_limit_bytes=60 << 20),
        cost_estimate=pl.CostEstimate(flops=20 * blocks * rows * rows * lanes, bytes_accessed=10 * blocks * rows * lanes, transcendentals=0),
    )(table, inverse, signal, filter_spectra)


def gate_kernel(long_ref, late_ref, skip_ref, out_ref):
    out_ref[...] = (late_ref[...] * (long_ref[0].astype(F32) + skip_ref[...])).astype(out_ref.dtype)


def gate_rows(long_part, late, skip, part):
    blocks, rows, lanes = long_part.shape
    column = pl.BlockSpec((rows, lanes), lambda i: (part, i))
    return pl.pallas_call(
        gate_kernel,
        grid=(blocks,),
        in_specs=[pl.BlockSpec((1, rows, lanes), lambda i: (i, 0, 0)), column, column],
        out_specs=pl.BlockSpec((rows, lanes), lambda i: (0, i)),
        out_shape=jax.ShapeDtypeStruct((rows, blocks * lanes), BF16),
        cost_estimate=pl.CostEstimate(flops=3 * blocks * rows * lanes, bytes_accessed=12 * blocks * rows * lanes, transcendentals=0),
    )(long_part, late, skip)


def project_kernel(order_ref, *refs):
    del order_ref
    *mixed_refs, weight_ref, out_ref, total_ref = refs
    step = pl.program_id(0)
    for at, mixed_ref in enumerate(mixed_refs):

        @pl.when(step == at)
        def _():
            product = jnp.dot(mixed_ref[...], weight_ref[...], preferred_element_type=F32)
            total_ref[...] = product if at == 0 else total_ref[...] + product

    @pl.when(step == len(mixed_refs) - 1)
    def _():
        out_ref[...] = total_ref[...].astype(out_ref.dtype)


def project(pieces, weight, order):
    rows, depth = pieces[0].shape
    width = weight.shape[1]
    count = len(pieces)
    whole = pl.BlockSpec((rows, depth), lambda i, order: (0, 0))
    return pl.pallas_call(
        project_kernel,
        grid_spec=pltpu.PrefetchScalarGridSpec(
            num_scalar_prefetch=1,
            grid=(count,),
            in_specs=[whole] * count + [pl.BlockSpec((depth, width), lambda i, order: (order[i], 0))],
            out_specs=pl.BlockSpec((rows, width), lambda i, order: (0, 0)),
            scratch_shapes=[pltpu.VMEM((rows, width), F32)],
        ),
        out_shape=jax.ShapeDtypeStruct((rows, width), BF16),
        compiler_params=pltpu.CompilerParams(vmem_limit_bytes=40 << 20),
        cost_estimate=pl.CostEstimate(flops=2 * rows * depth * count * width, bytes_accessed=2 * depth * count * width, transcendentals=0),
    )(order, *pieces, weight)


def gather_channels(block):
    count = lax.axis_size("ch")
    held = {0: block}
    bit = count // 2
    while bit:
        route = [(i, i ^ bit) for i in range(count)]
        held.update({at ^ bit: lax.ppermute(part, "ch", route) for at, part in list(held.items())})
        bit //= 2
    return [held[at] for at in range(count)]


def exchange(blocks):
    return lax.all_to_all(blocks, "seq", split_axis=0, concat_axis=0, tiled=True)


def send_spans(slices):
    count, rows, lanes = slices.shape
    devices = lax.axis_size("seq")
    cut = devices // count
    if cut > 1:
        slices = slices.reshape(count, rows, cut, lanes // cut).transpose(0, 2, 1, 3).reshape(devices, rows, lanes // cut)
    blocks = exchange(slices)
    return jnp.pad(blocks, ((0, 0), (0, 0), (0, lanes - lanes // cut))) if cut > 1 else blocks


def return_spans(blocks, count):
    devices, rows, lanes = blocks.shape
    cut = devices // count
    if cut == 1:
        return exchange(blocks)
    arrived = exchange(blocks[:, :, : lanes // cut])
    return arrived.reshape(count, cut, rows, lanes // cut).transpose(0, 2, 1, 3).reshape(count, rows, lanes)


OFFSETS = (0, 4, 1, 2, 3, 6, 5, 7)
FILTER_ORDER = (4, 1, 6, 2, 5, 3, 7)
SIGNAL_ORDER = (4, 1, 5, 2, 6, 3, 7)
RESULT_ORDER = (4, 1, 2, 3, 6, 5, 7)
EARLY = (0, 4, 1, 5)
LATE = (2, 6, 3, 7)
GROUP = 4
NEXT_OFFSETS = (1, 3, 7)
KEEP = 2
MIX_AFTER = 1
CHUNKS = ((0, 2), (2, 4), (4, 6), (6, 8))
PROJECTS = ((0, 1, 2), (3,))
PROJECT_COSTS = (0, 0)
PIECE_ORDER = (0, 2, 1, 3)


def cost(flops, scale=0):
    return pl.CostEstimate(flops=scale * flops, bytes_accessed=scale * flops // 128, transcendentals=0)


def lanes_at(order_ref, place):
    return pl.ds(pl.multiple_of(order_ref[place] * LANES, LANES), LANES)


def whole_specs(count):
    return [pl.BlockSpec(memory_space=pltpu.VMEM)] * count


def cut_kernel(filter_ref, *refs):
    own = lax.axis_index("seq")
    last_refs, (gate_top, value_top), out_refs = refs[:3], refs[3:5], refs[5:-1]
    rows, width = filter_ref.shape
    ends_ref = refs[-1]
    ends = [ref[...].astype(F32)[-KEEP:] for ref in last_refs]
    ends += [ref[...].astype(F32)[:KEEP] for ref in (gate_top, value_top)]
    ends.append(jnp.zeros((TILE - 5 * KEEP, width), F32))
    ends_ref[...] = jnp.concatenate(ends, axis=0)
    for place, out_ref in enumerate(out_refs):
        at = pl.ds(pl.multiple_of((own ^ OFFSETS[place]) * LANES, LANES), LANES)
        out_ref[:rows] = filter_ref[:, at].astype(BF16)
        out_ref[rows : rows + TILE] = ends_ref[:, at].astype(BF16)
        if OFFSETS[place] in NEXT_OFFSETS:
            for part in range(width // (2 * LANES)):
                pair = [ends_ref[: TILE // 2, q * LANES : (q + 1) * LANES] for q in (2 * part, 2 * part + 1)]
                out_ref[rows + (1 + part) * TILE : rows + (2 + part) * TILE] = jnp.concatenate(pair, axis=0).astype(BF16)


def cut_filter(long_filter, out_gate, in_gate, values):
    rows, width = long_filter.shape
    count = width // LANES
    heights = [rows + TILE * (1 + count // 2 * (offset in NEXT_OFFSETS)) for offset in OFFSETS]
    top = pl.BlockSpec((TILE, width), lambda i: (0, 0))
    last = pl.BlockSpec((TILE, width), lambda i: (rows // TILE - 1, 0))
    return pl.pallas_call(
        cut_kernel,
        grid=(1,),
        in_specs=[pl.BlockSpec((rows, width), lambda i: (0, 0))] + [last] * 3 + [top] * 2,
        out_specs=[pl.BlockSpec((height, LANES), lambda i: (0, 0)) for height in heights],
        out_shape=[jax.ShapeDtypeStruct((height, LANES), BF16) for height in heights],
        scratch_shapes=[pltpu.VMEM((TILE, width), F32)],
        compiler_params=pltpu.CompilerParams(vmem_limit_bytes=CUT_VMEM << 20),
        cost_estimate=cost(rows * width),
    )(long_filter, out_gate, in_gate, values, in_gate, values)


def mix_slices_kernel(order_ref, gate_ref, value_ref, taps_ref, after_ref, *rest):
    del after_ref
    out_refs, (pad_a, pad_b) = rest[:-2], rest[-2:]
    keep = taps_ref.shape[1] - 1
    for place, out_ref in enumerate(out_refs):
        at = lanes_at(order_ref, place)
        none = jnp.zeros((keep, LANES), F32)
        first = short_conv(pad_a.at[place % 2], gate_ref[:, at].astype(F32), none, taps_ref[1, :, at])
        second = short_conv(pad_b.at[place % 2], value_ref[:, at].astype(F32), none, taps_ref[2, :, at])
        out_ref[...] = (first * second).astype(BF16)


def mix_slices(order, in_gate, values, taps, after):
    rows, width = in_gate.shape
    count = width // LANES
    return pl.pallas_call(
        mix_slices_kernel,
        in_specs=[pl.BlockSpec(memory_space=pltpu.SMEM)] + whole_specs(3) + [pl.BlockSpec(memory_space=pl.ANY)],
        out_specs=whole_specs(count),
        out_shape=[jax.ShapeDtypeStruct((rows, LANES), BF16)] * count,
        scratch_shapes=[pltpu.VMEM((2, rows + 8, LANES), F32)] * 2,
        compiler_params=pltpu.CompilerParams(vmem_limit_bytes=12 << 20),
        cost_estimate=cost(14 * rows * width, 1),
    )(order, in_gate, values, taps, after)


def side_slices_kernel(order_ref, late_ref, gate_ref, value_ref, *refs):
    *before_refs, taps_ref, gain_ref, late_out, skip_out = refs[:-3]
    pads = refs[-3:]
    rows, keep = late_ref.shape[0], taps_ref.shape[1] - 1
    own = order_ref[0]
    for place in range(late_out.shape[0]):
        at = lanes_at(order_ref, place)
        start = pl.multiple_of(rows + (1 + order_ref[place] // 2) * TILE, TILE)
        rim = jnp.zeros((TILE // 2, LANES), F32)
        for offset, ref in zip(NEXT_OFFSETS, before_refs, strict=True):
            given = ref[pl.ds(start, TILE), :].astype(F32)
            given = jnp.where(order_ref[place] % 2 == 1, given[TILE // 2 :], given[: TILE // 2])
            rim = jnp.where((own & offset) == (offset + 1) // 2, given, rim)
        late, first, second = (
            short_conv(
                pad.at[place % 2],
                ref[:, at].astype(F32),
                rim[which * keep : (which + 1) * keep],
                taps_ref[which, :, at],
            )
            for which, (pad, ref) in enumerate(zip(pads, (late_ref, gate_ref, value_ref), strict=True))
        )
        late_out[place] = late
        skip_out[place] = gain_ref[:, at] * (first * second)


def side_slices(order, out_gate, in_gate, values, filter_blocks, taps, skip_gain):
    rows, width = out_gate.shape
    count = width // LANES
    before = [filter_blocks[OFFSETS.index(offset)] for offset in NEXT_OFFSETS]
    return pl.pallas_call(
        side_slices_kernel,
        in_specs=[pl.BlockSpec(memory_space=pltpu.SMEM)] + whole_specs(5 + len(before)),
        out_specs=whole_specs(2),
        out_shape=[jax.ShapeDtypeStruct((count, rows, LANES), F32)] * 2,
        scratch_shapes=[pltpu.VMEM((2, rows + 8, LANES), F32)] * 3,
        compiler_params=pltpu.CompilerParams(vmem_limit_bytes=16 << 20),
        cost_estimate=cost(20 * rows * width, 1),
    )(order, out_gate, in_gate, values, *before, taps, skip_gain.reshape(1, width))


def spectra_into(order_ref, places, table, blocks, out_ref):
    columns = jnp.concatenate(blocks, axis=1)
    spectra = jnp.dot(table, jnp.concatenate([columns, columns], axis=0), preferred_element_type=F32)
    for at, place in enumerate(places):
        out_ref[order_ref[place]] = spectra[:, at * LANES : (at + 1) * LANES]


def with_first(order_ref, places, signal_refs, first_ref):
    blocks = []
    for place, ref in zip(places, signal_refs, strict=True):
        top = ref[:TILE].astype(F32)
        row = lax.broadcasted_iota(jnp.int32, top.shape, 0)
        top = jnp.where(row < KEEP, first_ref[order_ref[place]], top).astype(BF16)
        blocks.append(jnp.concatenate([top, ref[TILE:]], axis=0))
    return blocks


def filter_kernel(places, order_ref, table_ref, taps_ref, after_ref, *refs):
    del after_ref
    *block_refs, out_ref, first_ref, ends_ref = refs
    rows = table_ref.shape[0] // 2
    for base in range(0, len(block_refs), GROUP):
        blocks = [ref[:rows] for ref in block_refs[base : base + GROUP]]
        spectra_into(order_ref, places[base : base + GROUP], table_ref[...], blocks, out_ref)
    for place, ref in zip(places, block_refs, strict=True):
        ends_ref[order_ref[place]] = ref[rows : rows + TILE].astype(F32)
    count = taps_ref.shape[1]
    at = lanes_at(order_ref, 0)
    for block in range(len(block_refs)):
        mixed = None
        for which in range(2):
            top = ends_ref[block, (3 + which) * KEEP : (4 + which) * KEEP]
            end = jnp.zeros_like(top)
            if block:
                end = ends_ref[block - 1, (1 + which) * KEEP : (2 + which) * KEEP]
            joined = jnp.concatenate([end, top], axis=0)
            taps = taps_ref[1 + which, :, at]
            total = taps[0:1] * joined[KEEP:]
            for offset in range(1, count):
                total = total + taps[offset : offset + 1] * joined[KEEP - offset : 2 * KEEP - offset]
            mixed = total if mixed is None else mixed * total
        first_ref[block] = jnp.concatenate([mixed, jnp.zeros((TILE - KEEP, LANES), F32)], axis=0)


def filter_spectra_of(order, table, taps, blocks, places, after):
    rows, lanes = table.shape[0] // 2, blocks[0].shape[1]
    count = len(blocks)
    return pl.pallas_call(
        functools.partial(filter_kernel, places),
        in_specs=[pl.BlockSpec(memory_space=pltpu.SMEM)] + whole_specs(2) + [pl.BlockSpec(memory_space=pl.ANY)] + whole_specs(count),
        out_specs=whole_specs(2),
        out_shape=[
            jax.ShapeDtypeStruct((count, 2 * rows, lanes), F32),
            jax.ShapeDtypeStruct((count, TILE, lanes), F32),
        ],
        scratch_shapes=[pltpu.VMEM((count, TILE, lanes), F32)],
        compiler_params=pltpu.CompilerParams(vmem_limit_bytes=12 << 20),
        cost_estimate=cost(8 * count * rows * rows * lanes, 1),
    )(order, table, taps, after, *[blocks[place] for place in places])


def early_kernel(places, order_ref, table_ref, first_ref, *refs):
    blocks = with_first(order_ref, places, refs[:-1], first_ref)
    spectra_into(order_ref, places, table_ref[...], blocks, refs[-1])


def early_spectra_of(order, table, first, blocks, places):
    rows, lanes = blocks[0].shape
    given = len(places)
    return pl.pallas_call(
        functools.partial(early_kernel, places),
        in_specs=[pl.BlockSpec(memory_space=pltpu.SMEM)] + whole_specs(2 + given),
        out_specs=pl.BlockSpec(memory_space=pltpu.VMEM),
        out_shape=jax.ShapeDtypeStruct((len(blocks), 2 * rows, lanes), F32),
        compiler_params=pltpu.CompilerParams(vmem_limit_bytes=12 << 20),
        cost_estimate=cost(8 * given * rows * rows * lanes, 1),
    )(order, table, first, *[blocks[place] for place in places])


def multiply_spectra(filter_ref, spectra_ref, high_ref, low_ref):
    blocks, depth, _ = spectra_ref.shape
    rows = depth // 2
    half, tile = rows // 2, 16

    def multiply(base, turn):
        def body(step, carry):
            start = pl.multiple_of(base + step * tile, tile)
            real, imag = pl.ds(start, tile), pl.ds(rows + start, tile)
            before = None
            for at in range(blocks):
                sum_real = sum_imag = None
                for other in range(at + 1):
                    a_real, a_imag = filter_ref[other, real, :], filter_ref[other, imag, :]
                    b_real, b_imag = spectra_ref[at - other, real, :], spectra_ref[at - other, imag, :]
                    part_real = a_real * b_real - a_imag * b_imag
                    part_imag = a_real * b_imag + a_imag * b_real
                    sum_real = part_real if sum_real is None else sum_real + part_real
                    sum_imag = part_imag if sum_imag is None else sum_imag + part_imag
                out_real, out_imag = sum_real, sum_imag
                if before is not None:
                    out_real = sum_real - turn * before[1]
                    out_imag = sum_imag + turn * before[0]
                before = (sum_real, sum_imag)
                for place, value in ((real, out_real), (imag, out_imag)):
                    high = value.astype(BF16)
                    high_ref[at, place, :] = high
                    low_ref[at, place, :] = (value - high.astype(F32)).astype(BF16)
            return carry

        lax.fori_loop(0, half // tile, body, 0)

    multiply(0, 1.0)
    multiply(half, -1.0)


def inverse_into(order_ref, base, inverse, high_ref, low_ref, out_refs):
    places = [order_ref[base + at] for at in range(len(out_refs))]
    high = jnp.concatenate([high_ref[place] for place in places], axis=1)
    low = jnp.concatenate([low_ref[place] for place in places], axis=1)
    result = jnp.dot(inverse, jnp.concatenate([high, high, low], axis=0), preferred_element_type=F32).astype(BF16)
    for at, out_ref in enumerate(out_refs):
        out_ref[...] = result[:, at * LANES : (at + 1) * LANES]


def conv_slices_kernel(places, order_ref, table_ref, inverse_ref, filter_ref, early_ref, first_ref, *refs):
    del early_ref
    count = filter_ref.shape[0]
    signal_refs = refs[: len(places)]
    spectra_ref, *out_refs, high_ref, low_ref = refs[-count - 3 :]
    blocks = with_first(order_ref, places, signal_refs, first_ref)
    spectra_into(order_ref, places, table_ref[...], blocks, spectra_ref)
    multiply_spectra(filter_ref, spectra_ref, high_ref, low_ref)
    inverse_into(order_ref, 0, inverse_ref[...], high_ref, low_ref, out_refs)


def conv_slices(order, table, inverse, filter_spectra, early_spectra, first, blocks, places, after):
    rows, lanes = blocks[0].shape
    count = filter_spectra.shape[0]
    _, *outs = pl.pallas_call(
        functools.partial(conv_slices_kernel, places),
        in_specs=[pl.BlockSpec(memory_space=pltpu.SMEM)] + whole_specs(5 + len(places)) + [pl.BlockSpec(memory_space=pl.ANY)] * len(after),
        out_specs=whole_specs(1 + count),
        out_shape=[jax.ShapeDtypeStruct((count, 2 * rows, lanes), F32)]
        + [jax.ShapeDtypeStruct((rows, lanes), BF16)] * count,
        input_output_aliases={4: 0},
        scratch_shapes=[pltpu.VMEM((count, 2 * rows, lanes), BF16)] * 2,
        compiler_params=pltpu.CompilerParams(vmem_limit_bytes=20 << 20),
        cost_estimate=cost(14 * count * rows * rows * lanes, 1),
    )(order, table, inverse, filter_spectra, early_spectra, first, *[blocks[place] for place in places], *after)
    return outs


def gate_chunk_kernel(first, late_ref, skip_ref, *refs):
    out_ref = refs[-1]
    for at, long_ref in enumerate(refs[:-1]):
        mixed = late_ref[first + at] * (long_ref[...].astype(F32) + skip_ref[first + at])
        out_ref[:, at * LANES : (at + 1) * LANES] = mixed.astype(BF16)


def gate_chunk(late, skip, long_blocks, first):
    rows, lanes = long_blocks[0].shape
    count = len(long_blocks)
    return pl.pallas_call(
        functools.partial(gate_chunk_kernel, first),
        in_specs=whole_specs(2 + count),
        out_specs=pl.BlockSpec(memory_space=pltpu.VMEM),
        out_shape=jax.ShapeDtypeStruct((rows, count * lanes), BF16),
        compiler_params=pltpu.CompilerParams(vmem_limit_bytes=8 << 20),
        cost_estimate=cost(3 * count * rows * lanes),
    )(late, skip, *long_blocks)


def weight_kernel(order_ref, channel_ref, weight_ref, out_ref, arrived):
    count, owners = out_ref.shape[:2]
    depth = weight_ref.shape[0] // owners
    copies = []
    for place in range(count):
        for offset in range(owners):
            start = pl.multiple_of((channel_ref[0] ^ offset) * depth + order_ref[place] * LANES, LANES)
            rows = weight_ref.at[pl.ds(start, LANES), :]
            copies.append(pltpu.make_async_copy(rows, out_ref.at[place, offset], arrived.at[place, offset]))
    for copy in copies:
        copy.start()
    for copy in copies:
        copy.wait()


def weight_rows_of(order, channel, weight):
    depth, width = weight.shape
    count, owners = order.shape[0], len(PIECE_ORDER)
    return pl.pallas_call(
        weight_kernel,
        in_specs=[pl.BlockSpec(memory_space=pltpu.SMEM)] * 2 + [pl.BlockSpec(memory_space=pl.ANY)],
        out_specs=pl.BlockSpec(memory_space=pltpu.VMEM),
        out_shape=jax.ShapeDtypeStruct((count, owners, LANES, width), BF16),
        scratch_shapes=[pltpu.SemaphoreType.DMA((count, owners))],
        compiler_params=pltpu.CompilerParams(vmem_limit_bytes=10 << 20),
        cost_estimate=pl.CostEstimate(flops=0, bytes_accessed=4 * depth * width, transcendentals=0),
    )(order, channel, weight)


def add_chunk(chunk, rows_ref, piece_refs, total):
    pieces = jnp.concatenate([ref[...] for ref in piece_refs], axis=1)
    rows = [rows_ref[place, offset] for offset in PIECE_ORDER for place in range(*CHUNKS[chunk])]
    product = jnp.dot(pieces, jnp.concatenate(rows, axis=0), preferred_element_type=F32)
    return product if total is None else total + product


def join_kernel(*refs):
    refs[-1][...] = jnp.concatenate([ref[...] for ref in refs[:-1]], axis=1)


def join(blocks):
    rows, lanes = blocks[0].shape
    count = len(blocks)
    return pl.pallas_call(
        join_kernel,
        in_specs=whole_specs(count),
        out_specs=pl.BlockSpec(memory_space=pltpu.VMEM),
        out_shape=jax.ShapeDtypeStruct((rows, count * lanes), blocks[0].dtype),
        compiler_params=pltpu.CompilerParams(vmem_limit_bytes=8 << 20),
        cost_estimate=cost(4 * rows * lanes),
    )(*blocks)


def project_kernel_slices(chunks, rows_ref, *refs):
    refs, more, out_ref = refs[: 2 * len(chunks)], refs[2 * len(chunks) : -1], refs[-1]
    total = more[0][...] if more else None
    for at, chunk in enumerate(chunks):
        total = add_chunk(chunk, rows_ref, refs[2 * at : 2 * at + 2], total)
    out_ref[...] = total.astype(out_ref.dtype)


def project_slices(weight_rows, chunks, pieces, total, out_type, scale):
    rows = pieces[0].shape[0]
    width = weight_rows.shape[3]
    more = () if total is None else (total,)
    return pl.pallas_call(
        functools.partial(project_kernel_slices, chunks),
        in_specs=whole_specs(1 + len(pieces) + len(more)),
        out_specs=pl.BlockSpec(memory_space=pltpu.VMEM),
        out_shape=jax.ShapeDtypeStruct((rows, width), out_type),
        compiler_params=pltpu.CompilerParams(vmem_limit_bytes=14 << 20),
        cost_estimate=cost(2 * rows * sum(piece.shape[1] for piece in pieces) * width, scale),
    )(weight_rows, *pieces, *more)


def swap_blocks(blocks, sequence):
    count = lax.axis_size("seq")
    arrived = list(blocks)
    for offset in sequence:
        place = OFFSETS.index(offset)
        arrived[place] = lax.ppermute(blocks[place], "seq", [(i, i ^ offset) for i in range(count)])
    return arrived


def on_device_slices(out_gate, in_gate, values, short_filter, long_filter, skip_gain, out_weight):
    rows, width = out_gate.shape
    devices = lax.axis_size("seq")
    table, inverse = transform_tables(rows)
    order = jnp.bitwise_xor(lax.axis_index("seq"), jnp.array(OFFSETS, jnp.int32))
    channel = lax.axis_index("ch").reshape(1)

    filter_blocks = swap_blocks(cut_filter(long_filter, out_gate, in_gate, values), FILTER_ORDER)
    sent = (0, *(OFFSETS.index(offset) for offset in FILTER_ORDER))
    mixed_blocks = swap_blocks(
        mix_slices(order, in_gate, values, short_filter, filter_blocks[OFFSETS.index(MIX_AFTER)]), SIGNAL_ORDER
    )
    late, skip = side_slices(order, out_gate, in_gate, values, filter_blocks, short_filter, skip_gain)
    weight_rows = weight_rows_of(order, channel, out_weight)
    filter_spectra, first = filter_spectra_of(order, table, short_filter, filter_blocks, sent, weight_rows)
    early, last = (tuple(OFFSETS.index(offset) for offset in group) for group in (EARLY, LATE))
    early_spectra = early_spectra_of(order, table, first, mixed_blocks, early)
    long_blocks = conv_slices(order, table, inverse, filter_spectra, early_spectra, first, mixed_blocks, last, (late, weight_rows))
    arrived = swap_blocks(long_blocks, RESULT_ORDER)

    pieces = []
    for start, stop in CHUNKS:
        mixed = gate_chunk(late, skip, arrived[start:stop], start)
        across = lax.ppermute(mixed, "ch", [(i, i ^ 2) for i in range(4)])
        joined = join([mixed, across])
        pieces.append((joined, lax.ppermute(joined, "ch", [(i, i ^ 1) for i in range(4)])))
    total = None
    for chunks, scale in zip(PROJECTS, PROJECT_COSTS, strict=True):
        kind = BF16 if chunks == PROJECTS[-1] else F32
        total = project_slices(weight_rows, chunks, [piece for chunk in chunks for piece in pieces[chunk]], total, kind, scale)
    return total


def on_device_spans(out_gate, in_gate, values, short_filter, long_filter, skip_gain, out_weight):
    rows, width = out_gate.shape
    devices = lax.axis_size("seq")
    slices = width // LANES
    taps = short_filter.shape[1]
    table, inverse = transform_tables(rows)

    rim = jnp.stack([a[rows - (taps - 1) :] for a in (out_gate, in_gate, values)])
    rim = lax.ppermute(rim, "seq", [(i, i + 1) for i in range(devices - 1)])
    rims = rim.astype(F32)

    filter_slices = long_filter.astype(BF16).reshape(rows, slices, LANES).transpose(1, 0, 2)
    filter_whole = send_spans(filter_slices)
    mixed_whole = send_spans(mix_inputs(in_gate, values, rims, short_filter))

    filter_spectra = forward(table, filter_whole)
    late, skip = side_terms(out_gate, in_gate, values, rims, short_filter, skip_gain)
    long_parts = block_conv(table, inverse, mixed_whole, filter_spectra, ROW_PARTS)
    channel = lax.axis_index("ch")
    order = jnp.bitwise_xor(channel, jnp.arange(lax.axis_size("ch"), dtype=jnp.int32))
    outs = []
    for part, long_part in enumerate(long_parts):
        returned = return_spans(long_part, slices)
        mixed = gate_rows(returned, late, skip, part)
        outs.append(project(gather_channels(mixed), out_weight, order))
    return jnp.concatenate(outs, axis=0)


def solution(mesh):
    devices = mesh.shape["seq"]

    def on_device(*arrays):
        width = arrays[0].shape[1]
        taps = arrays[3].shape[1]
        sliced = taps == KEEP + 1 and devices == len(OFFSETS) and width == devices * LANES and mesh.shape["ch"] == len(PIECE_ORDER)
        return (on_device_slices if sliced else on_device_spans)(*arrays)

    return jax.shard_map(
        on_device,
        mesh=mesh,
        in_specs=(
            P("seq", "ch"),
            P("seq", "ch"),
            P("seq", "ch"),
            P(None, None, "ch"),
            P("seq", "ch"),
            P("ch"),
            P(None, "ch"),
        ),
        out_specs=P("seq", "ch"),
        check_vma=False,
    )
```
